32 devices in a mesh: comp: 2 (over core), lat: 4 (over y, x), lon: 4 (over z).
Axes of the slice: x: 2, y: 2, z: 4, core: 2. Of those that a mesh axis runs over, the one named last changes fastest.
Arguments:
- state: float32 [2, 80, 32, 512], P('comp', None, 'lat', 'lon')
- mixing: float32 [2, 80, 80], P('comp')
- diffusivity: float32 [2, 80], P('comp'), may hold values from 0.22 to 0.25
- weights: float32 [2, 64], P('comp'), may hold values from 0.25 to 1
- links: int32 [2, 4, 4, 4, 8], P('comp', 'lat', 'lon'), may hold values from 0 to 63, as said below
- land: int32 [32, 4], P('lat', 'lon'), may hold values 0 or 1
- depth: int32 [32, 4], P('lat', 'lon'), may hold values from 79 to 80
Outputs:
- advanced: float32 [2, 80, 32, 512], P('comp', None, 'lat', 'lon')
The draws below stay inside these ranges and needn't reach their ends.
Inputs may be any that keep to these rules, and one draw needn't show every extreme that they name: Entries are source row below 8, destination lon index below 4, destination row below 8, weight index below 64. A device's links come in 2 consecutive groups of 4, each group with one destination, distinct within the device; in every latitude row of a section, the first group of every device has the same destination.
All inputs are finite; a program needn't handle non-finite values. No bound on the sum of `land` on one device may be relied on, other than what follows from the above.
Results may differ from the reference program's by a relative error of at most 0.0003.
Values sent between devices are 32-bit elements; how exact they have to be, the bound alone decides.
No kernel may reach another device: no remote copies, remote signals or barrier semaphores. Data moves between devices by JAX's collectives and lax.ppermute only.
A program may use at most 64 MiB of HBM per device.

```python
import math
import jax
import jax.numpy as jnp
from jax import lax

LEV = 80
ROWS = 8
BLOCK = 128
STEPS = 4
CAP = 4
NWEIGHT = 64
LINK_GROUPS = 2
LINKS = 8
NROW = 32
NCOL = 512
N_LAT = 4
N_LON = 4


def draw_state(key, part):
    shape = (2, LEV, NROW, NCOL)
    base = jnp.clip(jax.random.normal(key, shape, jnp.float32), -3.5, 3.5)
    along = jnp.roll(base, 2, axis=3) - 2.0 * base + jnp.roll(base, -2, axis=3)
    across = jnp.roll(along, 2, axis=2) - 2.0 * along + jnp.roll(along, -2, axis=2)
    return (across * 0.5).astype(jnp.float32)


def draw_mixing(key, part):
    keys = jax.random.split(key, 2)
    diagonal = jax.random.uniform(keys[0], (2, LEV), jnp.float32, 0.92, 1.0)
    offdiag = jax.random.normal(keys[1], (2, LEV, LEV), jnp.float32) * (0.25 / LEV ** 0.5)
    level_ids = jnp.arange(LEV)
    identity = (level_ids[:, None] == level_ids[None, :]).astype(jnp.float32)
    return (offdiag * (1.0 - identity) + identity * diagonal[:, :, None]).astype(jnp.float32)


def draw_links(key, part):
    keys = jax.random.split(key, 5)
    hottest = jax.random.randint(keys[0], (2, N_LAT, 1, 1), 0, N_LON)
    scores = jax.random.randint(keys[1], (2, N_LAT, N_LON, N_LON), 1, 1000)
    order = jnp.arange(N_LON, dtype=jnp.int32)
    scores = scores * N_LON + order
    scores = jnp.where(order == hottest, 0, scores)
    chosen = jnp.argsort(scores, axis=-1, stable=True)[..., :LINK_GROUPS].astype(jnp.int32)
    targets = jnp.repeat(chosen, CAP, axis=-1)
    sources = jax.random.randint(keys[2], (2, N_LAT, N_LON, LINKS), 0, ROWS)
    dest_rows = jax.random.randint(keys[3], (2, N_LAT, N_LON, LINKS), 0, ROWS)
    weight_ids = jax.random.randint(keys[4], (2, N_LAT, N_LON, LINKS), 0, NWEIGHT)
    return jnp.stack([sources, targets, dest_rows, weight_ids], axis=3).astype(jnp.int32)


def with_ends(drawn, rng, low, top_value):
    index_at = [jax.random.randint(jax.random.fold_in(rng, axis), (), 0, length) for axis, length in enumerate(drawn.shape)]
    longest = drawn.shape.index(max(drawn.shape))
    beside = index_at[:longest] + [(index_at[longest] + 1) % drawn.shape[longest]] + index_at[longest + 1:]
    return drawn.at[tuple(index_at)].set(low).at[tuple(beside)].set(top_value)


def block_scale(stream_key, extent, pieces, smallest, top_value):
    level, own = 1.0, jax.random.fold_in(stream_key, 6)
    for position, parts in pieces:
        steps = jnp.exp(jax.random.uniform(jax.random.fold_in(own, position), (parts,), jnp.float32, smallest / len(pieces), top_value / len(pieces)))
        level = level * jnp.repeat(steps, extent[position] // parts).reshape([-1 if axis == position else 1 for axis in range(len(extent))])
    return level


def setup_inputs(seed: int = 0) -> dict:
    key_list = jax.random.split(jax.random.key(seed), 8)
    state = draw_state(jax.random.fold_in(key_list[7], 71), 0)
    mixing = draw_mixing(jax.random.fold_in(key_list[7], 71), 0)
    diffusivity = jnp.clip(jnp.exp(math.log(0.25) - 0.12783338 * jax.random.uniform(key_list[2], (2, LEV), jnp.float32) ** block_scale(key_list[2], (2, LEV), ((0, 2),), -0.2, 0.2)), 0.22, 0.25)
    weights = jnp.clip(0.25 + 0.75 * jax.random.uniform(key_list[3], (2, NWEIGHT), jnp.float32) ** block_scale(key_list[3], (2, NWEIGHT), ((0, 2),), -0.2, 0.2), 0.25, 1.0)
    links = draw_links(jax.random.fold_in(key_list[7], 71), 0)
    land = with_ends((jax.random.randint(key_list[5], (NROW, N_LON), 0, 64) < 63).astype(jnp.int32), jax.random.fold_in(key_list[5], 1), 0, 1)
    depth = with_ends(jax.random.randint(key_list[6], (NROW, N_LON), LEV - 1, LEV + 1), jax.random.fold_in(key_list[6], 1), LEV - 1, LEV).astype(jnp.int32)
    return dict(state=state, mixing=mixing, diffusivity=diffusivity, weights=weights, links=links, land=land, depth=depth)


coupling_rate = 0.5


def regrid(surface, link_table, table):
    blocks = surface.reshape(N_LAT, ROWS, N_LON, BLOCK)
    sources = link_table[:, :, 0]
    targets = link_table[:, :, 1]
    dest_rows = link_table[:, :, 2]
    weight_ids = link_table[:, :, 3]
    lat_ids = jnp.arange(N_LAT, dtype=jnp.int32)[:, None, None]
    lon_ids = jnp.arange(N_LON, dtype=jnp.int32)[None, :, None]
    weight_link = table[weight_ids]
    values = blocks[lat_ids, sources, lon_ids] * weight_link[..., None]
    accum = jnp.zeros((N_LAT, ROWS, N_LON, BLOCK), jnp.float32).at[lat_ids, dest_rows, targets].add(values)
    totals = jnp.zeros((N_LAT, ROWS, N_LON), jnp.float32).at[lat_ids, dest_rows, targets].add(weight_link)
    return (accum / jnp.maximum(totals, 1.0)[..., None]).reshape(NROW, NCOL)


def reference(state, mixing, diffusivity, weights, links, land, depth):
    sea_cells = jnp.repeat(land.astype(jnp.float32), BLOCK, axis=1)
    deep_cells = jnp.repeat((land * depth).astype(jnp.float32), BLOCK, axis=1)
    surfaces = state[:, 0]
    imported = jnp.stack([regrid(surfaces[1], links[1], weights[1]), regrid(surfaces[0], links[0], weights[0])])
    flux_field = coupling_rate * sea_cells[None] * (imported - surfaces)
    level_ids = jnp.arange(LEV, dtype=jnp.float32)[:, None, None]

    def section(packed):
        tracer, mix_mat, diffuse, flux_one, section_id = packed
        ocean_part = (level_ids < deep_cells[None]).astype(jnp.float32)
        active = jnp.where(section_id == 1, ocean_part, jnp.ones_like(ocean_part))
        for step in range(STEPS):
            padded = jnp.pad(tracer, ((0, 0), (1, 1), (0, 0)))
            neighbours = padded[:, 2:] + padded[:, :-2] + jnp.roll(tracer, -1, axis=2) + jnp.roll(tracer, 1, axis=2)
            moved = tracer + diffuse[:, None, None] * (neighbours - 4.0 * tracer)
            moved = moved.at[0].add(flux_one)
            mixed = jnp.dot(mix_mat, (moved * active).reshape(LEV, -1), precision=lax.Precision.HIGHEST, preferred_element_type=jnp.float32).reshape(tracer.shape)
            tracer = active * mixed + (1.0 - active) * tracer
        return tracer

    return lax.map(section, (state, mixing, diffusivity, flux_field, jnp.arange(2, dtype=jnp.int32)))
```

```python
import functools

import jax
import jax.numpy as jnp
from jax import lax
from jax.experimental import pallas as pl
from jax.experimental.pallas import tpu as pltpu
from jax.sharding import PartitionSpec as P

STEPS = 4
EDGE = 8
AXES = ("comp", "lat", "lon")
VMEM_LIMIT = 32 * 1024 * 1024

coupling_rate = 0.5


def vmem_spec():
    return pl.BlockSpec(memory_space=pltpu.VMEM)


def lane_ids(shape):
    return lax.broadcasted_iota(jnp.int32, shape, len(shape) - 1)


def roll(value, shift):
    shift = shift % value.shape[-1]
    return value if shift == 0 else pltpu.roll(value, shift, 1)


def as_column(row):
    n = row.shape[1]
    diagonal = lax.broadcasted_iota(jnp.int32, (n, n), 0) == lane_ids((n, n))
    return jnp.sum(jnp.where(diagonal, row, 0.0), axis=1, keepdims=True)


def spread(column):
    rows = column.shape[0]
    shape = (rows, 128)
    mine = lane_ids(shape) // EDGE == lax.broadcasted_iota(jnp.int32, shape, 0)
    return jnp.sum(jnp.where(mine, column, 0.0), axis=0, keepdims=True)


def pack_kernel(surface_ref, links_ref, weights_ref, land_ref, depth_ref, out_ref):
    surface = surface_ref[0, 0]
    rows = surface.shape[0]
    table = links_ref[0, 0, 0].astype(jnp.float32)
    count = table.shape[1]
    source = as_column(table[0:1])
    weight_id = as_column(table[3:4])
    entries = weights_ref.shape[1]
    weight = jnp.sum(
        jnp.where(weight_id == lane_ids((count, entries)).astype(jnp.float32), weights_ref[...], 0.0),
        axis=1,
        keepdims=True,
    )
    picked = jnp.zeros((count, surface.shape[1]), jnp.float32)
    for row in range(rows):
        picked = jnp.where(source == float(row), surface[row : row + 1], picked)
    out_ref[0:count] = weight * picked
    code = table[1:2] * float(rows) + table[2:3]
    diagonal = lax.broadcasted_iota(jnp.int32, (count, 128), 0) == lane_ids((count, 128))
    weight_row = jnp.sum(jnp.where(diagonal, weight, 0.0), axis=0, keepdims=True)
    code_row = jnp.sum(jnp.where(diagonal, as_column(code), 0.0), axis=0, keepdims=True)
    land = land_ref[...].astype(jnp.float32)
    deep = land * depth_ref[...].astype(jnp.float32)
    out_ref[count : count + 1] = code_row
    out_ref[count + 1 : count + 2] = weight_row
    out_ref[count + 2 : count + 3] = spread(land)
    out_ref[count + 3 : count + 4] = spread(deep)
    out_ref[count + 4 :] = jnp.zeros((4, 128), jnp.float32)


def edge_kernel(state_ref, mixing_ref, diffuse_ref, edge_ref, first_ref, second_ref, mix_ref, rate_ref):
    levels, rows, cells = state_ref.shape[1:]
    half = levels // 2
    odd = lax.rem(lax.axis_index("lat"), 2) == 1
    lane = lane_ids((levels, 128))
    packed = jnp.zeros((levels, 128), jnp.float32)
    tiles = []
    for row in range(rows):
        tile = state_ref[0, :, row, :]
        tiles.append(tile)
        start = row * EDGE
        packed = jnp.where((lane >= start) & (lane < start + 4), roll(tile, start), packed)
        packed = jnp.where((lane >= start + 4) & (lane < start + 8), roll(tile, start + 8), packed)
    edge_ref[...] = jnp.where(lane_ids((half, 128)) < 64, packed[:half], roll(packed[half:], 64))
    for k in range(4):
        low, high = tiles[k], tiles[rows - 4 + k]
        first_ref[k] = jnp.where(odd, low, high)
        second_ref[k] = jnp.where(odd, high, low)
    mix = mixing_ref[0]
    top = mix.astype(jnp.bfloat16)
    rest = (mix - top.astype(jnp.float32)).astype(jnp.bfloat16)
    mix_ref[...] = jnp.zeros_like(mix_ref)
    mix_ref[:, 0:levels] = top
    mix_ref[:, levels : 2 * levels] = top
    mix_ref[:, 2 * levels : 3 * levels] = rest
    rate_ref[...] = jnp.broadcast_to(as_column(diffuse_ref[...]), rate_ref.shape)


def flux_kernel(count, slices, east_west, *refs):
    surface_ref, land_ref, depth_ref, *packs, out_ref = refs
    surface = surface_ref[0, 0]
    rows = surface.shape[0]
    half = out_ref.shape[0] - 2 * rows - 8
    lon, lon_count = lax.axis_index("lon"), lax.axis_size("lon")
    odd = lax.rem(lon, 2) == 1
    ocean = lax.axis_index("comp") == 1
    here = lon * rows
    after = lax.rem(lon + 1, lon_count) * rows
    before = lax.rem(lon + lon_count - 1, lon_count) * rows
    index = lax.broadcasted_iota(jnp.int32, (3 * rows, count), 0)
    wanted = jnp.where(
        index < rows, here + index, jnp.where(index < 2 * rows, after + index - rows, before + index - 2 * rows)
    ).astype(jnp.float32)
    accum = jnp.zeros((3 * rows, 128), jnp.float32)
    totals = jnp.zeros((3 * rows, 1), jnp.float32)
    for which, offset in slices:
        ref = packs[which]
        hit = (wanted == ref[offset + count : offset + count + 1, 0:count]).astype(jnp.float32)
        accum += jnp.dot(
            hit,
            ref[offset : offset + count],
            precision=lax.Precision.HIGHEST,
            preferred_element_type=jnp.float32,
        )
        totals += jnp.sum(
            hit * ref[offset + count + 1 : offset + count + 2, 0:count], axis=1, keepdims=True
        )
    imported = accum / jnp.maximum(totals, 1.0)
    land = land_ref[...].astype(jnp.float32)
    deep = land * depth_ref[...].astype(jnp.float32)
    all_levels = float(2 * half)
    deep = jnp.where(ocean, deep, all_levels)
    (first, first_at), (second, second_at) = east_west
    lane = lane_ids((1, 128))
    from_east = lax.rem(lane, EDGE) < 4

    def beside(offset_rows, size):
        one = packs[first][first_at + offset_rows : first_at + offset_rows + size]
        two = packs[second][second_at + offset_rows : second_at + offset_rows + size]
        east_is_one = lane_ids((size, 128)) % EDGE < 4
        return jnp.where(east_is_one != odd, one, two)

    middle = beside(0, half)
    land_beside = beside(half + count + 2, 1)
    deep_beside = jnp.where(ocean, beside(half + count + 3, 1), all_levels)
    imported_beside = jnp.zeros((1, 128), jnp.float32)
    for row in range(rows):
        start = row * EDGE
        east = roll(imported[rows + row : rows + row + 1], start)
        west = roll(imported[2 * rows + row : 2 * rows + row + 1], start + 8)
        mine = (lane >= start) & (lane < start + EDGE)
        imported_beside = jnp.where(mine, jnp.where(from_east, east, west), imported_beside)
    flux_beside = coupling_rate * land_beside * (imported_beside - middle[0:1])
    out_ref[0:half] = middle
    out_ref[half : half + rows] = coupling_rate * land * (imported[0:rows] - surface)
    out_ref[half + rows : half + 2 * rows] = jnp.broadcast_to(deep, (rows, 128))
    out_ref[half + 2 * rows : half + 2 * rows + 1] = flux_beside
    out_ref[half + 2 * rows + 1 : half + 2 * rows + 2] = deep_beside
    out_ref[half + 2 * rows + 2 :] = jnp.zeros((6, 128), jnp.float32)


def update_kernel(
    state_ref, own_ref, rows1_ref, rows2_ref, msg1_ref, msg2_ref, mix_ref, rate_ref, out_ref, x_ref, y_ref
):
    levels, rows, cells = state_ref.shape[1:]
    half = levels // 2
    slots = rows + 2 * STEPS
    odd = lax.rem(lax.axis_index("lat"), 2) == 1
    own = own_ref[...]
    one, two = msg1_ref[...], msg2_ref[...]
    top, bottom = jnp.where(odd, one, two), jnp.where(odd, two, one)
    first_at = jnp.where(odd, 0, rows + STEPS)
    for k in range(STEPS):
        x_ref[first_at + k] = rows1_ref[k]
        x_ref[rows + STEPS - first_at + k] = rows2_ref[k]
    for row in range(rows):
        x_ref[STEPS + row] = state_ref[0, :, row, :]

    def per_slot(value, at, slot):
        if slot < STEPS:
            at, value = at + rows - STEPS + slot, value[0]
        elif slot < STEPS + rows:
            at, value = at + slot - STEPS, value[1]
        else:
            at, value = at + slot - STEPS - rows, value[2]
        return value[at : at + 1]

    parts = (top, own, bottom)
    flux_rows = [per_slot(parts, half, s) for s in range(slots)]
    deep_rows = [per_slot(parts, half + rows, s) for s in range(slots)]

    lane1 = lane_ids((1, 128))
    lane = lane_ids((levels, 128))
    level = lax.broadcasted_iota(jnp.int32, (levels, 128), 0).astype(jnp.float32)
    first_level = lax.broadcasted_iota(jnp.int32, (8, 128), 0) == 0
    place = lane % EDGE

    def unfolded(fold, width):
        a, b, c = (roll(v, s) for v, s in zip(fold, (-4 * EDGE, 4 * EDGE, 12 * EDGE)))
        at = lane_ids(a.shape)
        return jnp.where(at < 4 * EDGE, a, jnp.where(at < 12 * EDGE, b, c))

    low = unfolded([v[:half] for v in parts], 128)
    high = unfolded([roll(v[:half], 64) for v in parts], 128)
    mid = jnp.concatenate([low, high], axis=0)
    at = half + 2 * rows
    flux_mid = unfolded([v[at : at + 1] for v in parts], 128)
    deep_mid = unfolded([v[at + 1 : at + 2] for v in parts], 128)
    left = jnp.zeros((levels, 128), jnp.float32)
    right = left
    flux_left = flux_right = deep_side = jnp.zeros((1, 128), jnp.float32)
    for slot in range(slots):
        start = slot * EDGE
        tile = x_ref[slot]
        mine = (lane >= start) & (lane < start + EDGE)
        left = jnp.where(mine, roll(tile, start + EDGE), left)
        right = jnp.where(mine, roll(tile, start), right)
        mine1 = (lane1 >= start) & (lane1 < start + EDGE)
        flux_left = jnp.where(mine1, roll(flux_rows[slot], start + EDGE), flux_left)
        flux_right = jnp.where(mine1, roll(flux_rows[slot], start), flux_right)
        deep_side = jnp.where(mine1, deep_rows[slot], deep_side)

    mixer = mix_ref[...]
    pad = jnp.zeros((mixer.shape[1] - 3 * levels, 256), jnp.bfloat16)

    def injection(row):
        return jnp.where(first_level, row, 0.0)

    def moved(x, neighbours, flux, active):
        rate = rate_ref[...]
        value = (1.0 - 4.0 * rate) * x + rate * neighbours
        value = jnp.concatenate([value[:8] + injection(flux), value[8:]], axis=0)
        return jnp.where(active, value, 0.0)

    def mixed(values):
        value = jnp.concatenate(values, axis=1)
        hi = value.astype(jnp.bfloat16)
        lo = (value - hi.astype(jnp.float32)).astype(jnp.bfloat16)
        full = jnp.concatenate([hi, lo, hi, pad[:, : value.shape[1]]], axis=0)
        out = jnp.dot(mixer, full, preferred_element_type=jnp.float32)
        return [out[:, 128 * k : 128 * (k + 1)] for k in range(len(values))]

    def strip(tile, west, east):
        around = roll(tile, EDGE) + roll(tile, -EDGE)
        to_west, to_east = roll(tile, 1), roll(tile, -1)
        if west is not None:
            to_west = jnp.where(place == 0, roll(west, 1 - EDGE), to_west)
        if east is not None:
            to_east = jnp.where(place == EDGE - 1, roll(east, EDGE - 1), to_east)
        return around + to_west + to_east

    source, target = x_ref, y_ref
    for step in range(STEPS):
        last = step == STEPS - 1
        active_side, active_mid = level < deep_side, level < deep_mid
        z_left = moved(left, strip(left, None, mid), flux_left, active_side)
        z_right = moved(right, strip(right, mid, None), flux_right, active_side)
        new_left, new_right = mixed([z_left, z_right])
        if not last:
            z_mid = moved(mid, strip(mid, left, right), flux_mid, active_mid)
            mid = jnp.where(active_mid, mixed([z_mid])[0], mid)
        left = jnp.where(active_side, new_left, left)
        right = jnp.where(active_side, new_right, right)
        for slot in range(step + 1, slots - step - 1, 2):
            old, values, masks = [], [], []
            for s in (slot, slot + 1):
                x = source[s]
                neighbours = source[s - 1] + source[s + 1] + roll(x, 1) + roll(x, -1)
                active = level < deep_rows[s]
                old.append(x)
                masks.append(active)
                values.append(moved(x, neighbours, flux_rows[s], active))
            for s, x, active, new in zip((slot, slot + 1), old, masks, mixed(values)):
                new = jnp.where(active, new, x)
                if not last:
                    target[s] = new
                    continue
                new = jnp.where(lane < 4, roll(right, -s * EDGE), new)
                new = jnp.where(lane >= cells - 4, roll(left, cells - EDGE - s * EDGE), new)
                out_ref[0, :, s - STEPS, :] = new
        source, target = target, source


def kernel_call(body, out_shape, blocks, scratch=(), flops=0, nbytes=0):
    return pl.pallas_call(
        body,
        out_shape=out_shape,
        in_specs=blocks,
        out_specs=jax.tree.map(lambda _: vmem_spec(), out_shape),
        scratch_shapes=scratch,
        compiler_params=pltpu.CompilerParams(vmem_limit_bytes=VMEM_LIMIT),
        cost_estimate=pl.CostEstimate(flops=flops, bytes_accessed=nbytes, transcendentals=0),
    )


def f32(*shape):
    return jax.ShapeDtypeStruct(shape, jnp.float32)


def exchange(value, axis, partner):
    size = lax.axis_size(axis)
    pairs = [(i, partner(i)) for i in range(size) if 0 <= partner(i) < size]
    return lax.ppermute(value, axis, pairs)


def on_device(state, mixing, diffusivity, weights, links, land, depth):
    levels, rows, cells = state.shape[1:]
    half = levels // 2
    count = links.shape[-1]
    pack_rows = count + 8
    lon_count = lax.axis_size("lon")

    def near(i):
        return i ^ 1

    def far(i):
        return i - 1 if i % 2 == 0 else i + 1

    def far_round(i):
        return far(i) % lon_count

    surface = lax.slice_in_dim(state, 0, 1, axis=1)
    pack = kernel_call(
        pack_kernel, f32(pack_rows, 128), [vmem_spec()] * 5, flops=20000, nbytes=20000
    )(surface, links, weights, land, depth)
    crossed = exchange(pack, "comp", near)
    edge, up_down_1, up_down_2, mix_parts, rates = kernel_call(
        edge_kernel,
        (
            f32(half, 128),
            f32(STEPS, levels, 128),
            f32(STEPS, levels, 128),
            jax.ShapeDtypeStruct((levels, 256), jnp.bfloat16),
            f32(levels, 128),
        ),
        [vmem_spec()] * 3,
        flops=400000,
        nbytes=900000,
    )(state, mixing, diffusivity)
    rows_1 = exchange(up_down_1, "lat", near)
    rows_2 = exchange(up_down_2, "lat", far)

    mine = jnp.concatenate([edge, crossed], axis=0)
    beside_1 = exchange(mine, "lon", near)
    if lon_count == 4:
        onward = jnp.concatenate([mine, beside_1[half:]], axis=0)
        beside_2 = exchange(onward, "lon", far_round)
        packs = [crossed, beside_1, beside_2]
        slices = [(0, 0), (1, half), (2, half), (2, half + pack_rows)]
        east_west = ((1, 0), (2, 0))
    else:
        beside_2 = exchange(mine, "lon", far_round)
        packs = [lax.all_gather(crossed, "lon", axis=0, tiled=True), beside_1, beside_2]
        slices = [(0, k * pack_rows) for k in range(lon_count)]
        east_west = ((1, 0), (2, 0))
    message = kernel_call(
        functools.partial(flux_kernel, count, slices, east_west),
        f32(half + 2 * rows + 8, 128),
        [vmem_spec()] * (3 + len(packs)),
        flops=200000,
        nbytes=100000,
    )(surface, land, depth, *packs)
    message_1 = exchange(message, "lat", near)
    message_2 = exchange(message, "lat", far)
    return kernel_call(
        update_kernel,
        f32(*state.shape),
        [vmem_spec()] * 8,
        scratch=[pltpu.VMEM((rows + 2 * STEPS, levels, 128), jnp.float32)] * 2,
        flops=300000000,
        nbytes=1500000,
    )(state, message, rows_1, rows_2, message_1, message_2, mix_parts, rates)


def solution(mesh):
    in_specs = (
        P("comp", None, "lat", "lon"),
        P("comp", None, None),
        P("comp", None),
        P("comp", None),
        P("comp", "lat", "lon", None, None),
        P("lat", "lon"),
        P("lat", "lon"),
    )
    out_specs = P("comp", None, "lat", "lon")
    return jax.shard_map(
        on_device, mesh=mesh, in_specs=in_specs, out_specs=out_specs, check_vma=False
    )
```

```python
import functools

import jax
import jax.numpy as jnp
from jax import lax
from jax.experimental import pallas as pl
from jax.experimental.pallas import tpu as pltpu
from jax.sharding import PartitionSpec as P

STEPS = 4
EDGE = 8
AXES = ("comp", "lat", "lon")
VMEM_LIMIT = 8 * 1024 * 1024
FRONT_VMEM_LIMIT = 4 * 1024 * 1024

coupling_rate = 0.5


def vmem_spec():
    return pl.BlockSpec(memory_space=pltpu.VMEM)


def lane_ids(shape):
    return lax.broadcasted_iota(jnp.int32, shape, len(shape) - 1)


def roll(value, shift):
    shift = shift % value.shape[-1]
    return value if shift == 0 else pltpu.roll(value, shift, 1)


def as_column(row):
    n = row.shape[1]
    diagonal = lax.broadcasted_iota(jnp.int32, (n, n), 0) == lane_ids((n, n))
    return jnp.sum(jnp.where(diagonal, row, 0.0), axis=1, keepdims=True)


def spread(column):
    rows = column.shape[0]
    shape = (rows, 128)
    mine = lane_ids(shape) // EDGE == lax.broadcasted_iota(jnp.int32, shape, 0)
    return jnp.sum(jnp.where(mine, column, 0.0), axis=0, keepdims=True)


def pack_kernel(
    state_hbm, weights_hbm, links_hbm, land_hbm, depth_hbm,
    out_ref, block_ref, surface_ref, links_ref, weights_ref, land_ref, depth_ref, sems,
):
    copies = [
        pltpu.make_async_copy(source, target, sems.at[k])
        for k, (source, target) in enumerate(
            (
                (links_hbm.at[0, 0, 0], links_ref),
                (weights_hbm, weights_ref),
                (land_hbm, land_ref),
                (depth_hbm, depth_ref),
                (state_hbm.at[0, 0], surface_ref),
                (state_hbm.at[0], block_ref),
            )
        )
    ]
    for copy in copies:
        copy.start()
    for copy in copies[:-1]:
        copy.wait()
    surface = surface_ref[...]
    rows = surface.shape[0]
    table = links_ref[...].astype(jnp.float32)
    count = table.shape[1]
    source = as_column(table[0:1])
    weight_id = as_column(table[3:4])
    entries = weights_ref.shape[1]
    weight = jnp.sum(
        jnp.where(weight_id == lane_ids((count, entries)).astype(jnp.float32), weights_ref[...], 0.0),
        axis=1,
        keepdims=True,
    )
    picked = jnp.zeros((count, surface.shape[1]), jnp.float32)
    for row in range(rows):
        picked = jnp.where(source == float(row), surface[row : row + 1], picked)
    out_ref[0:count] = weight * picked
    code = table[1:2] * float(rows) + table[2:3]
    diagonal = lax.broadcasted_iota(jnp.int32, (count, 128), 0) == lane_ids((count, 128))
    weight_row = jnp.sum(jnp.where(diagonal, weight, 0.0), axis=0, keepdims=True)
    code_row = jnp.sum(jnp.where(diagonal, as_column(code), 0.0), axis=0, keepdims=True)
    land = as_column(land_ref[...].astype(jnp.float32))
    deep = land * as_column(depth_ref[...].astype(jnp.float32))
    out_ref[count : count + 1] = code_row
    out_ref[count + 1 : count + 2] = weight_row
    out_ref[count + 2 : count + 3] = spread(land)
    out_ref[count + 3 : count + 4] = spread(deep)
    out_ref[count + 4 :] = jnp.zeros((4, 128), jnp.float32)
    copies[-1].wait()


def operator_kernel(mixing_ref, diffuse_ref, mix_ref, rate_ref):
    levels = mixing_ref.shape[1]
    mix = mixing_ref[0]
    top = mix.astype(jnp.bfloat16)
    rest = (mix - top.astype(jnp.float32)).astype(jnp.bfloat16)
    mix_ref[...] = jnp.zeros_like(mix_ref)
    mix_ref[:, 0:levels] = top
    mix_ref[:, levels : 2 * levels] = top
    mix_ref[:, 2 * levels : 3 * levels] = rest
    rate_ref[...] = jnp.broadcast_to(as_column(diffuse_ref[...]), rate_ref.shape)


def edge_kernel(state_ref, edge_ref, first_ref, second_ref):
    levels, rows, cells = state_ref.shape
    half = levels // 2
    odd = lax.rem(lax.axis_index("lat"), 2) == 1
    lane = lane_ids((levels, 128))
    packed = jnp.zeros((levels, 128), jnp.float32)
    tiles = []
    for row in range(rows):
        tile = state_ref[:, row, :]
        tiles.append(tile)
        start = row * EDGE
        packed = jnp.where((lane >= start) & (lane < start + 4), roll(tile, start), packed)
        packed = jnp.where((lane >= start + 4) & (lane < start + 8), roll(tile, start + 8), packed)
    edge_ref[...] = jnp.where(lane_ids((half, 128)) < 64, packed[:half], roll(packed[half:], 64))
    for k in range(4):
        low, high = tiles[k], tiles[rows - 4 + k]
        first_ref[k] = jnp.where(odd, low, high)
        second_ref[k] = jnp.where(odd, high, low)


def flux_kernel(count, slices, east_west, *refs):
    surface_ref, *packs, out_ref = refs
    surface = surface_ref[0]
    rows = surface.shape[0]
    half = out_ref.shape[0] - 2 * rows - 8
    lon, lon_count = lax.axis_index("lon"), lax.axis_size("lon")
    odd = lax.rem(lon, 2) == 1
    ocean = lax.axis_index("comp") == 1
    here = lon * rows
    after = lax.rem(lon + 1, lon_count) * rows
    before = lax.rem(lon + lon_count - 1, lon_count) * rows
    index = lax.broadcasted_iota(jnp.int32, (3 * rows, count), 0)
    wanted = jnp.where(
        index < rows, here + index, jnp.where(index < 2 * rows, after + index - rows, before + index - 2 * rows)
    ).astype(jnp.float32)
    accum = jnp.zeros((3 * rows, 128), jnp.float32)
    totals = jnp.zeros((3 * rows, 1), jnp.float32)
    for which, offset in slices:
        ref = packs[which]
        hit = (wanted == ref[offset + count : offset + count + 1, 0:count]).astype(jnp.float32)
        accum += jnp.dot(
            hit,
            ref[offset : offset + count],
            precision=lax.Precision.HIGHEST,
            preferred_element_type=jnp.float32,
        )
        totals += jnp.sum(
            hit * ref[offset + count + 1 : offset + count + 2, 0:count], axis=1, keepdims=True
        )
    imported = accum / jnp.maximum(totals, 1.0)
    here_which, here_at = slices[0]
    own_rows = packs[here_which]
    at = here_at + count + 2
    spread_rows = own_rows[at : at + 2]
    column = lax.broadcasted_iota(jnp.int32, (rows, 128), 0) * EDGE == lane_ids((rows, 128))
    land = jnp.sum(jnp.where(column, spread_rows[0:1], 0.0), axis=1, keepdims=True)
    deep = jnp.sum(jnp.where(column, spread_rows[1:2], 0.0), axis=1, keepdims=True)
    all_levels = float(2 * half)
    deep = jnp.where(ocean, deep, all_levels)
    (first, first_at), (second, second_at) = east_west
    lane = lane_ids((1, 128))
    from_east = lax.rem(lane, EDGE) < 4

    def beside(offset_rows, size):
        one = packs[first][first_at + offset_rows : first_at + offset_rows + size]
        two = packs[second][second_at + offset_rows : second_at + offset_rows + size]
        east_is_one = lane_ids((size, 128)) % EDGE < 4
        return jnp.where(east_is_one != odd, one, two)

    middle = beside(0, half)
    land_beside = beside(half + count + 2, 1)
    deep_beside = jnp.where(ocean, beside(half + count + 3, 1), all_levels)
    imported_beside = jnp.zeros((1, 128), jnp.float32)
    for row in range(rows):
        start = row * EDGE
        east = roll(imported[rows + row : rows + row + 1], start)
        west = roll(imported[2 * rows + row : 2 * rows + row + 1], start + 8)
        mine = (lane >= start) & (lane < start + EDGE)
        imported_beside = jnp.where(mine, jnp.where(from_east, east, west), imported_beside)
    flux_beside = coupling_rate * land_beside * (imported_beside - middle[0:1])
    out_ref[0:half] = middle
    out_ref[half : half + rows] = coupling_rate * land * (imported[0:rows] - surface)
    out_ref[half + rows : half + 2 * rows] = jnp.broadcast_to(deep, (rows, 128))
    out_ref[half + 2 * rows : half + 2 * rows + 1] = flux_beside
    out_ref[half + 2 * rows + 1 : half + 2 * rows + 2] = deep_beside
    out_ref[half + 2 * rows + 2 :] = jnp.zeros((6, 128), jnp.float32)


def update_kernel(
    state_ref, own_ref, rows1_ref, rows2_ref, msg1_ref, msg2_ref, mix_ref, rate_ref, out_ref, x_ref, y_ref
):
    levels, rows, cells = state_ref.shape
    half = levels // 2
    slots = rows + 2 * STEPS
    lat = lax.axis_index("lat")
    odd = lax.rem(lat, 2) == 1
    inside = (lat > 0) & (lat < lax.axis_size("lat") - 1)
    own = own_ref[...]
    one, two = msg1_ref[...], jnp.where(inside, msg2_ref[...], 0.0)
    top, bottom = jnp.where(odd, one, two), jnp.where(odd, two, one)
    first_at = jnp.where(odd, 0, rows + STEPS)
    for k in range(STEPS):
        x_ref[first_at + k] = rows1_ref[k]
        x_ref[rows + STEPS - first_at + k] = jnp.where(inside, rows2_ref[k], 0.0)
    for row in range(rows):
        x_ref[STEPS + row] = state_ref[:, row, :]

    def per_slot(value, at, slot):
        if slot < STEPS:
            at, value = at + rows - STEPS + slot, value[0]
        elif slot < STEPS + rows:
            at, value = at + slot - STEPS, value[1]
        else:
            at, value = at + slot - STEPS - rows, value[2]
        return value[at : at + 1]

    parts = (top, own, bottom)
    flux_rows = [per_slot(parts, half, s) for s in range(slots)]
    deep_rows = [per_slot(parts, half + rows, s) for s in range(slots)]

    lane1 = lane_ids((1, 128))
    lane = lane_ids((levels, 128))
    level = lax.broadcasted_iota(jnp.int32, (levels, 128), 0).astype(jnp.float32)
    first_level = lax.broadcasted_iota(jnp.int32, (8, 128), 0) == 0
    place = lane % EDGE

    def unfolded(fold, width):
        a, b, c = (roll(v, s) for v, s in zip(fold, (-4 * EDGE, 4 * EDGE, 12 * EDGE)))
        at = lane_ids(a.shape)
        return jnp.where(at < 4 * EDGE, a, jnp.where(at < 12 * EDGE, b, c))

    low = unfolded([v[:half] for v in parts], 128)
    high = unfolded([roll(v[:half], 64) for v in parts], 128)
    mid = jnp.concatenate([low, high], axis=0)
    at = half + 2 * rows
    flux_mid = unfolded([v[at : at + 1] for v in parts], 128)
    deep_mid = unfolded([v[at + 1 : at + 2] for v in parts], 128)
    left = jnp.zeros((levels, 128), jnp.float32)
    right = left
    flux_left = flux_right = deep_side = jnp.zeros((1, 128), jnp.float32)
    for slot in range(slots):
        start = slot * EDGE
        tile = x_ref[slot]
        mine = (lane >= start) & (lane < start + EDGE)
        left = jnp.where(mine, roll(tile, start + EDGE), left)
        right = jnp.where(mine, roll(tile, start), right)
        mine1 = (lane1 >= start) & (lane1 < start + EDGE)
        flux_left = jnp.where(mine1, roll(flux_rows[slot], start + EDGE), flux_left)
        flux_right = jnp.where(mine1, roll(flux_rows[slot], start), flux_right)
        deep_side = jnp.where(mine1, deep_rows[slot], deep_side)

    mixer = mix_ref[...]
    pad = jnp.zeros((mixer.shape[1] - 3 * levels, 256), jnp.bfloat16)

    def injection(row):
        return jnp.where(first_level, row, 0.0)

    def moved(x, neighbours, flux, active):
        rate = rate_ref[...]
        value = (1.0 - 4.0 * rate) * x + rate * neighbours
        value = jnp.concatenate([value[:8] + injection(flux), value[8:]], axis=0)
        return jnp.where(active, value, 0.0)

    def mixed(values):
        value = jnp.concatenate(values, axis=1)
        hi = value.astype(jnp.bfloat16)
        lo = (value - hi.astype(jnp.float32)).astype(jnp.bfloat16)
        full = jnp.concatenate([hi, lo, hi, pad[:, : value.shape[1]]], axis=0)
        out = jnp.dot(mixer, full, preferred_element_type=jnp.float32)
        return [out[:, 128 * k : 128 * (k + 1)] for k in range(len(values))]

    def strip(tile, west, east):
        around = roll(tile, EDGE) + roll(tile, -EDGE)
        to_west, to_east = roll(tile, 1), roll(tile, -1)
        if west is not None:
            to_west = jnp.where(place == 0, roll(west, 1 - EDGE), to_west)
        if east is not None:
            to_east = jnp.where(place == EDGE - 1, roll(east, EDGE - 1), to_east)
        return around + to_west + to_east

    source, target = x_ref, y_ref
    for step in range(STEPS):
        last = step == STEPS - 1
        active_side, active_mid = level < deep_side, level < deep_mid
        z_left = moved(left, strip(left, None, mid), flux_left, active_side)
        z_right = moved(right, strip(right, mid, None), flux_right, active_side)
        new_left, new_right = mixed([z_left, z_right])
        if not last:
            z_mid = moved(mid, strip(mid, left, right), flux_mid, active_mid)
            mid = jnp.where(active_mid, mixed([z_mid])[0], mid)
        left = jnp.where(active_side, new_left, left)
        right = jnp.where(active_side, new_right, right)
        for slot in range(step + 1, slots - step - 1, 2):
            old, values, masks = [], [], []
            for s in (slot, slot + 1):
                x = source[s]
                neighbours = source[s - 1] + source[s + 1] + roll(x, 1) + roll(x, -1)
                active = level < deep_rows[s]
                old.append(x)
                masks.append(active)
                values.append(moved(x, neighbours, flux_rows[s], active))
            for s, x, active, new in zip((slot, slot + 1), old, masks, mixed(values)):
                new = jnp.where(active, new, x)
                if not last:
                    target[s] = new
                    continue
                new = jnp.where(lane < 4, roll(right, -s * EDGE), new)
                new = jnp.where(lane >= cells - 4, roll(left, cells - EDGE - s * EDGE), new)
                out_ref[0, :, s - STEPS, :] = new
        source, target = target, source


def kernel_call(body, out_shape, blocks, scratch=(), flops=0, nbytes=0, vmem=VMEM_LIMIT, grid=()):
    return pl.pallas_call(
        body,
        out_shape=out_shape,
        grid=grid,
        in_specs=blocks,
        out_specs=jax.tree.map(lambda _: vmem_spec(), out_shape),
        scratch_shapes=scratch,
        compiler_params=pltpu.CompilerParams(vmem_limit_bytes=vmem),
        cost_estimate=pl.CostEstimate(flops=flops, bytes_accessed=nbytes, transcendentals=0),
    )


def f32(*shape):
    return jax.ShapeDtypeStruct(shape, jnp.float32)


def exchange(value, axis, partner):
    size = lax.axis_size(axis)
    pairs = [(i, partner(i)) for i in range(size) if 0 <= partner(i) < size]
    return lax.ppermute(value, axis, pairs)


def on_device(state, mixing, diffusivity, weights, links, land, depth):
    levels, rows, cells = state.shape[1:]
    half = levels // 2
    count = links.shape[-1]
    pack_rows = count + 8
    lat_count, lon_count = lax.axis_size("lat"), lax.axis_size("lon")

    def near(i):
        return i ^ 1

    def far_round(i):
        return (i - 1 if i % 2 == 0 else i + 1) % lon_count

    def far_lat(i):
        return (i - 1 if i % 2 == 0 else i + 1) % lat_count

    in_hbm = pl.BlockSpec(memory_space=pltpu.HBM)
    pack, block = kernel_call(
        pack_kernel,
        (f32(pack_rows, 128), f32(levels, rows, cells)),
        [in_hbm] * 5,
        scratch=[
            pltpu.VMEM((rows, cells), jnp.float32),
            pltpu.VMEM((4, count), jnp.int32),
            pltpu.VMEM((1, weights.shape[1]), jnp.float32),
            pltpu.VMEM((1, rows), jnp.int32),
            pltpu.VMEM((1, rows), jnp.int32),
            pltpu.SemaphoreType.DMA((6,)),
        ],
        flops=2_000_000_000,
        nbytes=700_000,
        vmem=FRONT_VMEM_LIMIT,
    )(state, weights, links, land.reshape(1, rows), depth.reshape(1, rows))
    crossed = exchange(pack, "comp", near)
    edge, up_down_1, up_down_2 = kernel_call(
        edge_kernel,
        (f32(half, 128), f32(STEPS, levels, 128), f32(STEPS, levels, 128)),
        [vmem_spec()],
        flops=2_000_000_000,
        nbytes=900_000,
        vmem=FRONT_VMEM_LIMIT,
    )(block)
    mix_parts, rates = kernel_call(
        operator_kernel,
        (jax.ShapeDtypeStruct((levels, 256), jnp.bfloat16), f32(levels, 128)),
        [vmem_spec()] * 2,
        flops=100_000,
        nbytes=100_000,
        vmem=FRONT_VMEM_LIMIT,
    )(mixing, diffusivity)
    mine = jnp.concatenate([edge, crossed], axis=0)
    beside_1 = exchange(mine, "lon", near)
    beside_2 = exchange(mine, "lon", far_round)
    east_west = ((1, 0), (2, 0))
    if lon_count == 4:
        across = exchange(crossed, "lon", lambda i: i ^ 2)
        packs = [crossed, beside_1, beside_2, across]
        slices = [(0, 0), (1, half), (2, half), (3, 0)]
    else:
        packs = [crossed, beside_1, beside_2, lax.all_gather(crossed, "lon", axis=0, tiled=True)]
        slices = [(3, k * pack_rows) for k in range(lon_count)]
    up_down_1, up_down_2, beside_1 = lax.optimization_barrier((up_down_1, up_down_2, beside_1))
    rows_1 = exchange(up_down_1, "lat", near)
    rows_2 = exchange(up_down_2, "lat", far_lat)
    message = kernel_call(
        functools.partial(flux_kernel, count, slices, east_west),
        f32(half + 2 * rows + 8, 128),
        [pl.BlockSpec((1, rows, cells), lambda i: (0, 0, 0))]
        + [pl.BlockSpec(p.shape, lambda i: (0, 0)) for p in packs],
        grid=(1,),
        flops=5_000_000_000,
        nbytes=100_000,
        vmem=FRONT_VMEM_LIMIT,
    )(block, *packs)
    message_1 = exchange(message, "lat", near)
    message_2 = exchange(message, "lat", far_lat)
    return kernel_call(
        update_kernel,
        f32(*state.shape),
        [vmem_spec()] * 8,
        scratch=[pltpu.VMEM((rows + 2 * STEPS, levels, 128), jnp.float32)] * 2,
        flops=300000000,
        nbytes=1500000,
    )(block, message, rows_1, rows_2, message_1, message_2, mix_parts, rates)


def solution(mesh):
    in_specs = (
        P("comp", None, "lat", "lon"),
        P("comp", None, None),
        P("comp", None),
        P("comp", None),
        P("comp", "lat", "lon", None, None),
        P("lat", "lon"),
        P("lat", "lon"),
    )
    out_specs = P("comp", None, "lat", "lon")
    return jax.shard_map(
        on_device, mesh=mesh, in_specs=in_specs, out_specs=out_specs, check_vma=False
    )
```

```python
import functools

import jax
import jax.numpy as jnp
from jax import lax
from jax.experimental import pallas as pl
from jax.experimental.pallas import tpu as pltpu
from jax.sharding import PartitionSpec as P

STEPS = 4
EDGE = 8
AXES = ("comp", "lat", "lon")
VMEM_LIMIT = 8 * 1024 * 1024
FRONT_VMEM_LIMIT = 4 * 1024 * 1024

coupling_rate = 0.5


def vmem_spec():
    return pl.BlockSpec(memory_space=pltpu.VMEM)


def lane_ids(shape):
    return lax.broadcasted_iota(jnp.int32, shape, len(shape) - 1)


def roll(value, shift):
    shift = shift % value.shape[-1]
    return value if shift == 0 else pltpu.roll(value, shift, 1)


def as_column(row):
    n = row.shape[1]
    diagonal = lax.broadcasted_iota(jnp.int32, (n, n), 0) == lane_ids((n, n))
    return jnp.sum(jnp.where(diagonal, row, 0.0), axis=1, keepdims=True)


def spread(column):
    rows = column.shape[0]
    shape = (rows, 128)
    mine = lane_ids(shape) // EDGE == lax.broadcasted_iota(jnp.int32, shape, 0)
    return jnp.sum(jnp.where(mine, column, 0.0), axis=0, keepdims=True)


def zero_kernel(out_ref):
    out_ref[...] = jnp.zeros_like(out_ref)


def pack_kernel(state_ref, weights_ref, links_ref, land_ref, depth_ref, zero_ref, out_ref):
    surface = state_ref[0, 0]
    rows = surface.shape[0]
    table = links_ref[0, 0, 0].astype(jnp.float32)
    count = table.shape[1]
    source = as_column(table[0:1])
    weight_id = as_column(table[3:4])
    entries = weights_ref.shape[1]
    weight = jnp.sum(
        jnp.where(weight_id == lane_ids((count, entries)).astype(jnp.float32), weights_ref[...], 0.0),
        axis=1,
        keepdims=True,
    )
    picked = jnp.zeros((count, surface.shape[1]), jnp.float32)
    for row in range(rows):
        picked = jnp.where(source == float(row), surface[row : row + 1], picked)
    out_ref[0:count] = weight * picked
    code = table[1:2] * float(rows) + table[2:3]
    diagonal = lax.broadcasted_iota(jnp.int32, (count, 128), 0) == lane_ids((count, 128))
    weight_row = jnp.sum(jnp.where(diagonal, weight, 0.0), axis=0, keepdims=True)
    code_row = jnp.sum(jnp.where(diagonal, as_column(code), 0.0), axis=0, keepdims=True)
    land = as_column(land_ref[...].astype(jnp.float32))
    deep = land * as_column(depth_ref[...].astype(jnp.float32))
    out_ref[count : count + 1] = code_row
    out_ref[count + 1 : count + 2] = weight_row
    out_ref[count + 2 : count + 3] = spread(land)
    out_ref[count + 3 : count + 4] = spread(deep)
    out_ref[count + 4 :] = zero_ref[0:4]


def operator_kernel(mixing_ref, diffuse_ref, mix_ref, rate_ref):
    levels = mixing_ref.shape[1]
    mix = mixing_ref[0]
    top = mix.astype(jnp.bfloat16)
    rest = (mix - top.astype(jnp.float32)).astype(jnp.bfloat16)
    mix_ref[...] = jnp.zeros_like(mix_ref)
    mix_ref[:, 0:levels] = top
    mix_ref[:, levels : 2 * levels] = top
    mix_ref[:, 2 * levels : 3 * levels] = rest
    rate = jnp.broadcast_to(as_column(diffuse_ref[...]), (levels, 128))
    rate_ref[0] = rate
    rate_ref[1] = 1.0 - 4.0 * rate


def edge_kernel(state_ref, edge_ref, first_ref, second_ref, surface_ref):
    levels, rows, cells = state_ref.shape[1:]
    surface_ref[...] = state_ref[0, 0]
    half = levels // 2
    odd = lax.rem(lax.axis_index("lat"), 2) == 1
    lane = lane_ids((levels, 128))
    first = last = jnp.zeros((levels, 128), jnp.float32)
    tiles = []
    for row in range(rows):
        tile = state_ref[0, :, row, :]
        tiles.append(tile)
        turned = roll(tile, row * EDGE)
        first = jnp.where(lane // EDGE == row, turned, first)
        last = jnp.where(lane // EDGE == (row - 1) % (128 // EDGE), turned, last)
    packed = jnp.where(lane % EDGE < 4, first, roll(last, EDGE))
    edge_ref[...] = jnp.where(lane_ids((half, 128)) < 64, packed[:half], roll(packed[half:], 64))
    for k in range(4):
        low, high = tiles[k], tiles[rows - 4 + k]
        first_ref[k] = jnp.where(odd, low, high)
        second_ref[k] = jnp.where(odd, high, low)


def flux_kernel(count, slices, east_west, *refs):
    surface_ref, *packs, out_ref = refs
    surface = surface_ref[...]
    rows = surface.shape[0]
    half = out_ref.shape[0] - 2 * rows - 8
    lon, lon_count = lax.axis_index("lon"), lax.axis_size("lon")
    odd = lax.rem(lon, 2) == 1
    ocean = lax.axis_index("comp") == 1
    here = lon * rows
    after = lax.rem(lon + 1, lon_count) * rows
    before = lax.rem(lon + lon_count - 1, lon_count) * rows
    index = lax.broadcasted_iota(jnp.int32, (3 * rows, count), 0)
    wanted = jnp.where(
        index < rows, here + index, jnp.where(index < 2 * rows, after + index - rows, before + index - 2 * rows)
    ).astype(jnp.float32)
    accum = jnp.zeros((3 * rows, 128), jnp.float32)
    totals = jnp.zeros((3 * rows, 1), jnp.float32)
    for which, offset in slices:
        ref = packs[which]
        hit = (wanted == ref[offset + count : offset + count + 1, 0:count]).astype(jnp.float32)
        accum += jnp.dot(
            hit,
            ref[offset : offset + count],
            precision=lax.Precision.HIGHEST,
            preferred_element_type=jnp.float32,
        )
        totals += jnp.sum(
            hit * ref[offset + count + 1 : offset + count + 2, 0:count], axis=1, keepdims=True
        )
    imported = accum / jnp.maximum(totals, 1.0)
    here_which, here_at = slices[0]
    own_rows = packs[here_which]
    at = here_at + count + 2
    spread_rows = own_rows[at : at + 2]
    column = lax.broadcasted_iota(jnp.int32, (rows, 128), 0) * EDGE == lane_ids((rows, 128))
    land = jnp.sum(jnp.where(column, spread_rows[0:1], 0.0), axis=1, keepdims=True)
    deep = jnp.sum(jnp.where(column, spread_rows[1:2], 0.0), axis=1, keepdims=True)
    all_levels = float(2 * half)
    deep = jnp.where(ocean, deep, all_levels)
    (first, first_at), (second, second_at) = east_west
    lane = lane_ids((1, 128))
    from_east = lax.rem(lane, EDGE) < 4

    def beside(offset_rows, size):
        one = packs[first][first_at + offset_rows : first_at + offset_rows + size]
        two = packs[second][second_at + offset_rows : second_at + offset_rows + size]
        east_is_one = lane_ids((size, 128)) % EDGE < 4
        return jnp.where(east_is_one != odd, one, two)

    middle = beside(0, half)
    land_beside = beside(half + count + 2, 1)
    deep_beside = jnp.where(ocean, beside(half + count + 3, 1), all_levels)
    imported_beside = jnp.zeros((1, 128), jnp.float32)
    for row in range(rows):
        start = row * EDGE
        east = roll(imported[rows + row : rows + row + 1], start)
        west = roll(imported[2 * rows + row : 2 * rows + row + 1], start + 8)
        mine = (lane >= start) & (lane < start + EDGE)
        imported_beside = jnp.where(mine, jnp.where(from_east, east, west), imported_beside)
    flux_beside = coupling_rate * land_beside * (imported_beside - middle[0:1])
    out_ref[0:half] = middle
    out_ref[half : half + rows] = coupling_rate * land * (imported[0:rows] - surface)
    out_ref[half + rows : half + 2 * rows] = jnp.broadcast_to(deep, (rows, 128))
    out_ref[half + 2 * rows : half + 2 * rows + 1] = flux_beside
    out_ref[half + 2 * rows + 1 : half + 2 * rows + 2] = deep_beside
    out_ref[half + 2 * rows + 2 :] = jnp.zeros((6, 128), jnp.float32)


def halves(value):
    hi = value.astype(jnp.bfloat16)
    return hi, (value - hi.astype(jnp.float32)).astype(jnp.bfloat16)


class Update:
    def __init__(self, mix_ref, rate_ref):
        self.mixer, self.rate_ref = mix_ref[...], rate_ref
        self.levels = rate_ref.shape[1]
        self.pad = jnp.zeros((self.mixer.shape[1] - 3 * self.levels, 256), jnp.bfloat16)
        tail = lax.broadcasted_iota(jnp.int32, (8, 128), 0)
        self.first = tail == 0
        self.tail = (tail + (self.levels - 8)).astype(jnp.float32)

    def moved(self, x, neighbours, flux, deep):
        value = self.rate_ref[1] * x + self.rate_ref[0] * neighbours
        head = value[:8] + jnp.where(self.first, flux, 0.0)
        tail = jnp.where(self.tail < deep, value[-8:], 0.0)
        return jnp.concatenate([head, value[8:-8], tail], axis=0)

    def mixed(self, values):
        value = jnp.concatenate(values, axis=1)
        hi, lo = halves(value)
        full = jnp.concatenate([hi, lo, hi, self.pad[:, : value.shape[1]]], axis=0)
        out = jnp.dot(self.mixer, full, preferred_element_type=jnp.float32)
        return [out[:, 128 * k : 128 * (k + 1)] for k in range(len(values))]

    def settled(self, new, x, deep):
        sea = jnp.broadcast_to(deep, (self.levels - 8, 128)) > 0.0
        body = jnp.where(sea, new[:-8], x[:-8])
        tail = jnp.where(self.tail < deep, new[-8:], x[-8:])
        return jnp.concatenate([body, tail], axis=0)

    def rows(self, tiles, flux, deep):
        values = [
            self.moved(x, above + below + roll(x, 1) + roll(x, -1), f, d)
            for (above, x, below), f, d in zip(tiles, flux, deep)
        ]
        return [self.settled(new, t[1], d) for new, t, d in zip(self.mixed(values), tiles, deep)]


def lat_place():
    lat = lax.axis_index("lat")
    return lax.rem(lat, 2) == 1, (lat > 0) & (lat < lax.axis_size("lat") - 1)


def inner_kernel(state_ref, own_ref, rows1_ref, rows2_ref, mix_ref, rate_ref, x_ref, side_ref, *inner_refs):
    levels, rows, cells = state_ref.shape[1:]
    half = levels // 2
    slots = rows + 2 * STEPS
    odd, inside = lat_place()
    first_at = jnp.where(odd, 0, rows + STEPS)
    for k in range(STEPS):
        x_ref[first_at + k] = rows1_ref[k]
        x_ref[rows + STEPS - first_at + k] = jnp.where(inside, rows2_ref[k], 0.0)
    for row in range(rows):
        x_ref[STEPS + row] = state_ref[0, :, row, :]
    update = Update(mix_ref, rate_ref)
    flux = [own_ref[half + r : half + r + 1] for r in range(rows)]
    deep = [own_ref[half + rows + r : half + rows + r + 1] for r in range(rows)]
    source, first = x_ref, 0
    for step in range(STEPS):
        target, at = inner_refs[step], STEPS + step
        for slot in range(at, slots - at, 2):
            pair = (slot, slot + 1)
            tiles = [[source[s - first + k] for k in (-1, 0, 1)] for s in pair]
            new = update.rows(tiles, [flux[s - STEPS] for s in pair], [deep[s - STEPS] for s in pair])
            for s, tile in zip(pair, new):
                target[s - at] = tile
        source, first = target, at
    lane = lane_ids((levels, 128))
    left = right = jnp.zeros((levels, 128), jnp.float32)
    for slot in range(slots):
        start = slot * EDGE
        turned = roll(x_ref[slot], start)
        right = jnp.where(lane // EDGE == slot, turned, right)
        left = jnp.where(lane // EDGE == (slot - 1) % slots, turned, left)
    side_ref[0] = roll(left, EDGE)
    side_ref[1] = right


def outer_kernel(own_ref, msg1_ref, msg2_ref, mix_ref, rate_ref, x_ref, side_ref, *refs):
    inner_refs, out_ref, outer_refs = refs[:STEPS], refs[STEPS], refs[STEPS + 1 :]
    levels, rows, cells = out_ref.shape[1:]
    half = levels // 2
    slots = rows + 2 * STEPS
    odd, inside = lat_place()
    own = own_ref[...]
    one, two = msg1_ref[...], jnp.where(inside, msg2_ref[...], 0.0)
    top, bottom = jnp.where(odd, one, two), jnp.where(odd, two, one)
    parts = (top, own, bottom)

    def per_slot(at, slot):
        if slot < STEPS:
            at, value = at + rows - STEPS + slot, top
        elif slot < STEPS + rows:
            at, value = at + slot - STEPS, own
        else:
            at, value = at + slot - STEPS - rows, bottom
        return value[at : at + 1]

    flux_rows = [per_slot(half, s) for s in range(slots)]
    deep_rows = [per_slot(half + rows, s) for s in range(slots)]
    lane1 = lane_ids((1, 128))
    lane = lane_ids((levels, 128))
    place = lane % EDGE

    def unfolded(fold):
        a, b, c = (roll(v, s) for v, s in zip(fold, (-4 * EDGE, 4 * EDGE, 12 * EDGE)))
        at = lane_ids(a.shape)
        return jnp.where(at < 4 * EDGE, a, jnp.where(at < 12 * EDGE, b, c))

    low = unfolded([v[:half] for v in parts])
    high = unfolded([roll(v[:half], 64) for v in parts])
    mid = jnp.concatenate([low, high], axis=0)
    at = half + 2 * rows
    flux_mid = unfolded([v[at : at + 1] for v in parts])
    deep_mid = unfolded([v[at + 1 : at + 2] for v in parts])
    left, right = side_ref[0], side_ref[1]
    flux_left = flux_right = deep_side = jnp.zeros((1, 128), jnp.float32)
    for slot in range(slots):
        start = slot * EDGE
        mine1 = (lane1 >= start) & (lane1 < start + EDGE)
        flux_left = jnp.where(mine1, roll(flux_rows[slot], start + EDGE), flux_left)
        flux_right = jnp.where(mine1, roll(flux_rows[slot], start), flux_right)
        deep_side = jnp.where(mine1, deep_rows[slot], deep_side)

    def strip(tile, west, east):
        around = roll(tile, EDGE) + roll(tile, -EDGE)
        to_west, to_east = roll(tile, 1), roll(tile, -1)
        if west is not None:
            to_west = jnp.where(place == 0, roll(west, 1 - EDGE), to_west)
        if east is not None:
            to_east = jnp.where(place == EDGE - 1, roll(east, EDGE - 1), to_east)
        return around + to_west + to_east

    update = Update(mix_ref, rate_ref)

    def tile_at(step, s):
        if step == 0:
            return x_ref[s]
        if 3 + step <= s <= slots - 4 - step:
            return inner_refs[step - 1][s - 3 - step]
        return outer_refs[step - 1][s - step if s < slots // 2 else s - (slots - 6 - step)]

    def put(s, tile):
        tile = jnp.where((lane < 4) | (lane >= cells - 4), roll(sides, -s * EDGE), tile)
        out_ref[0, :, s - STEPS, :] = tile

    for step in range(STEPS):
        last = step == STEPS - 1
        z_left = update.moved(left, strip(left, None, mid), flux_left, deep_side)
        z_right = update.moved(right, strip(right, mid, None), flux_right, deep_side)
        new_left, new_right = update.mixed([z_left, z_right])
        if not last:
            z_mid = update.moved(mid, strip(mid, left, right), flux_mid, deep_mid)
            mid = update.settled(update.mixed([z_mid])[0], mid, deep_mid)
        left = update.settled(new_left, left, deep_side)
        right = update.settled(new_right, right, deep_side)
        if last:
            sides = jnp.where(place < 4, right, roll(left, -EDGE))
        low_rows = list(range(step + 1, step + 4))
        todo = low_rows + [slots - 1 - s for s in reversed(low_rows)]
        for k in range(0, len(todo), 2):
            pair = todo[k : k + 2]
            tiles = [[tile_at(step, s + j) for j in (-1, 0, 1)] for s in pair]
            new = update.rows(tiles, [flux_rows[s] for s in pair], [deep_rows[s] for s in pair])
            for j, (s, tile) in enumerate(zip(pair, new)):
                if last:
                    put(s, tile)
                else:
                    outer_refs[step][k + j] = tile
    for s in (slots // 2 - 1, slots // 2):
        put(s, inner_refs[STEPS - 1][s - slots // 2 + 1])


def kernel_call(body, out_shape, blocks, scratch=(), flops=0, nbytes=0, vmem=VMEM_LIMIT, grid=()):
    return pl.pallas_call(
        body,
        out_shape=out_shape,
        grid=grid,
        in_specs=blocks,
        out_specs=jax.tree.map(lambda _: vmem_spec(), out_shape),
        scratch_shapes=scratch,
        compiler_params=pltpu.CompilerParams(vmem_limit_bytes=vmem),
        cost_estimate=pl.CostEstimate(flops=flops, bytes_accessed=nbytes, transcendentals=0),
    )


def f32(*shape):
    return jax.ShapeDtypeStruct(shape, jnp.float32)


def exchange(value, axis, partner):
    size = lax.axis_size(axis)
    pairs = [(i, partner(i)) for i in range(size) if 0 <= partner(i) < size]
    return lax.ppermute(value, axis, pairs)


def on_device(state, mixing, diffusivity, weights, links, land, depth):
    levels, rows, cells = state.shape[1:]
    half = levels // 2
    count = links.shape[-1]
    pack_rows = count + 8
    lat_count, lon_count = lax.axis_size("lat"), lax.axis_size("lon")

    def near(i):
        return i ^ 1

    def far_round(i):
        return (i - 1 if i % 2 == 0 else i + 1) % lon_count

    def far_lat(i):
        return (i - 1 if i % 2 == 0 else i + 1) % lat_count

    zeros = kernel_call(
        zero_kernel, f32(8, 128), [], flops=2_000_000_000, nbytes=4096, vmem=FRONT_VMEM_LIMIT
    )()
    pack = kernel_call(
        pack_kernel,
        f32(pack_rows, 128),
        [vmem_spec()] * 6,
        flops=2_000_000_000,
        nbytes=700_000,
        vmem=FRONT_VMEM_LIMIT,
    )(state, weights, links, land.reshape(1, rows), depth.reshape(1, rows), zeros)
    state, pack = lax.optimization_barrier((state, pack))
    crossed = exchange(pack, "comp", near)
    edge, up_down_1, up_down_2, surface = kernel_call(
        edge_kernel,
        (f32(half, 128), f32(STEPS, levels, 128), f32(STEPS, levels, 128), f32(rows, cells)),
        [vmem_spec()],
        flops=2_000_000_000,
        nbytes=900_000,
        vmem=FRONT_VMEM_LIMIT,
    )(state)
    mine = jnp.concatenate([edge, crossed], axis=0)
    beside_1 = exchange(mine, "lon", near)
    beside_2 = exchange(mine, "lon", far_round)
    east_west = ((1, 0), (2, 0))
    if lon_count == 4:
        across = exchange(crossed, "lon", lambda i: i ^ 2)
        packs = [crossed, beside_1, beside_2, across]
        slices = [(0, 0), (1, half), (2, half), (3, 0)]
    else:
        packs = [crossed, beside_1, beside_2, lax.all_gather(crossed, "lon", axis=0, tiled=True)]
        slices = [(3, k * pack_rows) for k in range(lon_count)]
    rows_1 = exchange(up_down_1, "lat", near)
    rows_2 = exchange(up_down_2, "lat", far_lat)
    mixing, packs[1] = lax.optimization_barrier((mixing, packs[1]))
    operators = kernel_call(
        operator_kernel,
        (
            jax.ShapeDtypeStruct((levels, 256), jnp.bfloat16),
            f32(2, levels, 128),
        ),
        [vmem_spec()] * 2,
        flops=100_000,
        nbytes=100_000,
        vmem=FRONT_VMEM_LIMIT,
    )(mixing, diffusivity)
    rows_1, operators, packs[0] = lax.optimization_barrier((rows_1, operators, packs[0]))
    message = kernel_call(
        functools.partial(flux_kernel, count, slices, east_west),
        f32(half + 2 * rows + 8, 128),
        [vmem_spec()] * (1 + len(packs)),
        flops=3_000_000_000,
        nbytes=100_000,
        vmem=FRONT_VMEM_LIMIT,
    )(surface, *packs)
    message_1 = exchange(message, "lat", near)
    message_2 = exchange(message, "lat", far_lat)
    laid_out = kernel_call(
        inner_kernel,
        (f32(rows + 2 * STEPS, levels, 128), f32(2, levels, 128))
        + tuple(f32(rows - 2 * k, levels, 128) for k in range(STEPS)),
        [vmem_spec()] * 6,
        flops=2_000_000_000,
        nbytes=2_000_000,
    )(state, message, rows_1, rows_2, *operators)
    return kernel_call(
        outer_kernel,
        f32(*state.shape),
        [vmem_spec()] * (5 + len(laid_out)),
        scratch=[pltpu.VMEM((6, levels, 128), jnp.float32)] * (STEPS - 1),
        flops=300_000_000,
        nbytes=2_000_000,
    )(message, message_1, message_2, *operators, *laid_out)


def solution(mesh):
    in_specs = (
        P("comp", None, "lat", "lon"),
        P("comp", None, None),
        P("comp", None),
        P("comp", None),
        P("comp", "lat", "lon", None, None),
        P("lat", "lon"),
        P("lat", "lon"),
    )
    out_specs = P("comp", None, "lat", "lon")
    return jax.shard_map(
        on_device, mesh=mesh, in_specs=in_specs, out_specs=out_specs, check_vma=False
    )
```

```python
import functools

import jax
import jax.numpy as jnp
from jax import lax
from jax.experimental import pallas as pl
from jax.experimental.pallas import tpu as pltpu
from jax.sharding import PartitionSpec as P

STEPS = 4
EDGE = 8
FOLD = 24
AXES = ("comp", "lat", "lon")
VMEM_LIMIT = 8 * 1024 * 1024
FRONT_VMEM_LIMIT = 4 * 1024 * 1024

coupling_rate = 0.5


def vmem_spec():
    return pl.BlockSpec(memory_space=pltpu.VMEM)


def lane_ids(shape):
    return lax.broadcasted_iota(jnp.int32, shape, len(shape) - 1)


def roll(value, shift):
    shift = shift % value.shape[-1]
    return value if shift == 0 else pltpu.roll(value, shift, 1)


def as_column(row):
    n = row.shape[1]
    diagonal = lax.broadcasted_iota(jnp.int32, (n, n), 0) == lane_ids((n, n))
    return jnp.sum(jnp.where(diagonal, row, 0.0), axis=1, keepdims=True)


def spread(column):
    rows = column.shape[0]
    shape = (rows, 128)
    mine = lane_ids(shape) // EDGE == lax.broadcasted_iota(jnp.int32, shape, 0)
    return jnp.sum(jnp.where(mine, column, 0.0), axis=0, keepdims=True)


def zero_kernel(out_ref):
    out_ref[...] = jnp.zeros_like(out_ref)


def pack_kernel(state_ref, weights_ref, links_ref, land_ref, depth_ref, zero_ref, out_ref):
    surface = state_ref[0, 0]
    rows = surface.shape[0]
    table = links_ref[0, 0, 0].astype(jnp.float32)
    count = table.shape[1]
    source = as_column(table[0:1])
    weight_id = as_column(table[3:4])
    entries = weights_ref.shape[1]
    weight = jnp.sum(
        jnp.where(weight_id == lane_ids((count, entries)).astype(jnp.float32), weights_ref[...], 0.0),
        axis=1,
        keepdims=True,
    )
    picked = jnp.zeros((count, surface.shape[1]), jnp.float32)
    for row in range(rows):
        picked = jnp.where(source == float(row), surface[row : row + 1], picked)
    out_ref[0:count] = weight * picked
    code = table[1:2] * float(rows) + table[2:3]
    diagonal = lax.broadcasted_iota(jnp.int32, (count, 128), 0) == lane_ids((count, 128))
    weight_row = jnp.sum(jnp.where(diagonal, weight, 0.0), axis=0, keepdims=True)
    code_row = jnp.sum(jnp.where(diagonal, as_column(code), 0.0), axis=0, keepdims=True)
    land = as_column(land_ref[...].astype(jnp.float32))
    deep = land * as_column(depth_ref[...].astype(jnp.float32))
    out_ref[count : count + 1] = code_row
    out_ref[count + 1 : count + 2] = weight_row
    out_ref[count + 2 : count + 3] = spread(land)
    out_ref[count + 3 : count + 4] = spread(deep)
    out_ref[count + 4 :] = zero_ref[0:4]


def operator_kernel(mixing_ref, diffuse_ref, mix_ref, rate_ref):
    levels = mixing_ref.shape[1]
    mix = mixing_ref[0]
    top = mix.astype(jnp.bfloat16)
    rest = (mix - top.astype(jnp.float32)).astype(jnp.bfloat16)
    mix_ref[...] = jnp.zeros_like(mix_ref)
    mix_ref[:, 0:levels] = top
    mix_ref[:, levels : 2 * levels] = top
    mix_ref[:, 2 * levels : 3 * levels] = rest
    rate = jnp.broadcast_to(as_column(diffuse_ref[...]), (levels, 128))
    rate_ref[0] = rate
    rate_ref[1] = 1.0 - 4.0 * rate


def edge_kernel(state_ref, edge_ref, first_ref, second_ref, surface_ref):
    levels, rows, cells = state_ref.shape[1:]
    surface_ref[...] = state_ref[0, 0]
    half = levels // 2
    odd = lax.rem(lax.axis_index("lat"), 2) == 1
    lane = lane_ids((levels, 128))
    first = last = jnp.zeros((levels, 128), jnp.float32)
    tiles = []
    for row in range(rows):
        tile = state_ref[0, :, row, :]
        tiles.append(tile)
        turned = roll(tile, row * EDGE)
        first = jnp.where(lane // EDGE == row, turned, first)
        last = jnp.where(lane // EDGE == (row - 1) % (128 // EDGE), turned, last)
    packed = jnp.where(lane % EDGE < 4, first, roll(last, EDGE))
    edge_ref[...] = jnp.where(lane_ids((half, 128)) < 64, packed[:half], roll(packed[half:], 64))
    for k in range(4):
        low, high = tiles[k], tiles[rows - 4 + k]
        first_ref[k] = jnp.where(odd, low, high)
        second_ref[k] = jnp.where(odd, high, low)


def flux_kernel(count, slices, east_west, *refs):
    surface_ref, *packs, own_ref, first_ref, second_ref = refs
    surface = surface_ref[...]
    rows = surface.shape[0]
    levels = own_ref.shape[0] - 2 * rows - 8
    half = levels // 2
    lon, lon_count = lax.axis_index("lon"), lax.axis_size("lon")
    odd = lax.rem(lon, 2) == 1
    ocean = lax.axis_index("comp") == 1
    here = lon * rows
    after = lax.rem(lon + 1, lon_count) * rows
    before = lax.rem(lon + lon_count - 1, lon_count) * rows
    index = lax.broadcasted_iota(jnp.int32, (3 * rows, count), 0)
    wanted = jnp.where(
        index < rows, here + index, jnp.where(index < 2 * rows, after + index - rows, before + index - 2 * rows)
    ).astype(jnp.float32)
    accum = jnp.zeros((3 * rows, 128), jnp.float32)
    totals = jnp.zeros((3 * rows, 1), jnp.float32)
    for which, offset in slices:
        ref = packs[which]
        hit = (wanted == ref[offset + count : offset + count + 1, 0:count]).astype(jnp.float32)
        accum += jnp.dot(
            hit,
            ref[offset : offset + count],
            precision=lax.Precision.HIGHEST,
            preferred_element_type=jnp.float32,
        )
        totals += jnp.sum(
            hit * ref[offset + count + 1 : offset + count + 2, 0:count], axis=1, keepdims=True
        )
    imported = accum / jnp.maximum(totals, 1.0)
    here_which, here_at = slices[0]
    own_rows = packs[here_which]
    at = here_at + count + 2
    spread_rows = own_rows[at : at + 2]
    column = lax.broadcasted_iota(jnp.int32, (rows, 128), 0) * EDGE == lane_ids((rows, 128))
    land = jnp.sum(jnp.where(column, spread_rows[0:1], 0.0), axis=1, keepdims=True)
    deep = jnp.sum(jnp.where(column, spread_rows[1:2], 0.0), axis=1, keepdims=True)
    all_levels = float(levels)
    deep = jnp.where(ocean, deep, all_levels)
    (first, first_at), (second, second_at) = east_west
    lane = lane_ids((1, 128))
    from_east = lax.rem(lane, EDGE) < 4

    def beside(offset_rows, size):
        one = packs[first][first_at + offset_rows : first_at + offset_rows + size]
        two = packs[second][second_at + offset_rows : second_at + offset_rows + size]
        east_is_one = lane_ids((size, 128)) % EDGE < 4
        return jnp.where(east_is_one != odd, one, two)

    middle = beside(0, half)
    land_beside = beside(half + count + 2, 1)
    deep_beside = jnp.where(ocean, beside(half + count + 3, 1), all_levels)
    imported_beside = jnp.zeros((1, 128), jnp.float32)
    for row in range(rows):
        start = row * EDGE
        east = roll(imported[rows + row : rows + row + 1], start)
        west = roll(imported[2 * rows + row : 2 * rows + row + 1], start + 8)
        mine = (lane >= start) & (lane < start + EDGE)
        imported_beside = jnp.where(mine, jnp.where(from_east, east, west), imported_beside)
    flux_beside = coupling_rate * land_beside * (imported_beside - middle[0:1])
    flux = coupling_rate * land * (imported[0:rows] - surface)
    deep = jnp.broadcast_to(deep, (rows, 128))
    whole = jnp.concatenate([middle, roll(middle, 64)], axis=0)
    own_ref[0:levels] = roll(whole, STEPS * EDGE)
    own_ref[levels : levels + rows] = flux
    own_ref[levels + rows : levels + 2 * rows] = deep
    own_ref[levels + 2 * rows : levels + 2 * rows + 1] = roll(flux_beside, STEPS * EDGE)
    own_ref[levels + 2 * rows + 1 : levels + 2 * rows + 2] = roll(deep_beside, STEPS * EDGE)
    own_ref[levels + 2 * rows + 2 :] = jnp.zeros((6, 128), jnp.float32)
    width = STEPS * EDGE
    sides = []
    for at in (0, rows - STEPS):
        lane_at = at * EDGE
        folded = jnp.zeros((FOLD, 128), jnp.float32)
        lane_fold = lane_ids((FOLD, 128))
        for group in range(-(-levels // FOLD)):
            part = whole[group * FOLD : min((group + 1) * FOLD, levels)]
            if part.shape[0] < FOLD:
                extra = jnp.zeros((FOLD - part.shape[0], 128), jnp.float32)
                index = lax.broadcasted_iota(jnp.int32, extra.shape, 0)
                extra = jnp.where(index == 0, flux_beside, jnp.where(index == 1, deep_beside, extra))
                part = jnp.concatenate([part, extra], axis=0)
            folded = jnp.where(lane_fold // width == group, roll(part, group * width - lane_at), folded)
        sides.append((folded, flux[at : at + STEPS], deep[at : at + STEPS]))
    lat_odd = lax.rem(lax.axis_index("lat"), 2) == 1
    starts = (0, FOLD, FOLD + STEPS, FOLD + 2 * STEPS)
    for (low, high), begin, end in zip(zip(*sides), starts, starts[1:]):
        first_ref[begin:end] = jnp.where(lat_odd, low, high)
        second_ref[begin:end] = jnp.where(lat_odd, high, low)


def halves(value):
    hi = value.astype(jnp.bfloat16)
    return hi, (value - hi.astype(jnp.float32)).astype(jnp.bfloat16)


class Update:
    def __init__(self, mix_ref, rate_ref):
        self.mixer, self.rate_ref = mix_ref[...], rate_ref
        self.levels = rate_ref.shape[1]
        self.pad = jnp.zeros((self.mixer.shape[1] - 3 * self.levels, 256), jnp.bfloat16)
        tail = lax.broadcasted_iota(jnp.int32, (8, 128), 0)
        self.first = tail == 0
        self.tail = (tail + (self.levels - 8)).astype(jnp.float32)

    def moved(self, x, neighbours, flux, deep):
        value = self.rate_ref[1] * x + self.rate_ref[0] * neighbours
        head = value[:8] + jnp.where(self.first, flux, 0.0)
        tail = jnp.where(self.tail < deep, value[-8:], 0.0)
        return jnp.concatenate([head, value[8:-8], tail], axis=0)

    def mixed(self, values):
        value = jnp.concatenate(values, axis=1)
        hi, lo = halves(value)
        full = jnp.concatenate([hi, lo, hi, self.pad[:, : value.shape[1]]], axis=0)
        out = jnp.dot(self.mixer, full, preferred_element_type=jnp.float32)
        return [out[:, 128 * k : 128 * (k + 1)] for k in range(len(values))]

    def settled(self, new, x, deep):
        sea = jnp.broadcast_to(deep, (self.levels - 8, 128)) > 0.0
        body = jnp.where(sea, new[:-8], x[:-8])
        tail = jnp.where(self.tail < deep, new[-8:], x[-8:])
        return jnp.concatenate([body, tail], axis=0)

    def rows(self, tiles, flux, deep):
        values = [
            self.moved(x, above + below + roll(x, 1) + roll(x, -1), f, d)
            for (above, x, below), f, d in zip(tiles, flux, deep)
        ]
        return [self.settled(new, t[1], d) for new, t, d in zip(self.mixed(values), tiles, deep)]


def lat_place():
    lat = lax.axis_index("lat")
    return lax.rem(lat, 2) == 1, (lat > 0) & (lat < lax.axis_size("lat") - 1)


def inner_kernel(state_ref, own_ref, rows1_ref, rows2_ref, mix_ref, rate_ref, x_ref, side_ref, *inner_refs):
    levels, rows, cells = state_ref.shape[1:]
    slots = rows + 2 * STEPS
    odd, inside = lat_place()
    first_at = jnp.where(odd, 0, rows + STEPS)
    for k in range(STEPS):
        x_ref[first_at + k] = rows1_ref[k]
        x_ref[rows + STEPS - first_at + k] = jnp.where(inside, rows2_ref[k], 0.0)
    for row in range(rows):
        x_ref[STEPS + row] = state_ref[0, :, row, :]
    update = Update(mix_ref, rate_ref)
    flux = [own_ref[levels + r : levels + r + 1] for r in range(rows)]
    deep = [own_ref[levels + rows + r : levels + rows + r + 1] for r in range(rows)]
    source, first = x_ref, 0
    for step in range(STEPS):
        target, at = inner_refs[step], STEPS + step
        for slot in range(at, slots - at, 2):
            pair = (slot, slot + 1)
            tiles = [[source[s - first + k] for k in (-1, 0, 1)] for s in pair]
            new = update.rows(tiles, [flux[s - STEPS] for s in pair], [deep[s - STEPS] for s in pair])
            for s, tile in zip(pair, new):
                target[s - at] = tile
        source, first = target, at
    lane = lane_ids((levels, 128))
    left = right = jnp.zeros((levels, 128), jnp.float32)
    for slot in range(slots):
        start = slot * EDGE
        turned = roll(x_ref[slot], start)
        right = jnp.where(lane // EDGE == slot, turned, right)
        left = jnp.where(lane // EDGE == (slot - 1) % slots, turned, left)
    side_ref[0] = roll(left, EDGE)
    side_ref[1] = right


def outer_kernel(own_ref, msg2_ref, msg1_ref, mix_ref, rate_ref, x_ref, side_ref, *refs):
    inner_refs, out_ref, outer_refs = refs[:STEPS], refs[STEPS], refs[STEPS + 1 :]
    levels, rows, cells = out_ref.shape[1:]
    slots = rows + 2 * STEPS
    odd, inside = lat_place()
    one, two = msg1_ref[...], jnp.where(inside, msg2_ref[...], 0.0)
    top, bottom = jnp.where(odd, one, two), jnp.where(odd, two, one)

    def per_slot(at, own_at, slot):
        if slot < STEPS:
            return top[at + slot : at + slot + 1]
        if slot < STEPS + rows:
            return own_ref[own_at + slot - STEPS : own_at + slot - STEPS + 1]
        return bottom[at + slot - STEPS - rows : at + slot - STEPS - rows + 1]

    flux_rows = [per_slot(FOLD, levels, s) for s in range(slots)]
    deep_rows = [per_slot(FOLD + STEPS, levels + rows, s) for s in range(slots)]
    lane1 = lane_ids((1, 128))
    lane = lane_ids((levels, 128))
    place = lane % EDGE
    width = STEPS * EDGE

    def around(upper, own, lower, group):
        at = lane_ids(own.shape)
        upper, lower = roll(upper, -group * width), roll(lower, 128 - width - group * width)
        return jnp.where(at < width, upper, jnp.where(at < 128 - width, own, lower))

    pieces = []
    for start in range(0, levels, FOLD):
        size = min(FOLD, levels - start)
        pieces.append(around(top[:size], own_ref[start : start + size], bottom[:size], start // FOLD))
    mid = jnp.concatenate(pieces, axis=0)
    beside = levels % FOLD
    at = levels + 2 * rows
    flux_mid, deep_mid = (
        around(
            top[beside + k : beside + k + 1],
            own_ref[at + k : at + k + 1],
            bottom[beside + k : beside + k + 1],
            levels // FOLD,
        )
        for k in range(2)
    )
    left, right = side_ref[0], side_ref[1]
    flux_left = flux_right = deep_side = jnp.zeros((1, 128), jnp.float32)
    for slot in range(slots):
        start = slot * EDGE
        mine1 = (lane1 >= start) & (lane1 < start + EDGE)
        flux_left = jnp.where(mine1, roll(flux_rows[slot], start + EDGE), flux_left)
        flux_right = jnp.where(mine1, roll(flux_rows[slot], start), flux_right)
        deep_side = jnp.where(mine1, deep_rows[slot], deep_side)

    def strip(tile, west, east):
        above_below = roll(tile, EDGE) + roll(tile, -EDGE)
        to_west, to_east = roll(tile, 1), roll(tile, -1)
        if west is not None:
            to_west = jnp.where(place == 0, roll(west, 1 - EDGE), to_west)
        if east is not None:
            to_east = jnp.where(place == EDGE - 1, roll(east, EDGE - 1), to_east)
        return above_below + to_west + to_east

    update = Update(mix_ref, rate_ref)

    def tile_at(step, s):
        if step == 0:
            return x_ref[s]
        if 3 + step <= s <= slots - 4 - step:
            return inner_refs[step - 1][s - 3 - step]
        return outer_refs[step - 1][s - step if s < slots // 2 else s - (slots - 6 - step)]

    def put(s, tile):
        tile = jnp.where((lane < 4) | (lane >= cells - 4), roll(sides, -s * EDGE), tile)
        out_ref[0, :, s - STEPS, :] = tile

    for step in range(STEPS):
        last = step == STEPS - 1
        z_left = update.moved(left, strip(left, None, mid), flux_left, deep_side)
        z_right = update.moved(right, strip(right, mid, None), flux_right, deep_side)
        new_left, new_right = update.mixed([z_left, z_right])
        if not last:
            z_mid = update.moved(mid, strip(mid, left, right), flux_mid, deep_mid)
            mid = update.settled(update.mixed([z_mid])[0], mid, deep_mid)
        left = update.settled(new_left, left, deep_side)
        right = update.settled(new_right, right, deep_side)
        if last:
            sides = jnp.where(place < 4, right, roll(left, -EDGE))
        low_rows = list(range(step + 1, step + 4))
        todo = low_rows + [slots - 1 - s for s in reversed(low_rows)]
        for k in range(0, len(todo), 2):
            pair = todo[k : k + 2]
            tiles = [[tile_at(step, s + j) for j in (-1, 0, 1)] for s in pair]
            new = update.rows(tiles, [flux_rows[s] for s in pair], [deep_rows[s] for s in pair])
            for j, (s, tile) in enumerate(zip(pair, new)):
                if last:
                    put(s, tile)
                else:
                    outer_refs[step][k + j] = tile
    for s in (slots // 2 - 1, slots // 2):
        put(s, inner_refs[STEPS - 1][s - slots // 2 + 1])


def kernel_call(body, out_shape, blocks, scratch=(), flops=0, nbytes=0, vmem=VMEM_LIMIT, grid=()):
    return pl.pallas_call(
        body,
        out_shape=out_shape,
        grid=grid,
        in_specs=blocks,
        out_specs=jax.tree.map(lambda _: vmem_spec(), out_shape),
        scratch_shapes=scratch,
        compiler_params=pltpu.CompilerParams(vmem_limit_bytes=vmem),
        cost_estimate=pl.CostEstimate(flops=flops, bytes_accessed=nbytes, transcendentals=0),
    )


def f32(*shape):
    return jax.ShapeDtypeStruct(shape, jnp.float32)


def exchange(value, axis, partner):
    size = lax.axis_size(axis)
    pairs = [(i, partner(i)) for i in range(size) if 0 <= partner(i) < size]
    return lax.ppermute(value, axis, pairs)


def on_device(state, mixing, diffusivity, weights, links, land, depth):
    levels, rows, cells = state.shape[1:]
    half = levels // 2
    count = links.shape[-1]
    pack_rows = count + 8
    lat_count, lon_count = lax.axis_size("lat"), lax.axis_size("lon")

    def near(i):
        return i ^ 1

    def far_round(i):
        return (i - 1 if i % 2 == 0 else i + 1) % lon_count

    def far_lat(i):
        return (i - 1 if i % 2 == 0 else i + 1) % lat_count

    zeros = kernel_call(
        zero_kernel, f32(8, 128), [], flops=2_000_000_000, nbytes=4096, vmem=FRONT_VMEM_LIMIT
    )()
    pack = kernel_call(
        pack_kernel,
        f32(pack_rows, 128),
        [vmem_spec()] * 6,
        flops=2_000_000_000,
        nbytes=700_000,
        vmem=FRONT_VMEM_LIMIT,
    )(state, weights, links, land.reshape(1, rows), depth.reshape(1, rows), zeros)
    state, pack = lax.optimization_barrier((state, pack))
    crossed = exchange(pack, "comp", near)
    edge, up_down_1, up_down_2, surface = kernel_call(
        edge_kernel,
        (f32(half, 128), f32(STEPS, levels, 128), f32(STEPS, levels, 128), f32(rows, cells)),
        [vmem_spec()],
        flops=2_000_000_000,
        nbytes=900_000,
        vmem=FRONT_VMEM_LIMIT,
    )(state)
    mine = jnp.concatenate([edge, crossed], axis=0)
    beside_1 = exchange(mine, "lon", near)
    beside_2 = exchange(mine, "lon", far_round)
    east_west = ((1, 0), (2, 0))
    if lon_count == 4:
        across = exchange(crossed, "lon", lambda i: i ^ 2)
        packs = [crossed, beside_2, across, beside_1]
        slices = [(0, 0), (1, half), (2, 0), (3, half)]
        east_west = ((3, 0), (1, 0))
    else:
        packs = [crossed, beside_1, beside_2, lax.all_gather(crossed, "lon", axis=0, tiled=True)]
        slices = [(3, k * pack_rows) for k in range(lon_count)]
    rows_1 = exchange(up_down_1, "lat", near)
    rows_2 = exchange(up_down_2, "lat", far_lat)
    mixing, packs[1] = lax.optimization_barrier((mixing, packs[1]))
    operators = kernel_call(
        operator_kernel,
        (
            jax.ShapeDtypeStruct((levels, 256), jnp.bfloat16),
            f32(2, levels, 128),
        ),
        [vmem_spec()] * 2,
        flops=100_000,
        nbytes=100_000,
        vmem=FRONT_VMEM_LIMIT,
    )(mixing, diffusivity)
    rows_1, operators, packs[0] = lax.optimization_barrier((rows_1, operators, packs[0]))
    own, for_first, for_second = kernel_call(
        functools.partial(flux_kernel, count, slices, east_west),
        (f32(levels + 2 * rows + 8, 128),) + (f32(FOLD + 2 * STEPS, 128),) * 2,
        [vmem_spec()] * (1 + len(packs)),
        flops=3_000_000_000,
        nbytes=100_000,
        vmem=FRONT_VMEM_LIMIT,
    )(surface, *packs)
    message_2 = exchange(for_second, "lat", far_lat)
    message_1 = exchange(for_first, "lat", near)
    laid_out = kernel_call(
        inner_kernel,
        (f32(rows + 2 * STEPS, levels, 128), f32(2, levels, 128))
        + tuple(f32(rows - 2 * k, levels, 128) for k in range(STEPS)),
        [vmem_spec()] * 6,
        flops=2_000_000_000,
        nbytes=2_000_000,
    )(state, own, rows_1, rows_2, *operators)
    return kernel_call(
        outer_kernel,
        f32(*state.shape),
        [vmem_spec()] * (5 + len(laid_out)),
        scratch=[pltpu.VMEM((6, levels, 128), jnp.float32)] * (STEPS - 1),
        flops=300_000_000,
        nbytes=2_000_000,
    )(own, message_2, message_1, *operators, *laid_out)


def solution(mesh):
    in_specs = (
        P("comp", None, "lat", "lon"),
        P("comp", None, None),
        P("comp", None),
        P("comp", None),
        P("comp", "lat", "lon", None, None),
        P("lat", "lon"),
        P("lat", "lon"),
    )
    out_specs = P("comp", None, "lat", "lon")
    return jax.shard_map(
        on_device, mesh=mesh, in_specs=in_specs, out_specs=out_specs, check_vma=False
    )
```

```python
import functools

import jax
import jax.numpy as jnp
from jax import lax
from jax.experimental import pallas as pl
from jax.experimental.pallas import tpu as pltpu
from jax.sharding import PartitionSpec as P

STEPS = 4
EDGE = 8
FOLD = 24
AXES = ("comp", "lat", "lon")
VMEM_LIMIT = 8 * 1024 * 1024
FRONT_VMEM_LIMIT = 4 * 1024 * 1024

coupling_rate = 0.5


def vmem_spec():
    return pl.BlockSpec(memory_space=pltpu.VMEM)


def lane_ids(shape):
    return lax.broadcasted_iota(jnp.int32, shape, len(shape) - 1)


def roll(value, shift):
    shift = shift % value.shape[-1]
    return value if shift == 0 else pltpu.roll(value, shift, 1)


def as_column(row):
    n = row.shape[1]
    diagonal = lax.broadcasted_iota(jnp.int32, (n, n), 0) == lane_ids((n, n))
    return jnp.sum(jnp.where(diagonal, row, 0.0), axis=1, keepdims=True)


def spread(column):
    rows = column.shape[0]
    shape = (rows, 128)
    mine = lane_ids(shape) // EDGE == lax.broadcasted_iota(jnp.int32, shape, 0)
    return jnp.sum(jnp.where(mine, column, 0.0), axis=0, keepdims=True)


def zero_kernel(out_ref):
    out_ref[...] = jnp.zeros_like(out_ref)


def pack_kernel(state_ref, weights_ref, links_ref, land_ref, depth_ref, zero_ref, out_ref):
    surface = state_ref[0, 0]
    rows = surface.shape[0]
    table = links_ref[0, 0, 0].astype(jnp.float32)
    count = table.shape[1]
    source = as_column(table[0:1])
    weight_id = as_column(table[3:4])
    entries = weights_ref.shape[1]
    weight = jnp.sum(
        jnp.where(weight_id == lane_ids((count, entries)).astype(jnp.float32), weights_ref[...], 0.0),
        axis=1,
        keepdims=True,
    )
    picked = jnp.zeros((count, surface.shape[1]), jnp.float32)
    for row in range(rows):
        picked = jnp.where(source == float(row), surface[row : row + 1], picked)
    out_ref[0:count] = weight * picked
    code = table[1:2] * float(rows) + table[2:3]
    diagonal = lax.broadcasted_iota(jnp.int32, (count, 128), 0) == lane_ids((count, 128))
    weight_row = jnp.sum(jnp.where(diagonal, weight, 0.0), axis=0, keepdims=True)
    code_row = jnp.sum(jnp.where(diagonal, as_column(code), 0.0), axis=0, keepdims=True)
    land = as_column(land_ref[...].astype(jnp.float32))
    deep = land * as_column(depth_ref[...].astype(jnp.float32))
    out_ref[count : count + 1] = code_row
    out_ref[count + 1 : count + 2] = weight_row
    out_ref[count + 2 : count + 3] = spread(land)
    out_ref[count + 3 : count + 4] = spread(deep)
    out_ref[count + 4 : count + 8] = zero_ref[0:4]
    out_ref[count + 8 :] = surface


def operator_kernel(mixing_ref, diffuse_ref, mix_ref, rate_ref):
    levels = mixing_ref.shape[1]
    mix = mixing_ref[0]
    top = mix.astype(jnp.bfloat16)
    rest = (mix - top.astype(jnp.float32)).astype(jnp.bfloat16)
    mix_ref[...] = jnp.zeros_like(mix_ref)
    mix_ref[:, 0:levels] = top
    mix_ref[:, levels : 2 * levels] = top
    mix_ref[:, 2 * levels : 3 * levels] = rest
    rate = jnp.broadcast_to(as_column(diffuse_ref[...]), (levels, 128))
    rate_ref[0] = rate
    rate_ref[1] = 1.0 - 4.0 * rate


def fold_shift(group):
    return group % 2 * 4 + group // 2 * 64


def edge_kernel(state_ref, near_ref, far_ref, first_ref, second_ref):
    levels, rows, cells = state_ref.shape[1:]
    lat_odd = lax.rem(lax.axis_index("lat"), 2) == 1
    lon_odd = lax.rem(lax.axis_index("lon"), 2) == 1
    lane = lane_ids((levels, 128))
    first = last = jnp.zeros((levels, 128), jnp.float32)
    tiles = []
    for row in range(rows):
        tile = state_ref[0, :, row, :]
        tiles.append(tile)
        turned = roll(tile, row * EDGE)
        first = jnp.where(lane // EDGE == row, turned, first)
        last = jnp.where(lane // EDGE == (row - 1) % (128 // EDGE), turned, last)
    last = roll(last, 4)
    near, far = jnp.where(lon_odd, first, last), jnp.where(lon_odd, last, first)
    for ref, cells_out in ((near_ref, near), (far_ref, far)):
        folded = jnp.zeros((FOLD, 128), jnp.float32)
        lane_fold = lane_ids((FOLD, 128))
        for group in range(-(-levels // FOLD)):
            part = cells_out[group * FOLD : min((group + 1) * FOLD, levels)]
            if part.shape[0] < FOLD:
                part = jnp.concatenate([part, jnp.zeros((FOLD - part.shape[0], 128), jnp.float32)], axis=0)
            mine = (lane_fold // 64 == group // 2) & (lane_fold % EDGE // 4 == group % 2)
            folded = jnp.where(mine, roll(part, fold_shift(group)), folded)
        ref[...] = folded
    for k in range(4):
        low, high = tiles[k], tiles[rows - 4 + k]
        first_ref[k] = jnp.where(lat_odd, low, high)
        second_ref[k] = jnp.where(lat_odd, high, low)


def flux_kernel(count, slices, east_west, *refs):
    crossed_ref, *packs, own_ref, first_ref, second_ref = refs
    surface = crossed_ref[count + 8 :]
    rows = surface.shape[0]
    levels = own_ref.shape[0] - 2 * rows - 8
    lon, lon_count = lax.axis_index("lon"), lax.axis_size("lon")
    odd = lax.rem(lon, 2) == 1
    ocean = lax.axis_index("comp") == 0
    here = lon * rows
    after = lax.rem(lon + 1, lon_count) * rows
    before = lax.rem(lon + lon_count - 1, lon_count) * rows
    index = lax.broadcasted_iota(jnp.int32, (3 * rows, count), 0)
    wanted = jnp.where(
        index < rows, here + index, jnp.where(index < 2 * rows, after + index - rows, before + index - 2 * rows)
    ).astype(jnp.float32)
    accum = jnp.zeros((3 * rows, 128), jnp.float32)
    totals = jnp.zeros((3 * rows, 1), jnp.float32)
    for which, offset in slices:
        ref = packs[which]
        hit = (wanted == ref[offset + count : offset + count + 1, 0:count]).astype(jnp.float32)
        accum += jnp.dot(
            hit,
            ref[offset : offset + count],
            precision=lax.Precision.HIGHEST,
            preferred_element_type=jnp.float32,
        )
        totals += jnp.sum(
            hit * ref[offset + count + 1 : offset + count + 2, 0:count], axis=1, keepdims=True
        )
    imported = accum / jnp.maximum(totals, 1.0)
    spread_rows = packs[0][count + 2 : count + 4]
    column = lax.broadcasted_iota(jnp.int32, (rows, 128), 0) * EDGE == lane_ids((rows, 128))
    land = jnp.sum(jnp.where(column, spread_rows[0:1], 0.0), axis=1, keepdims=True)
    deep = jnp.sum(jnp.where(column, spread_rows[1:2], 0.0), axis=1, keepdims=True)
    all_levels = float(levels)
    deep = jnp.where(ocean, deep, all_levels)
    (first, first_at), (second, second_at) = east_west
    lane = lane_ids((1, 128))
    from_east = lax.rem(lane, EDGE) < 4

    one = packs[first][first_at : first_at + FOLD + count + 4]
    two = packs[second][second_at : second_at + FOLD + count + 4]
    to_east, to_west = jnp.where(odd, two, one), jnp.where(odd, one, two)

    def beside(at):
        return jnp.where(from_east, to_east[at : at + 1], to_west[at : at + 1])

    pieces = []
    for start in range(0, levels, FOLD):
        size = min(FOLD, levels - start)
        shift = fold_shift(start // FOLD)
        pieces.append(
            jnp.where(
                lane_ids((size, 128)) % EDGE < 4, roll(to_east[:size], -shift), roll(to_west[:size], 4 - shift)
            )
        )
    whole = jnp.concatenate(pieces, axis=0)
    land_beside = beside(FOLD + count + 2)
    deep_beside = jnp.where(ocean, beside(FOLD + count + 3), all_levels)
    imported_beside = jnp.zeros((1, 128), jnp.float32)
    for row in range(rows):
        start = row * EDGE
        east = roll(imported[rows + row : rows + row + 1], start)
        west = roll(imported[2 * rows + row : 2 * rows + row + 1], start + 8)
        mine = (lane >= start) & (lane < start + EDGE)
        imported_beside = jnp.where(mine, jnp.where(from_east, east, west), imported_beside)
    flux_beside = coupling_rate * land_beside * (imported_beside - whole[0:1])
    flux = coupling_rate * land * (imported[0:rows] - surface)
    deep = jnp.broadcast_to(deep, (rows, 128))
    own_ref[0:levels] = roll(whole, STEPS * EDGE)
    own_ref[levels : levels + rows] = flux
    own_ref[levels + rows : levels + 2 * rows] = deep
    own_ref[levels + 2 * rows : levels + 2 * rows + 1] = roll(flux_beside, STEPS * EDGE)
    own_ref[levels + 2 * rows + 1 : levels + 2 * rows + 2] = roll(deep_beside, STEPS * EDGE)
    own_ref[levels + 2 * rows + 2 :] = jnp.zeros((6, 128), jnp.float32)
    width = STEPS * EDGE
    sides = []
    for at in (0, rows - STEPS):
        lane_at = at * EDGE
        folded = jnp.zeros((FOLD, 128), jnp.float32)
        lane_fold = lane_ids((FOLD, 128))
        for group in range(-(-levels // FOLD)):
            part = whole[group * FOLD : min((group + 1) * FOLD, levels)]
            if part.shape[0] < FOLD:
                extra = jnp.zeros((FOLD - part.shape[0], 128), jnp.float32)
                index = lax.broadcasted_iota(jnp.int32, extra.shape, 0)
                extra = jnp.where(index == 0, flux_beside, jnp.where(index == 1, deep_beside, extra))
                part = jnp.concatenate([part, extra], axis=0)
            folded = jnp.where(lane_fold // width == group, roll(part, group * width - lane_at), folded)
        sides.append((folded, flux[at : at + STEPS], deep[at : at + STEPS]))
    lat_odd = lax.rem(lax.axis_index("lat"), 2) == 1
    starts = (0, FOLD, FOLD + STEPS, FOLD + 2 * STEPS)
    for (low, high), begin, end in zip(zip(*sides), starts, starts[1:]):
        first_ref[begin:end] = jnp.where(lat_odd, low, high)
        second_ref[begin:end] = jnp.where(lat_odd, high, low)


def halves(value):
    hi = value.astype(jnp.bfloat16)
    return hi, (value - hi.astype(jnp.float32)).astype(jnp.bfloat16)


class Update:
    def __init__(self, mix_ref, rate_ref):
        self.mixer, self.rate_ref = mix_ref[...], rate_ref
        self.levels = rate_ref.shape[1]
        self.pad = jnp.zeros((self.mixer.shape[1] - 3 * self.levels, 256), jnp.bfloat16)
        tail = lax.broadcasted_iota(jnp.int32, (8, 128), 0)
        self.first = tail == 0
        self.tail = (tail + (self.levels - 8)).astype(jnp.float32)

    def moved(self, x, neighbours, flux, deep):
        value = self.rate_ref[1] * x + self.rate_ref[0] * neighbours
        head = value[:8] + jnp.where(self.first, flux, 0.0)
        tail = jnp.where(self.tail < deep, value[-8:], 0.0)
        return jnp.concatenate([head, value[8:-8], tail], axis=0)

    def mixed(self, values):
        value = jnp.concatenate(values, axis=1)
        hi, lo = halves(value)
        full = jnp.concatenate([hi, lo, hi, self.pad[:, : value.shape[1]]], axis=0)
        out = jnp.dot(self.mixer, full, preferred_element_type=jnp.float32)
        return [out[:, 128 * k : 128 * (k + 1)] for k in range(len(values))]

    def settled(self, new, x, deep):
        sea = jnp.broadcast_to(deep, (self.levels - 8, 128)) > 0.0
        body = jnp.where(sea, new[:-8], x[:-8])
        tail = jnp.where(self.tail < deep, new[-8:], x[-8:])
        return jnp.concatenate([body, tail], axis=0)

    def rows(self, tiles, flux, deep):
        values = [
            self.moved(x, above + below + roll(x, 1) + roll(x, -1), f, d)
            for (above, x, below), f, d in zip(tiles, flux, deep)
        ]
        return [self.settled(new, t[1], d) for new, t, d in zip(self.mixed(values), tiles, deep)]


def lat_place():
    lat = lax.axis_index("lat")
    return lax.rem(lat, 2) == 1, (lat > 0) & (lat < lax.axis_size("lat") - 1)


def inner_kernel(state_ref, own_ref, rows1_ref, rows2_ref, mix_ref, rate_ref, x_ref, side_ref, *inner_refs):
    levels, rows, cells = state_ref.shape[1:]
    slots = rows + 2 * STEPS
    odd, inside = lat_place()
    first_at = jnp.where(odd, 0, rows + STEPS)
    for k in range(STEPS):
        x_ref[first_at + k] = rows1_ref[k]
        x_ref[rows + STEPS - first_at + k] = jnp.where(inside, rows2_ref[k], 0.0)
    for row in range(rows):
        x_ref[STEPS + row] = state_ref[0, :, row, :]
    update = Update(mix_ref, rate_ref)
    flux = [own_ref[levels + r : levels + r + 1] for r in range(rows)]
    deep = [own_ref[levels + rows + r : levels + rows + r + 1] for r in range(rows)]
    source, first = x_ref, 0
    for step in range(STEPS):
        target, at = inner_refs[step], STEPS + step
        for slot in range(at, slots - at, 2):
            pair = (slot, slot + 1)
            tiles = [[source[s - first + k] for k in (-1, 0, 1)] for s in pair]
            new = update.rows(tiles, [flux[s - STEPS] for s in pair], [deep[s - STEPS] for s in pair])
            for s, tile in zip(pair, new):
                target[s - at] = tile
        source, first = target, at
    lane = lane_ids((levels, 128))
    left = right = jnp.zeros((levels, 128), jnp.float32)
    for slot in range(slots):
        start = slot * EDGE
        turned = roll(x_ref[slot], start)
        right = jnp.where(lane // EDGE == slot, turned, right)
        left = jnp.where(lane // EDGE == (slot - 1) % slots, turned, left)
    side_ref[0] = roll(left, EDGE)
    side_ref[1] = right


def outer_kernel(own_ref, msg2_ref, msg1_ref, mix_ref, rate_ref, x_ref, side_ref, *refs):
    inner_refs, out_ref, outer_refs = refs[:STEPS], refs[STEPS], refs[STEPS + 1 :]
    levels, rows, cells = out_ref.shape[1:]
    slots = rows + 2 * STEPS
    odd, inside = lat_place()
    one, two = msg1_ref[...], jnp.where(inside, msg2_ref[...], 0.0)
    top, bottom = jnp.where(odd, one, two), jnp.where(odd, two, one)

    def per_slot(at, own_at, slot):
        if slot < STEPS:
            return top[at + slot : at + slot + 1]
        if slot < STEPS + rows:
            return own_ref[own_at + slot - STEPS : own_at + slot - STEPS + 1]
        return bottom[at + slot - STEPS - rows : at + slot - STEPS - rows + 1]

    flux_rows = [per_slot(FOLD, levels, s) for s in range(slots)]
    deep_rows = [per_slot(FOLD + STEPS, levels + rows, s) for s in range(slots)]
    lane1 = lane_ids((1, 128))
    lane = lane_ids((levels, 128))
    place = lane % EDGE
    width = STEPS * EDGE

    def around(upper, own, lower, group):
        at = lane_ids(own.shape)
        upper, lower = roll(upper, -group * width), roll(lower, 128 - width - group * width)
        return jnp.where(at < width, upper, jnp.where(at < 128 - width, own, lower))

    pieces = []
    for start in range(0, levels, FOLD):
        size = min(FOLD, levels - start)
        pieces.append(around(top[:size], own_ref[start : start + size], bottom[:size], start // FOLD))
    mid = jnp.concatenate(pieces, axis=0)
    beside = levels % FOLD
    at = levels + 2 * rows
    flux_mid, deep_mid = (
        around(
            top[beside + k : beside + k + 1],
            own_ref[at + k : at + k + 1],
            bottom[beside + k : beside + k + 1],
            levels // FOLD,
        )
        for k in range(2)
    )
    left, right = side_ref[0], side_ref[1]
    flux_left = flux_right = deep_side = jnp.zeros((1, 128), jnp.float32)
    for slot in range(slots):
        start = slot * EDGE
        mine1 = (lane1 >= start) & (lane1 < start + EDGE)
        flux_left = jnp.where(mine1, roll(flux_rows[slot], start + EDGE), flux_left)
        flux_right = jnp.where(mine1, roll(flux_rows[slot], start), flux_right)
        deep_side = jnp.where(mine1, deep_rows[slot], deep_side)

    def strip(tile, west, east):
        above_below = roll(tile, EDGE) + roll(tile, -EDGE)
        to_west, to_east = roll(tile, 1), roll(tile, -1)
        if west is not None:
            to_west = jnp.where(place == 0, roll(west, 1 - EDGE), to_west)
        if east is not None:
            to_east = jnp.where(place == EDGE - 1, roll(east, EDGE - 1), to_east)
        return above_below + to_west + to_east

    update = Update(mix_ref, rate_ref)

    def tile_at(step, s):
        if step == 0:
            return x_ref[s]
        if 3 + step <= s <= slots - 4 - step:
            return inner_refs[step - 1][s - 3 - step]
        return outer_refs[step - 1][s - step if s < slots // 2 else s - (slots - 6 - step)]

    def put(s, tile):
        tile = jnp.where((lane < 4) | (lane >= cells - 4), roll(sides, -s * EDGE), tile)
        out_ref[0, :, s - STEPS, :] = tile

    for step in range(STEPS):
        last = step == STEPS - 1
        z_left = update.moved(left, strip(left, None, mid), flux_left, deep_side)
        z_right = update.moved(right, strip(right, mid, None), flux_right, deep_side)
        new_left, new_right = update.mixed([z_left, z_right])
        if not last:
            z_mid = update.moved(mid, strip(mid, left, right), flux_mid, deep_mid)
            mid = update.settled(update.mixed([z_mid])[0], mid, deep_mid)
        left = update.settled(new_left, left, deep_side)
        right = update.settled(new_right, right, deep_side)
        if last:
            sides = jnp.where(place < 4, right, roll(left, -EDGE))
        low_rows = list(range(step + 1, step + 4))
        todo = low_rows + [slots - 1 - s for s in reversed(low_rows)]
        for k in range(0, len(todo), 2):
            pair = todo[k : k + 2]
            tiles = [[tile_at(step, s + j) for j in (-1, 0, 1)] for s in pair]
            new = update.rows(tiles, [flux_rows[s] for s in pair], [deep_rows[s] for s in pair])
            for j, (s, tile) in enumerate(zip(pair, new)):
                if last:
                    put(s, tile)
                else:
                    outer_refs[step][k + j] = tile
    for s in (slots // 2 - 1, slots // 2):
        put(s, inner_refs[STEPS - 1][s - slots // 2 + 1])


def kernel_call(body, out_shape, blocks, scratch=(), flops=0, nbytes=0, vmem=VMEM_LIMIT, grid=()):
    return pl.pallas_call(
        body,
        out_shape=out_shape,
        grid=grid,
        in_specs=blocks,
        out_specs=jax.tree.map(lambda _: vmem_spec(), out_shape),
        scratch_shapes=scratch,
        compiler_params=pltpu.CompilerParams(vmem_limit_bytes=vmem),
        cost_estimate=pl.CostEstimate(flops=flops, bytes_accessed=nbytes, transcendentals=0),
    )


def f32(*shape):
    return jax.ShapeDtypeStruct(shape, jnp.float32)


def exchange(value, axis, partner):
    size = lax.axis_size(axis)
    pairs = [(i, partner(i)) for i in range(size) if 0 <= partner(i) < size]
    return lax.ppermute(value, axis, pairs)


def exchange_over(value, axis, partner):
    size, sections = lax.axis_size(axis), lax.axis_size("comp")
    pairs = [
        (section * size + i, (sections - 1 - section) * size + partner(i))
        for section in range(sections)
        for i in range(size)
    ]
    return lax.ppermute(value, ("comp", axis), pairs)


def on_device(state, mixing, diffusivity, weights, links, land, depth):
    levels, rows, cells = state.shape[1:]
    count = links.shape[-1]
    pack_rows = count + 8
    lat_count, lon_count = lax.axis_size("lat"), lax.axis_size("lon")

    def near(i):
        return i ^ 1

    def far_round(i):
        return (i - 1 if i % 2 == 0 else i + 1) % lon_count

    def far_lat(i):
        return (i - 1 if i % 2 == 0 else i + 1) % lat_count

    zeros = kernel_call(
        zero_kernel, f32(8, 128), [], flops=2_000_000_000, nbytes=4096, vmem=FRONT_VMEM_LIMIT
    )()
    pack = kernel_call(
        pack_kernel,
        f32(pack_rows + rows, 128),
        [vmem_spec()] * 6,
        flops=2_000_000_000,
        nbytes=700_000,
        vmem=FRONT_VMEM_LIMIT,
    )(state, weights, links, land.reshape(1, rows), depth.reshape(1, rows), zeros)
    state, pack = lax.optimization_barrier((state, pack))
    crossed = exchange(pack, "comp", near)
    edge_near, edge_far, up_down_1, up_down_2 = kernel_call(
        edge_kernel,
        (f32(FOLD, 128),) * 2 + (f32(STEPS, levels, 128),) * 2,
        [vmem_spec()],
        flops=2_000_000_000,
        nbytes=900_000,
        vmem=FRONT_VMEM_LIMIT,
    )(state)
    operators = kernel_call(
        operator_kernel,
        (
            jax.ShapeDtypeStruct((levels, 256), jnp.bfloat16),
            f32(2, levels, 128),
        ),
        [vmem_spec()] * 2,
        flops=2_000_000_000,
        nbytes=100_000,
        vmem=FRONT_VMEM_LIMIT,
    )(mixing, diffusivity)
    operators, edge_near = lax.optimization_barrier((operators, edge_near))
    beside_1 = exchange_over(jnp.concatenate([edge_near, crossed[:pack_rows]], axis=0), "lon", near)
    beside_2 = exchange_over(jnp.concatenate([edge_far, crossed[:pack_rows]], axis=0), "lon", far_round)
    if lon_count == 4:
        across = exchange_over(crossed[:pack_rows], "lon", lambda i: i ^ 2)
        packs = [pack, beside_1, across, beside_2]
        slices = [(0, 0), (1, FOLD), (2, 0), (3, FOLD)]
        east_west = ((1, 0), (3, 0))
    else:
        packs = [pack, beside_1, beside_2, lax.all_gather(pack[:pack_rows], "lon", axis=0, tiled=True)]
        slices = [(3, k * pack_rows) for k in range(lon_count)]
        east_west = ((1, 0), (2, 0))
    rows_1 = exchange(up_down_1, "lat", near)
    rows_2 = exchange(up_down_2, "lat", far_lat)
    rows_1, packs[0] = lax.optimization_barrier((rows_1, packs[0]))
    own, for_first, for_second = kernel_call(
        functools.partial(flux_kernel, count, slices, east_west),
        (f32(levels + 2 * rows + 8, 128),) + (f32(FOLD + 2 * STEPS, 128),) * 2,
        [vmem_spec()] * (1 + len(packs)),
        flops=3_000_000_000,
        nbytes=100_000,
        vmem=FRONT_VMEM_LIMIT,
    )(crossed, *packs)
    own = exchange(own, "comp", near)
    message_2 = exchange_over(for_second, "lat", far_lat)
    message_1 = exchange_over(for_first, "lat", near)
    laid_out = kernel_call(
        inner_kernel,
        (f32(rows + 2 * STEPS, levels, 128), f32(2, levels, 128))
        + tuple(f32(rows - 2 * k, levels, 128) for k in range(STEPS)),
        [vmem_spec()] * 6,
        flops=2_000_000_000,
        nbytes=2_000_000,
    )(state, own, rows_1, rows_2, *operators)
    return kernel_call(
        outer_kernel,
        f32(*state.shape),
        [vmem_spec()] * (5 + len(laid_out)),
        scratch=[pltpu.VMEM((6, levels, 128), jnp.float32)] * (STEPS - 1),
        flops=300_000_000,
        nbytes=2_000_000,
    )(own, message_2, message_1, *operators, *laid_out)


def solution(mesh):
    in_specs = (
        P("comp", None, "lat", "lon"),
        P("comp", None, None),
        P("comp", None),
        P("comp", None),
        P("comp", "lat", "lon", None, None),
        P("lat", "lon"),
        P("lat", "lon"),
    )
    out_specs = P("comp", None, "lat", "lon")
    return jax.shard_map(
        on_device, mesh=mesh, in_specs=in_specs, out_specs=out_specs, check_vma=False
    )
```

```python
import functools

import jax
import jax.numpy as jnp
from jax import lax
from jax.experimental import pallas as pl
from jax.experimental.pallas import tpu as pltpu
from jax.sharding import PartitionSpec as P

STEPS = 4
EDGE = 8
FOLD = 24
AXES = ("comp", "lat", "lon")
VMEM_LIMIT = 8 * 1024 * 1024
FRONT_VMEM_LIMIT = 4 * 1024 * 1024

coupling_rate = 0.5


def vmem_spec():
    return pl.BlockSpec(memory_space=pltpu.VMEM)


def lane_ids(shape):
    return lax.broadcasted_iota(jnp.int32, shape, len(shape) - 1)


def roll(value, shift):
    shift = shift % value.shape[-1]
    return value if shift == 0 else pltpu.roll(value, shift, 1)


def as_column(row):
    n = row.shape[1]
    diagonal = lax.broadcasted_iota(jnp.int32, (n, n), 0) == lane_ids((n, n))
    return jnp.sum(jnp.where(diagonal, row, 0.0), axis=1, keepdims=True)


def spread(column):
    rows = column.shape[0]
    shape = (rows, 128)
    mine = lane_ids(shape) // EDGE == lax.broadcasted_iota(jnp.int32, shape, 0)
    return jnp.sum(jnp.where(mine, column, 0.0), axis=0, keepdims=True)


def zero_kernel(out_ref):
    out_ref[...] = jnp.zeros_like(out_ref)


def pack_kernel(state_ref, weights_ref, links_ref, land_ref, depth_ref, zero_ref, out_ref):
    surface = state_ref[0, 0]
    rows = surface.shape[0]
    table = links_ref[0, 0, 0].astype(jnp.float32)
    count = table.shape[1]
    source = as_column(table[0:1])
    weight_id = as_column(table[3:4])
    entries = weights_ref.shape[1]
    weight = jnp.sum(
        jnp.where(weight_id == lane_ids((count, entries)).astype(jnp.float32), weights_ref[...], 0.0),
        axis=1,
        keepdims=True,
    )
    picked = jnp.zeros((count, surface.shape[1]), jnp.float32)
    for row in range(rows):
        picked = jnp.where(source == float(row), surface[row : row + 1], picked)
    out_ref[0:count] = weight * picked
    code = table[1:2] * float(rows) + table[2:3]
    diagonal = lax.broadcasted_iota(jnp.int32, (count, 128), 0) == lane_ids((count, 128))
    weight_row = jnp.sum(jnp.where(diagonal, weight, 0.0), axis=0, keepdims=True)
    code_row = jnp.sum(jnp.where(diagonal, as_column(code), 0.0), axis=0, keepdims=True)
    land = as_column(land_ref[...].astype(jnp.float32))
    deep = land * as_column(depth_ref[...].astype(jnp.float32))
    out_ref[count : count + 1] = code_row
    out_ref[count + 1 : count + 2] = weight_row
    out_ref[count + 2 : count + 3] = spread(land)
    out_ref[count + 3 : count + 4] = spread(deep)
    out_ref[count + 4 : count + 8] = zero_ref[0:4]
    out_ref[count + 8 :] = surface


def operator_kernel(mixing_ref, diffuse_ref, mix_ref, rate_ref):
    levels = mixing_ref.shape[1]
    mix = mixing_ref[0]
    top = mix.astype(jnp.bfloat16)
    rest = (mix - top.astype(jnp.float32)).astype(jnp.bfloat16)
    mix_ref[...] = jnp.zeros_like(mix_ref)
    mix_ref[:, 0:levels] = top
    mix_ref[:, levels : 2 * levels] = top
    mix_ref[:, 2 * levels : 3 * levels] = rest
    rate = jnp.broadcast_to(as_column(diffuse_ref[...]), (levels, 128))
    rate_ref[0] = rate
    rate_ref[1] = 1.0 - 4.0 * rate


def fold_shift(group):
    return group % 2 * 4 + group // 2 * 64


def edge_kernel(state_ref, near_ref, far_ref, first_ref, second_ref):
    levels, rows, cells = state_ref.shape[1:]
    lat_odd = lax.rem(lax.axis_index("lat"), 2) == 1
    lon_odd = lax.rem(lax.axis_index("lon"), 2) == 1
    lane = lane_ids((levels, 128))
    first = last = jnp.zeros((levels, 128), jnp.float32)
    tiles = jnp.swapaxes(state_ref[0], 0, 1)
    for row in range(rows):
        turned = roll(tiles[row], row * EDGE)
        first = jnp.where(lane // EDGE == row, turned, first)
        last = jnp.where(lane // EDGE == (row - 1) % (128 // EDGE), turned, last)
    last = roll(last, 4)
    near, far = jnp.where(lon_odd, first, last), jnp.where(lon_odd, last, first)
    for ref, cells_out in ((near_ref, near), (far_ref, far)):
        folded = jnp.zeros((FOLD, 128), jnp.float32)
        lane_fold = lane_ids((FOLD, 128))
        for group in range(-(-levels // FOLD)):
            part = cells_out[group * FOLD : min((group + 1) * FOLD, levels)]
            if part.shape[0] < FOLD:
                part = jnp.concatenate([part, jnp.zeros((FOLD - part.shape[0], 128), jnp.float32)], axis=0)
            mine = (lane_fold // 64 == group // 2) & (lane_fold % EDGE // 4 == group % 2)
            folded = jnp.where(mine, roll(part, fold_shift(group)), folded)
        ref[...] = folded
    for k in range(4):
        low, high = tiles[k], tiles[rows - 4 + k]
        first_ref[k] = jnp.where(lat_odd, low, high)
        second_ref[k] = jnp.where(lat_odd, high, low)


def flux_kernel(count, slices, east_west, *refs):
    crossed_ref, *packs, own_ref, first_ref, second_ref = refs
    surface = crossed_ref[count + 8 :]
    rows = surface.shape[0]
    levels = own_ref.shape[0] - 2 * rows - 8
    lon, lon_count = lax.axis_index("lon"), lax.axis_size("lon")
    odd = lax.rem(lon, 2) == 1
    ocean = lax.axis_index("comp") == 0
    here = lon * rows
    after = lax.rem(lon + 1, lon_count) * rows
    before = lax.rem(lon + lon_count - 1, lon_count) * rows
    index = lax.broadcasted_iota(jnp.int32, (3 * rows, count), 0)
    wanted = jnp.where(
        index < rows, here + index, jnp.where(index < 2 * rows, after + index - rows, before + index - 2 * rows)
    ).astype(jnp.float32)
    accum = jnp.zeros((3 * rows, 128), jnp.float32)
    totals = jnp.zeros((3 * rows, 1), jnp.float32)
    for which, offset in slices:
        ref = packs[which]
        hit = (wanted == ref[offset + count : offset + count + 1, 0:count]).astype(jnp.float32)
        accum += jnp.dot(
            hit,
            ref[offset : offset + count],
            precision=lax.Precision.HIGHEST,
            preferred_element_type=jnp.float32,
        )
        totals += jnp.sum(
            hit * ref[offset + count + 1 : offset + count + 2, 0:count], axis=1, keepdims=True
        )
    imported = accum / jnp.maximum(totals, 1.0)
    spread_rows = packs[0][count + 2 : count + 4]
    column = lax.broadcasted_iota(jnp.int32, (rows, 128), 0) * EDGE == lane_ids((rows, 128))
    land = jnp.sum(jnp.where(column, spread_rows[0:1], 0.0), axis=1, keepdims=True)
    deep = jnp.sum(jnp.where(column, spread_rows[1:2], 0.0), axis=1, keepdims=True)
    all_levels = float(levels)
    deep = jnp.where(ocean, deep, all_levels)
    (first, first_at), (second, second_at) = east_west
    lane = lane_ids((1, 128))
    from_east = lax.rem(lane, EDGE) < 4

    one = packs[first][first_at : first_at + FOLD + count + 4]
    two = packs[second][second_at : second_at + FOLD + count + 4]
    to_east, to_west = jnp.where(odd, two, one), jnp.where(odd, one, two)

    def beside(at):
        return jnp.where(from_east, to_east[at : at + 1], to_west[at : at + 1])

    pieces = []
    for start in range(0, levels, FOLD):
        size = min(FOLD, levels - start)
        shift = fold_shift(start // FOLD)
        pieces.append(
            jnp.where(
                lane_ids((size, 128)) % EDGE < 4, roll(to_east[:size], -shift), roll(to_west[:size], 4 - shift)
            )
        )
    whole = jnp.concatenate(pieces, axis=0)
    land_beside = beside(FOLD + count + 2)
    deep_beside = jnp.where(ocean, beside(FOLD + count + 3), all_levels)
    imported_beside = jnp.zeros((1, 128), jnp.float32)
    for row in range(rows):
        start = row * EDGE
        east = roll(imported[rows + row : rows + row + 1], start)
        west = roll(imported[2 * rows + row : 2 * rows + row + 1], start + 8)
        mine = (lane >= start) & (lane < start + EDGE)
        imported_beside = jnp.where(mine, jnp.where(from_east, east, west), imported_beside)
    flux_beside = coupling_rate * land_beside * (imported_beside - whole[0:1])
    flux = coupling_rate * land * (imported[0:rows] - surface)
    deep = jnp.broadcast_to(deep, (rows, 128))
    own_ref[0:levels] = roll(whole, STEPS * EDGE)
    own_ref[levels : levels + rows] = flux
    own_ref[levels + rows : levels + 2 * rows] = deep
    own_ref[levels + 2 * rows : levels + 2 * rows + 1] = roll(flux_beside, STEPS * EDGE)
    own_ref[levels + 2 * rows + 1 : levels + 2 * rows + 2] = roll(deep_beside, STEPS * EDGE)
    own_ref[levels + 2 * rows + 2 :] = jnp.zeros((6, 128), jnp.float32)
    width = STEPS * EDGE
    sides = []
    for at in (0, rows - STEPS):
        lane_at = at * EDGE
        folded = jnp.zeros((FOLD, 128), jnp.float32)
        lane_fold = lane_ids((FOLD, 128))
        for group in range(-(-levels // FOLD)):
            part = whole[group * FOLD : min((group + 1) * FOLD, levels)]
            if part.shape[0] < FOLD:
                extra = jnp.zeros((FOLD - part.shape[0], 128), jnp.float32)
                index = lax.broadcasted_iota(jnp.int32, extra.shape, 0)
                extra = jnp.where(index == 0, flux_beside, jnp.where(index == 1, deep_beside, extra))
                part = jnp.concatenate([part, extra], axis=0)
            folded = jnp.where(lane_fold // width == group, roll(part, group * width - lane_at), folded)
        sides.append((folded, flux[at : at + STEPS], deep[at : at + STEPS]))
    lat_odd = lax.rem(lax.axis_index("lat"), 2) == 1
    starts = (0, FOLD, FOLD + STEPS, FOLD + 2 * STEPS)
    for (low, high), begin, end in zip(zip(*sides), starts, starts[1:]):
        first_ref[begin:end] = jnp.where(lat_odd, low, high)
        second_ref[begin:end] = jnp.where(lat_odd, high, low)


def halves(value):
    hi = value.astype(jnp.bfloat16)
    return hi, (value - hi.astype(jnp.float32)).astype(jnp.bfloat16)


class Update:
    def __init__(self, mix_ref, rate_ref):
        self.mixer, self.rate_ref = mix_ref[...], rate_ref
        self.levels = rate_ref.shape[1]
        self.pad = jnp.zeros((self.mixer.shape[1] - 3 * self.levels, 256), jnp.bfloat16)
        tail = lax.broadcasted_iota(jnp.int32, (8, 128), 0)
        self.first = tail == 0
        self.tail = (tail + (self.levels - 8)).astype(jnp.float32)

    def moved(self, x, neighbours, flux, deep):
        value = self.rate_ref[1] * x + self.rate_ref[0] * neighbours
        head = value[:8] + jnp.where(self.first, flux, 0.0)
        tail = jnp.where(self.tail < deep, value[-8:], 0.0)
        return jnp.concatenate([head, value[8:-8], tail], axis=0)

    def mixed(self, values):
        value = jnp.concatenate(values, axis=1)
        hi, lo = halves(value)
        full = jnp.concatenate([hi, lo, hi, self.pad[:, : value.shape[1]]], axis=0)
        out = jnp.dot(self.mixer, full, preferred_element_type=jnp.float32)
        return [out[:, 128 * k : 128 * (k + 1)] for k in range(len(values))]

    def settled(self, new, x, deep):
        sea = jnp.broadcast_to(deep, (self.levels - 8, 128)) > 0.0
        body = jnp.where(sea, new[:-8], x[:-8])
        tail = jnp.where(self.tail < deep, new[-8:], x[-8:])
        return jnp.concatenate([body, tail], axis=0)

    def rows(self, tiles, flux, deep):
        values = [
            self.moved(x, above + below + roll(x, 1) + roll(x, -1), f, d)
            for (above, x, below), f, d in zip(tiles, flux, deep)
        ]
        return [self.settled(new, t[1], d) for new, t, d in zip(self.mixed(values), tiles, deep)]


def lat_place():
    lat = lax.axis_index("lat")
    return lax.rem(lat, 2) == 1, (lat > 0) & (lat < lax.axis_size("lat") - 1)


def inner_kernel(state_ref, own_ref, rows1_ref, rows2_ref, mix_ref, rate_ref, x_ref, side_ref, *inner_refs):
    levels, rows, cells = state_ref.shape[1:]
    slots = rows + 2 * STEPS
    odd, inside = lat_place()
    first_at = jnp.where(odd, 0, rows + STEPS)
    for k in range(STEPS):
        x_ref[first_at + k] = rows1_ref[k]
        x_ref[rows + STEPS - first_at + k] = jnp.where(inside, rows2_ref[k], 0.0)
    x_ref[STEPS : STEPS + rows] = jnp.swapaxes(state_ref[0], 0, 1)
    update = Update(mix_ref, rate_ref)
    flux = [own_ref[levels + r : levels + r + 1] for r in range(rows)]
    deep = [own_ref[levels + rows + r : levels + rows + r + 1] for r in range(rows)]
    source, first = x_ref, 0
    for step in range(STEPS):
        target, at = inner_refs[step], STEPS + step
        for slot in range(at, slots - at, 2):
            pair = (slot, slot + 1)
            tiles = [[source[s - first + k] for k in (-1, 0, 1)] for s in pair]
            new = update.rows(tiles, [flux[s - STEPS] for s in pair], [deep[s - STEPS] for s in pair])
            for s, tile in zip(pair, new):
                target[s - at] = tile
        source, first = target, at
    lane = lane_ids((levels, 128))
    left = right = jnp.zeros((levels, 128), jnp.float32)
    for slot in range(slots):
        start = slot * EDGE
        turned = roll(x_ref[slot], start)
        right = jnp.where(lane // EDGE == slot, turned, right)
        left = jnp.where(lane // EDGE == (slot - 1) % slots, turned, left)
    side_ref[0] = roll(left, EDGE)
    side_ref[1] = right


def outer_kernel(own_ref, msg2_ref, msg1_ref, mix_ref, rate_ref, x_ref, side_ref, *refs):
    inner_refs, out_ref, outer_refs = refs[:STEPS], refs[STEPS], refs[STEPS + 1 :]
    levels, rows, cells = out_ref.shape[1:]
    slots = rows + 2 * STEPS
    odd, inside = lat_place()
    one, two = msg1_ref[...], jnp.where(inside, msg2_ref[...], 0.0)
    top, bottom = jnp.where(odd, one, two), jnp.where(odd, two, one)

    def per_slot(at, own_at, slot):
        if slot < STEPS:
            return top[at + slot : at + slot + 1]
        if slot < STEPS + rows:
            return own_ref[own_at + slot - STEPS : own_at + slot - STEPS + 1]
        return bottom[at + slot - STEPS - rows : at + slot - STEPS - rows + 1]

    flux_rows = [per_slot(FOLD, levels, s) for s in range(slots)]
    deep_rows = [per_slot(FOLD + STEPS, levels + rows, s) for s in range(slots)]
    lane1 = lane_ids((1, 128))
    lane = lane_ids((levels, 128))
    place = lane % EDGE
    width = STEPS * EDGE

    def around(upper, own, lower, group):
        at = lane_ids(own.shape)
        upper, lower = roll(upper, -group * width), roll(lower, 128 - width - group * width)
        return jnp.where(at < width, upper, jnp.where(at < 128 - width, own, lower))

    pieces = []
    for start in range(0, levels, FOLD):
        size = min(FOLD, levels - start)
        pieces.append(around(top[:size], own_ref[start : start + size], bottom[:size], start // FOLD))
    mid = jnp.concatenate(pieces, axis=0)
    beside = levels % FOLD
    at = levels + 2 * rows
    flux_mid, deep_mid = (
        around(
            top[beside + k : beside + k + 1],
            own_ref[at + k : at + k + 1],
            bottom[beside + k : beside + k + 1],
            levels // FOLD,
        )
        for k in range(2)
    )
    left, right = side_ref[0], side_ref[1]
    flux_left = flux_right = deep_side = jnp.zeros((1, 128), jnp.float32)
    for slot in range(slots):
        start = slot * EDGE
        mine1 = (lane1 >= start) & (lane1 < start + EDGE)
        flux_left = jnp.where(mine1, roll(flux_rows[slot], start + EDGE), flux_left)
        flux_right = jnp.where(mine1, roll(flux_rows[slot], start), flux_right)
        deep_side = jnp.where(mine1, deep_rows[slot], deep_side)

    def strip(tile, west, east):
        above_below = roll(tile, EDGE) + roll(tile, -EDGE)
        to_west, to_east = roll(tile, 1), roll(tile, -1)
        if west is not None:
            to_west = jnp.where(place == 0, roll(west, 1 - EDGE), to_west)
        if east is not None:
            to_east = jnp.where(place == EDGE - 1, roll(east, EDGE - 1), to_east)
        return above_below + to_west + to_east

    update = Update(mix_ref, rate_ref)

    def tile_at(step, s):
        if step == 0:
            return x_ref[s]
        if 3 + step <= s <= slots - 4 - step:
            return inner_refs[step - 1][s - 3 - step]
        return outer_refs[step - 1][s - step if s < slots // 2 else s - (slots - 6 - step)]

    done = [None] * rows

    def put(s, tile):
        tile = jnp.where((lane < 4) | (lane >= cells - 4), roll(sides, -s * EDGE), tile)
        done[s - STEPS] = tile

    for step in range(STEPS):
        last = step == STEPS - 1
        z_left = update.moved(left, strip(left, None, mid), flux_left, deep_side)
        z_right = update.moved(right, strip(right, mid, None), flux_right, deep_side)
        new_left, new_right = update.mixed([z_left, z_right])
        if not last:
            z_mid = update.moved(mid, strip(mid, left, right), flux_mid, deep_mid)
            mid = update.settled(update.mixed([z_mid])[0], mid, deep_mid)
        left = update.settled(new_left, left, deep_side)
        right = update.settled(new_right, right, deep_side)
        if last:
            sides = jnp.where(place < 4, right, roll(left, -EDGE))
        low_rows = list(range(step + 1, step + 4))
        todo = low_rows + [slots - 1 - s for s in reversed(low_rows)]
        for k in range(0, len(todo), 2):
            pair = todo[k : k + 2]
            tiles = [[tile_at(step, s + j) for j in (-1, 0, 1)] for s in pair]
            new = update.rows(tiles, [flux_rows[s] for s in pair], [deep_rows[s] for s in pair])
            for j, (s, tile) in enumerate(zip(pair, new)):
                if last:
                    put(s, tile)
                else:
                    outer_refs[step][k + j] = tile
    for s in (slots // 2 - 1, slots // 2):
        put(s, inner_refs[STEPS - 1][s - slots // 2 + 1])
    out_ref[0] = jnp.swapaxes(jnp.stack(done, axis=0), 0, 1)


def kernel_call(body, out_shape, blocks, scratch=(), flops=0, nbytes=0, vmem=VMEM_LIMIT, grid=()):
    return pl.pallas_call(
        body,
        out_shape=out_shape,
        grid=grid,
        in_specs=blocks,
        out_specs=jax.tree.map(lambda _: vmem_spec(), out_shape),
        scratch_shapes=scratch,
        compiler_params=pltpu.CompilerParams(vmem_limit_bytes=vmem),
        cost_estimate=pl.CostEstimate(flops=flops, bytes_accessed=nbytes, transcendentals=0),
    )


def f32(*shape):
    return jax.ShapeDtypeStruct(shape, jnp.float32)


def exchange(value, axis, partner):
    size = lax.axis_size(axis)
    pairs = [(i, partner(i)) for i in range(size) if 0 <= partner(i) < size]
    return lax.ppermute(value, axis, pairs)


def exchange_over(value, axis, partner):
    size, sections = lax.axis_size(axis), lax.axis_size("comp")
    pairs = [
        (section * size + i, (sections - 1 - section) * size + partner(i))
        for section in range(sections)
        for i in range(size)
    ]
    return lax.ppermute(value, ("comp", axis), pairs)


def on_device(state, mixing, diffusivity, weights, links, land, depth):
    levels, rows, cells = state.shape[1:]
    count = links.shape[-1]
    pack_rows = count + 8
    lat_count, lon_count = lax.axis_size("lat"), lax.axis_size("lon")

    def near(i):
        return i ^ 1

    def far_round(i):
        return (i - 1 if i % 2 == 0 else i + 1) % lon_count

    def far_lat(i):
        return (i - 1 if i % 2 == 0 else i + 1) % lat_count

    zeros = kernel_call(
        zero_kernel, f32(8, 128), [], flops=2_000_000_000, nbytes=4096, vmem=FRONT_VMEM_LIMIT
    )()
    pack = kernel_call(
        pack_kernel,
        f32(pack_rows + rows, 128),
        [vmem_spec()] * 6,
        flops=2_000_000_000,
        nbytes=700_000,
        vmem=FRONT_VMEM_LIMIT,
    )(state, weights, links, land.reshape(1, rows), depth.reshape(1, rows), zeros)
    state, pack = lax.optimization_barrier((state, pack))
    crossed = exchange(pack, "comp", near)
    edge_near, edge_far, up_down_1, up_down_2 = kernel_call(
        edge_kernel,
        (f32(FOLD, 128),) * 2 + (f32(STEPS, levels, 128),) * 2,
        [vmem_spec()],
        flops=2_000_000_000,
        nbytes=900_000,
        vmem=FRONT_VMEM_LIMIT,
    )(state)
    operators = kernel_call(
        operator_kernel,
        (
            jax.ShapeDtypeStruct((levels, 256), jnp.bfloat16),
            f32(2, levels, 128),
        ),
        [vmem_spec()] * 2,
        flops=2_000_000_000,
        nbytes=100_000,
        vmem=FRONT_VMEM_LIMIT,
    )(mixing, diffusivity)
    operators, edge_near = lax.optimization_barrier((operators, edge_near))
    beside_1 = exchange_over(jnp.concatenate([edge_near, crossed[:pack_rows]], axis=0), "lon", near)
    beside_2 = exchange_over(jnp.concatenate([edge_far, crossed[:pack_rows]], axis=0), "lon", far_round)
    if lon_count == 4:
        across = exchange_over(crossed[:pack_rows], "lon", lambda i: i ^ 2)
        packs = [pack, beside_1, across, beside_2]
        slices = [(0, 0), (1, FOLD), (2, 0), (3, FOLD)]
        east_west = ((1, 0), (3, 0))
    else:
        packs = [pack, beside_1, beside_2, lax.all_gather(pack[:pack_rows], "lon", axis=0, tiled=True)]
        slices = [(3, k * pack_rows) for k in range(lon_count)]
        east_west = ((1, 0), (2, 0))
    rows_1 = exchange(up_down_1, "lat", near)
    rows_2 = exchange(up_down_2, "lat", far_lat)
    rows_1, packs[0] = lax.optimization_barrier((rows_1, packs[0]))
    own, for_first, for_second = kernel_call(
        functools.partial(flux_kernel, count, slices, east_west),
        (f32(levels + 2 * rows + 8, 128),) + (f32(FOLD + 2 * STEPS, 128),) * 2,
        [vmem_spec()] * (1 + len(packs)),
        flops=3_000_000_000,
        nbytes=100_000,
        vmem=FRONT_VMEM_LIMIT,
    )(crossed, *packs)
    own = exchange(own, "comp", near)
    message_2 = exchange_over(for_second, "lat", far_lat)
    message_1 = exchange_over(for_first, "lat", near)
    laid_out = kernel_call(
        inner_kernel,
        (f32(rows + 2 * STEPS, levels, 128), f32(2, levels, 128))
        + tuple(f32(rows - 2 * k, levels, 128) for k in range(STEPS)),
        [vmem_spec()] * 6,
        flops=2_000_000_000,
        nbytes=2_000_000,
    )(state, own, rows_1, rows_2, *operators)
    return kernel_call(
        outer_kernel,
        f32(*state.shape),
        [vmem_spec()] * (5 + len(laid_out)),
        scratch=[pltpu.VMEM((6, levels, 128), jnp.float32)] * (STEPS - 1),
        flops=300_000_000,
        nbytes=2_000_000,
    )(own, message_2, message_1, *operators, *laid_out)


def solution(mesh):
    in_specs = (
        P("comp", None, "lat", "lon"),
        P("comp", None, None),
        P("comp", None),
        P("comp", None),
        P("comp", "lat", "lon", None, None),
        P("lat", "lon"),
        P("lat", "lon"),
    )
    out_specs = P("comp", None, "lat", "lon")
    return jax.shard_map(
        on_device, mesh=mesh, in_specs=in_specs, out_specs=out_specs, check_vma=False
    )
```

```python
import functools

import jax
import jax.numpy as jnp
from jax import lax
from jax.experimental import pallas as pl
from jax.experimental.pallas import tpu as pltpu
from jax.sharding import PartitionSpec as P

STEPS = 4
EDGE = 8
FOLD = 24
AXES = ("comp", "lat", "lon")
VMEM_LIMIT = 8 * 1024 * 1024
FRONT_VMEM_LIMIT = 4 * 1024 * 1024

coupling_rate = 0.5


def vmem_spec():
    return pl.BlockSpec(memory_space=pltpu.VMEM)


def lane_ids(shape):
    return lax.broadcasted_iota(jnp.int32, shape, len(shape) - 1)


def roll(value, shift):
    shift = shift % value.shape[-1]
    return value if shift == 0 else pltpu.roll(value, shift, 1)


def as_column(row):
    n = row.shape[1]
    diagonal = lax.broadcasted_iota(jnp.int32, (n, n), 0) == lane_ids((n, n))
    return jnp.sum(jnp.where(diagonal, row, 0.0), axis=1, keepdims=True)


def spread(column):
    rows = column.shape[0]
    shape = (rows, 128)
    mine = lane_ids(shape) // EDGE == lax.broadcasted_iota(jnp.int32, shape, 0)
    return jnp.sum(jnp.where(mine, column, 0.0), axis=0, keepdims=True)


def zero_kernel(out_ref):
    out_ref[...] = jnp.zeros_like(out_ref)


def pack_kernel(state_ref, weights_ref, links_ref, land_ref, depth_ref, zero_ref, out_ref):
    surface = state_ref[0, 0]
    rows = surface.shape[0]
    table = links_ref[0, 0, 0].astype(jnp.float32)
    count = table.shape[1]
    source = as_column(table[0:1])
    weight_id = as_column(table[3:4])
    entries = weights_ref.shape[1]
    weight = jnp.sum(
        jnp.where(weight_id == lane_ids((count, entries)).astype(jnp.float32), weights_ref[...], 0.0),
        axis=1,
        keepdims=True,
    )
    picked = jnp.zeros((count, surface.shape[1]), jnp.float32)
    for row in range(rows):
        picked = jnp.where(source == float(row), surface[row : row + 1], picked)
    out_ref[0:count] = weight * picked
    code = table[1:2] * float(rows) + table[2:3]
    diagonal = lax.broadcasted_iota(jnp.int32, (count, 128), 0) == lane_ids((count, 128))
    weight_row = jnp.sum(jnp.where(diagonal, weight, 0.0), axis=0, keepdims=True)
    code_row = jnp.sum(jnp.where(diagonal, as_column(code), 0.0), axis=0, keepdims=True)
    land = as_column(land_ref[...].astype(jnp.float32))
    deep = land * as_column(depth_ref[...].astype(jnp.float32))
    out_ref[count : count + 1] = code_row
    out_ref[count + 1 : count + 2] = weight_row
    out_ref[count + 2 : count + 3] = spread(land)
    out_ref[count + 3 : count + 4] = spread(deep)
    out_ref[count + 4 : count + 8] = zero_ref[0:4]
    out_ref[count + 8 :] = surface


def write_operators(mixing_ref, diffuse_ref, mix_ref, rate_ref):
    levels = mixing_ref.shape[1]
    mix = mixing_ref[0]
    top = mix.astype(jnp.bfloat16)
    rest = (mix - top.astype(jnp.float32)).astype(jnp.bfloat16)
    mix_ref[...] = jnp.zeros_like(mix_ref)
    mix_ref[:, 0:levels] = top
    mix_ref[:, levels : 2 * levels] = top
    mix_ref[:, 2 * levels : 3 * levels] = rest
    rate = jnp.broadcast_to(as_column(diffuse_ref[...]), (levels, 128))
    rate_ref[0] = rate
    rate_ref[1] = 1.0 - 4.0 * rate


def fold_shift(group):
    return group % 2 * 4 + group // 2 * 64


def edge_kernel(state_ref, near_ref, far_ref, first_ref, second_ref):
    levels, rows, cells = state_ref.shape[1:]
    lat_odd = lax.rem(lax.axis_index("lat"), 2) == 1
    lon_odd = lax.rem(lax.axis_index("lon"), 2) == 1
    lane = lane_ids((levels, 128))
    first = last = jnp.zeros((levels, 128), jnp.float32)
    tiles = jnp.swapaxes(state_ref[0], 0, 1)
    for row in range(rows):
        turned = roll(tiles[row], row * EDGE)
        first = jnp.where(lane // EDGE == row, turned, first)
        last = jnp.where(lane // EDGE == (row - 1) % (128 // EDGE), turned, last)
    last = roll(last, 4)
    near, far = jnp.where(lon_odd, first, last), jnp.where(lon_odd, last, first)
    for ref, cells_out in ((near_ref, near), (far_ref, far)):
        folded = jnp.zeros((FOLD, 128), jnp.float32)
        lane_fold = lane_ids((FOLD, 128))
        for group in range(-(-levels // FOLD)):
            part = cells_out[group * FOLD : min((group + 1) * FOLD, levels)]
            if part.shape[0] < FOLD:
                part = jnp.concatenate([part, jnp.zeros((FOLD - part.shape[0], 128), jnp.float32)], axis=0)
            mine = (lane_fold // 64 == group // 2) & (lane_fold % EDGE // 4 == group % 2)
            folded = jnp.where(mine, roll(part, fold_shift(group)), folded)
        ref[...] = folded
    for k in range(4):
        low, high = tiles[k], tiles[rows - 4 + k]
        first_ref[k] = jnp.where(lat_odd, low, high)
        second_ref[k] = jnp.where(lat_odd, high, low)


def flux_kernel(count, slices, east_west, *refs):
    crossed_ref, zero_ref, *packs, own_ref, first_ref, second_ref = refs
    surface = crossed_ref[count + 8 :]
    rows = surface.shape[0]
    levels = own_ref.shape[0] - 2 * rows - 8
    lon, lon_count = lax.axis_index("lon"), lax.axis_size("lon")
    odd = lax.rem(lon, 2) == 1
    ocean = lax.axis_index("comp") == 0
    here = lon * rows
    after = lax.rem(lon + 1, lon_count) * rows
    before = lax.rem(lon + lon_count - 1, lon_count) * rows
    index = lax.broadcasted_iota(jnp.int32, (3 * rows, count), 0)
    wanted = jnp.where(
        index < rows, here + index, jnp.where(index < 2 * rows, after + index - rows, before + index - 2 * rows)
    ).astype(jnp.float32)
    accum = jnp.zeros((3 * rows, 128), jnp.float32)
    totals = jnp.zeros((3 * rows, 1), jnp.float32)
    for which, offset in slices:
        ref = packs[which]
        hit = (wanted == ref[offset + count : offset + count + 1, 0:count]).astype(jnp.float32)
        accum += jnp.dot(
            hit,
            ref[offset : offset + count],
            precision=lax.Precision.HIGHEST,
            preferred_element_type=jnp.float32,
        )
        totals += jnp.sum(
            hit * ref[offset + count + 1 : offset + count + 2, 0:count], axis=1, keepdims=True
        )
    imported = accum / jnp.maximum(totals, 1.0)
    spread_rows = packs[0][count + 2 : count + 4]
    column = lax.broadcasted_iota(jnp.int32, (rows, 128), 0) * EDGE == lane_ids((rows, 128))
    land = jnp.sum(jnp.where(column, spread_rows[0:1], 0.0), axis=1, keepdims=True)
    deep = jnp.sum(jnp.where(column, spread_rows[1:2], 0.0), axis=1, keepdims=True)
    all_levels = float(levels)
    deep = jnp.where(ocean, deep, all_levels)
    (first, first_at), (second, second_at) = east_west
    lane = lane_ids((1, 128))
    from_east = lax.rem(lane, EDGE) < 4

    one = packs[first][first_at : first_at + FOLD + count + 4]
    two = packs[second][second_at : second_at + FOLD + count + 4]
    to_east, to_west = jnp.where(odd, two, one), jnp.where(odd, one, two)

    def beside(at):
        return jnp.where(from_east, to_east[at : at + 1], to_west[at : at + 1])

    pieces = []
    for start in range(0, levels, FOLD):
        size = min(FOLD, levels - start)
        shift = fold_shift(start // FOLD)
        pieces.append(
            jnp.where(
                lane_ids((size, 128)) % EDGE < 4, roll(to_east[:size], -shift), roll(to_west[:size], 4 - shift)
            )
        )
    whole = jnp.concatenate(pieces, axis=0)
    land_beside = beside(FOLD + count + 2)
    deep_beside = jnp.where(ocean, beside(FOLD + count + 3), all_levels)
    imported_beside = jnp.zeros((1, 128), jnp.float32)
    for row in range(rows):
        start = row * EDGE
        east = roll(imported[rows + row : rows + row + 1], start)
        west = roll(imported[2 * rows + row : 2 * rows + row + 1], start + 8)
        mine = (lane >= start) & (lane < start + EDGE)
        imported_beside = jnp.where(mine, jnp.where(from_east, east, west), imported_beside)
    flux_beside = coupling_rate * land_beside * (imported_beside - whole[0:1])
    flux = coupling_rate * land * (imported[0:rows] - surface)
    deep = jnp.broadcast_to(deep, (rows, 128))
    own_ref[0:levels] = roll(whole, STEPS * EDGE)
    own_ref[levels : levels + rows] = flux
    own_ref[levels + rows : levels + 2 * rows] = deep
    own_ref[levels + 2 * rows : levels + 2 * rows + 1] = roll(flux_beside, STEPS * EDGE)
    own_ref[levels + 2 * rows + 1 : levels + 2 * rows + 2] = roll(deep_beside, STEPS * EDGE)
    own_ref[levels + 2 * rows + 2 :] = zero_ref[0:6]
    width = STEPS * EDGE
    sides = []
    for at in (0, rows - STEPS):
        lane_at = at * EDGE
        folded = jnp.zeros((FOLD, 128), jnp.float32)
        lane_fold = lane_ids((FOLD, 128))
        for group in range(-(-levels // FOLD)):
            part = whole[group * FOLD : min((group + 1) * FOLD, levels)]
            if part.shape[0] < FOLD:
                extra = jnp.zeros((FOLD - part.shape[0], 128), jnp.float32)
                index = lax.broadcasted_iota(jnp.int32, extra.shape, 0)
                extra = jnp.where(index == 0, flux_beside, jnp.where(index == 1, deep_beside, extra))
                part = jnp.concatenate([part, extra], axis=0)
            folded = jnp.where(lane_fold // width == group, roll(part, group * width - lane_at), folded)
        sides.append((folded, flux[at : at + STEPS], deep[at : at + STEPS]))
    lat_odd = lax.rem(lax.axis_index("lat"), 2) == 1
    starts = (0, FOLD, FOLD + STEPS, FOLD + 2 * STEPS)
    for (low, high), begin, end in zip(zip(*sides), starts, starts[1:]):
        first_ref[begin:end] = jnp.where(lat_odd, low, high)
        second_ref[begin:end] = jnp.where(lat_odd, high, low)


def halves(value):
    hi = value.astype(jnp.bfloat16)
    return hi, (value - hi.astype(jnp.float32)).astype(jnp.bfloat16)


class Update:
    def __init__(self, mix_ref, rate_ref):
        self.mixer, self.rate_ref = mix_ref[...], rate_ref
        self.levels = rate_ref.shape[1]
        self.pad = jnp.zeros((self.mixer.shape[1] - 3 * self.levels, 256), jnp.bfloat16)
        tail = lax.broadcasted_iota(jnp.int32, (8, 128), 0)
        self.first = tail == 0
        self.tail = (tail + (self.levels - 8)).astype(jnp.float32)

    def moved(self, x, neighbours, flux, deep):
        value = self.rate_ref[1] * x + self.rate_ref[0] * neighbours
        head = value[:8] + jnp.where(self.first, flux, 0.0)
        tail = jnp.where(self.tail < deep, value[-8:], 0.0)
        return jnp.concatenate([head, value[8:-8], tail], axis=0)

    def mixed(self, values):
        value = jnp.concatenate(values, axis=1)
        hi, lo = halves(value)
        full = jnp.concatenate([hi, lo, hi, self.pad[:, : value.shape[1]]], axis=0)
        out = jnp.dot(self.mixer, full, preferred_element_type=jnp.float32)
        return [out[:, 128 * k : 128 * (k + 1)] for k in range(len(values))]

    def settled(self, new, x, deep):
        sea = jnp.broadcast_to(deep, (self.levels - 8, 128)) > 0.0
        body = jnp.where(sea, new[:-8], x[:-8])
        tail = jnp.where(self.tail < deep, new[-8:], x[-8:])
        return jnp.concatenate([body, tail], axis=0)

    def rows(self, tiles, flux, deep):
        values = [
            self.moved(x, above + below + roll(x, 1) + roll(x, -1), f, d)
            for (above, x, below), f, d in zip(tiles, flux, deep)
        ]
        return [self.settled(new, t[1], d) for new, t, d in zip(self.mixed(values), tiles, deep)]


def lat_place():
    lat = lax.axis_index("lat")
    return lax.rem(lat, 2) == 1, (lat > 0) & (lat < lax.axis_size("lat") - 1)


def inner_kernel(
    state_ref, own_ref, rows1_ref, rows2_ref, mixing_ref, diffuse_ref, mix_ref, rate_ref, x_ref, side_ref, *inner_refs
):
    levels, rows, cells = state_ref.shape[1:]
    slots = rows + 2 * STEPS
    odd, inside = lat_place()
    first_at = jnp.where(odd, 0, rows + STEPS)
    for k in range(STEPS):
        x_ref[first_at + k] = rows1_ref[k]
        x_ref[rows + STEPS - first_at + k] = jnp.where(inside, rows2_ref[k], 0.0)
    x_ref[STEPS : STEPS + rows] = jnp.swapaxes(state_ref[0], 0, 1)
    write_operators(mixing_ref, diffuse_ref, mix_ref, rate_ref)
    update = Update(mix_ref, rate_ref)
    flux = [own_ref[levels + r : levels + r + 1] for r in range(rows)]
    deep = [own_ref[levels + rows + r : levels + rows + r + 1] for r in range(rows)]
    source, first = x_ref, 0
    for step in range(STEPS):
        target, at = inner_refs[step], STEPS + step
        for slot in range(at, slots - at, 2):
            pair = (slot, slot + 1)
            tiles = [[source[s - first + k] for k in (-1, 0, 1)] for s in pair]
            new = update.rows(tiles, [flux[s - STEPS] for s in pair], [deep[s - STEPS] for s in pair])
            for s, tile in zip(pair, new):
                target[s - at] = tile
        source, first = target, at
    lane = lane_ids((levels, 128))
    left = right = jnp.zeros((levels, 128), jnp.float32)
    for slot in range(slots):
        start = slot * EDGE
        turned = roll(x_ref[slot], start)
        right = jnp.where(lane // EDGE == slot, turned, right)
        left = jnp.where(lane // EDGE == (slot - 1) % slots, turned, left)
    side_ref[0] = roll(left, EDGE)
    side_ref[1] = right


def outer_kernel(own_ref, msg2_ref, msg1_ref, mix_ref, rate_ref, x_ref, side_ref, *refs):
    inner_refs, out_ref, outer_refs = refs[:STEPS], refs[STEPS], refs[STEPS + 1 :]
    levels, rows, cells = out_ref.shape[1:]
    slots = rows + 2 * STEPS
    odd, inside = lat_place()
    one, two = msg1_ref[...], jnp.where(inside, msg2_ref[...], 0.0)
    top, bottom = jnp.where(odd, one, two), jnp.where(odd, two, one)

    def per_slot(at, own_at, slot):
        if slot < STEPS:
            return top[at + slot : at + slot + 1]
        if slot < STEPS + rows:
            return own_ref[own_at + slot - STEPS : own_at + slot - STEPS + 1]
        return bottom[at + slot - STEPS - rows : at + slot - STEPS - rows + 1]

    flux_rows = [per_slot(FOLD, levels, s) for s in range(slots)]
    deep_rows = [per_slot(FOLD + STEPS, levels + rows, s) for s in range(slots)]
    lane1 = lane_ids((1, 128))
    lane = lane_ids((levels, 128))
    place = lane % EDGE
    width = STEPS * EDGE

    def around(upper, own, lower, group):
        at = lane_ids(own.shape)
        upper, lower = roll(upper, -group * width), roll(lower, 128 - width - group * width)
        return jnp.where(at < width, upper, jnp.where(at < 128 - width, own, lower))

    pieces = []
    for start in range(0, levels, FOLD):
        size = min(FOLD, levels - start)
        pieces.append(around(top[:size], own_ref[start : start + size], bottom[:size], start // FOLD))
    mid = jnp.concatenate(pieces, axis=0)
    beside = levels % FOLD
    at = levels + 2 * rows
    flux_mid, deep_mid = (
        around(
            top[beside + k : beside + k + 1],
            own_ref[at + k : at + k + 1],
            bottom[beside + k : beside + k + 1],
            levels // FOLD,
        )
        for k in range(2)
    )
    left, right = side_ref[0], side_ref[1]
    flux_left = flux_right = deep_side = jnp.zeros((1, 128), jnp.float32)
    for slot in range(slots):
        start = slot * EDGE
        mine1 = (lane1 >= start) & (lane1 < start + EDGE)
        flux_left = jnp.where(mine1, roll(flux_rows[slot], start + EDGE), flux_left)
        flux_right = jnp.where(mine1, roll(flux_rows[slot], start), flux_right)
        deep_side = jnp.where(mine1, deep_rows[slot], deep_side)

    def strip(tile, west, east):
        above_below = roll(tile, EDGE) + roll(tile, -EDGE)
        to_west, to_east = roll(tile, 1), roll(tile, -1)
        if west is not None:
            to_west = jnp.where(place == 0, roll(west, 1 - EDGE), to_west)
        if east is not None:
            to_east = jnp.where(place == EDGE - 1, roll(east, EDGE - 1), to_east)
        return above_below + to_west + to_east

    update = Update(mix_ref, rate_ref)

    def tile_at(step, s):
        if step == 0:
            return x_ref[s]
        if 3 + step <= s <= slots - 4 - step:
            return inner_refs[step - 1][s - 3 - step]
        return outer_refs[step - 1][s - step if s < slots // 2 else s - (slots - 6 - step)]

    done = [None] * rows

    def put(s, tile):
        tile = jnp.where((lane < 4) | (lane >= cells - 4), roll(sides, -s * EDGE), tile)
        done[s - STEPS] = tile

    for step in range(STEPS):
        last = step == STEPS - 1
        z_left = update.moved(left, strip(left, None, mid), flux_left, deep_side)
        z_right = update.moved(right, strip(right, mid, None), flux_right, deep_side)
        new_left, new_right = update.mixed([z_left, z_right])
        if not last:
            z_mid = update.moved(mid, strip(mid, left, right), flux_mid, deep_mid)
            mid = update.settled(update.mixed([z_mid])[0], mid, deep_mid)
        left = update.settled(new_left, left, deep_side)
        right = update.settled(new_right, right, deep_side)
        if last:
            sides = jnp.where(place < 4, right, roll(left, -EDGE))
        low_rows = list(range(step + 1, step + 4))
        todo = low_rows + [slots - 1 - s for s in reversed(low_rows)]
        for k in range(0, len(todo), 2):
            pair = todo[k : k + 2]
            tiles = [[tile_at(step, s + j) for j in (-1, 0, 1)] for s in pair]
            new = update.rows(tiles, [flux_rows[s] for s in pair], [deep_rows[s] for s in pair])
            for j, (s, tile) in enumerate(zip(pair, new)):
                if last:
                    put(s, tile)
                else:
                    outer_refs[step][k + j] = tile
    for s in (slots // 2 - 1, slots // 2):
        put(s, inner_refs[STEPS - 1][s - slots // 2 + 1])
    out_ref[0] = jnp.swapaxes(jnp.stack(done, axis=0), 0, 1)


def kernel_call(body, out_shape, blocks, scratch=(), flops=0, nbytes=0, vmem=VMEM_LIMIT, grid=()):
    return pl.pallas_call(
        body,
        out_shape=out_shape,
        grid=grid,
        in_specs=blocks,
        out_specs=jax.tree.map(lambda _: vmem_spec(), out_shape),
        scratch_shapes=scratch,
        compiler_params=pltpu.CompilerParams(vmem_limit_bytes=vmem),
        cost_estimate=pl.CostEstimate(flops=flops, bytes_accessed=nbytes, transcendentals=0),
    )


def f32(*shape):
    return jax.ShapeDtypeStruct(shape, jnp.float32)


def exchange(value, axis, partner):
    size = lax.axis_size(axis)
    pairs = [(i, partner(i)) for i in range(size) if 0 <= partner(i) < size]
    return lax.ppermute(value, axis, pairs)


def exchange_over(value, axis, partner):
    size, sections = lax.axis_size(axis), lax.axis_size("comp")
    pairs = [
        (section * size + i, (sections - 1 - section) * size + partner(i))
        for section in range(sections)
        for i in range(size)
    ]
    return lax.ppermute(value, ("comp", axis), pairs)


def on_device(state, mixing, diffusivity, weights, links, land, depth):
    levels, rows, cells = state.shape[1:]
    count = links.shape[-1]
    pack_rows = count + 8
    lat_count, lon_count = lax.axis_size("lat"), lax.axis_size("lon")

    def near(i):
        return i ^ 1

    def far_round(i):
        return (i - 1 if i % 2 == 0 else i + 1) % lon_count

    def far_lat(i):
        return (i - 1 if i % 2 == 0 else i + 1) % lat_count

    zeros = kernel_call(
        zero_kernel, f32(8, 128), [], flops=2_000_000_000, nbytes=4096, vmem=FRONT_VMEM_LIMIT
    )()
    pack = kernel_call(
        pack_kernel,
        f32(pack_rows + rows, 128),
        [vmem_spec()] * 6,
        flops=2_000_000_000,
        nbytes=700_000,
        vmem=FRONT_VMEM_LIMIT,
    )(state, weights, links, land.reshape(1, rows), depth.reshape(1, rows), zeros)
    state, pack = lax.optimization_barrier((state, pack))
    crossed = exchange(pack, "comp", near)
    edge_near, edge_far, up_down_1, up_down_2 = kernel_call(
        edge_kernel,
        (f32(FOLD, 128),) * 2 + (f32(STEPS, levels, 128),) * 2,
        [vmem_spec()],
        flops=2_000_000_000,
        nbytes=900_000,
        vmem=FRONT_VMEM_LIMIT,
    )(state)
    spare = kernel_call(
        zero_kernel, f32(16, 128), [], flops=2_000_000_000, nbytes=4096, vmem=FRONT_VMEM_LIMIT
    )()
    spare, edge_near = lax.optimization_barrier((spare, edge_near))
    beside_1 = exchange_over(jnp.concatenate([edge_near, crossed[:pack_rows]], axis=0), "lon", near)
    beside_2 = exchange_over(jnp.concatenate([edge_far, crossed[:pack_rows]], axis=0), "lon", far_round)
    if lon_count == 4:
        across = exchange_over(crossed[:pack_rows], "lon", lambda i: i ^ 2)
        packs = [pack, beside_1, across, beside_2]
        slices = [(0, 0), (1, FOLD), (2, 0), (3, FOLD)]
        east_west = ((1, 0), (3, 0))
    else:
        packs = [pack, beside_1, beside_2, lax.all_gather(pack[:pack_rows], "lon", axis=0, tiled=True)]
        slices = [(3, k * pack_rows) for k in range(lon_count)]
        east_west = ((1, 0), (2, 0))
    rows_1 = exchange(up_down_1, "lat", near)
    rows_2 = exchange(up_down_2, "lat", far_lat)
    rows_1, packs[0] = lax.optimization_barrier((rows_1, packs[0]))
    own, for_first, for_second = kernel_call(
        functools.partial(flux_kernel, count, slices, east_west),
        (f32(levels + 2 * rows + 8, 128),) + (f32(FOLD + 2 * STEPS, 128),) * 2,
        [vmem_spec()] * (2 + len(packs)),
        flops=3_000_000_000,
        nbytes=100_000,
        vmem=FRONT_VMEM_LIMIT,
    )(crossed, spare, *packs)
    own = exchange(own, "comp", near)
    message_2 = exchange_over(for_second, "lat", far_lat)
    message_1 = exchange_over(for_first, "lat", near)
    laid_out = kernel_call(
        inner_kernel,
        (
            jax.ShapeDtypeStruct((levels, 256), jnp.bfloat16),
            f32(2, levels, 128),
            f32(rows + 2 * STEPS, levels, 128),
            f32(2, levels, 128),
        )
        + tuple(f32(rows - 2 * k, levels, 128) for k in range(STEPS)),
        [vmem_spec()] * 6,
        flops=2_000_000_000,
        nbytes=2_000_000,
    )(state, own, rows_1, rows_2, mixing, diffusivity)
    return kernel_call(
        outer_kernel,
        f32(*state.shape),
        [vmem_spec()] * (3 + len(laid_out)),
        scratch=[pltpu.VMEM((6, levels, 128), jnp.float32)] * (STEPS - 1),
        flops=300_000_000,
        nbytes=2_000_000,
    )(own, message_2, message_1, *laid_out)


def solution(mesh):
    in_specs = (
        P("comp", None, "lat", "lon"),
        P("comp", None, None),
        P("comp", None),
        P("comp", None),
        P("comp", "lat", "lon", None, None),
        P("lat", "lon"),
        P("lat", "lon"),
    )
    out_specs = P("comp", None, "lat", "lon")
    return jax.shard_map(
        on_device, mesh=mesh, in_specs=in_specs, out_specs=out_specs, check_vma=False
    )
```

```python
import functools

import jax
import jax.numpy as jnp
from jax import lax
from jax.experimental import pallas as pl
from jax.experimental.pallas import tpu as pltpu
from jax.sharding import PartitionSpec as P

STEPS = 4
EDGE = 8
FOLD = 24
AXES = ("comp", "lat", "lon")
VMEM_LIMIT = 8 * 1024 * 1024
FRONT_VMEM_LIMIT = 4 * 1024 * 1024

coupling_rate = 0.5


def vmem_spec():
    return pl.BlockSpec(memory_space=pltpu.VMEM)


def lane_ids(shape):
    return lax.broadcasted_iota(jnp.int32, shape, len(shape) - 1)


def roll(value, shift):
    shift = shift % value.shape[-1]
    return value if shift == 0 else pltpu.roll(value, shift, 1)


def as_column(row):
    n = row.shape[1]
    diagonal = lax.broadcasted_iota(jnp.int32, (n, n), 0) == lane_ids((n, n))
    return jnp.sum(jnp.where(diagonal, row, 0.0), axis=1, keepdims=True)


def spread(column):
    rows = column.shape[0]
    shape = (rows, 128)
    mine = lane_ids(shape) // EDGE == lax.broadcasted_iota(jnp.int32, shape, 0)
    return jnp.sum(jnp.where(mine, column, 0.0), axis=0, keepdims=True)


def zero_kernel(out_ref):
    out_ref[...] = jnp.zeros_like(out_ref)


def pack_kernel(state_ref, weights_ref, links_ref, land_ref, depth_ref, zero_ref, out_ref):
    surface = state_ref[0, 0]
    rows = surface.shape[0]
    table = links_ref[0, 0, 0].astype(jnp.float32)
    count = table.shape[1]
    source = as_column(table[0:1])
    weight_id = as_column(table[3:4])
    entries = weights_ref.shape[1]
    weight = jnp.sum(
        jnp.where(weight_id == lane_ids((count, entries)).astype(jnp.float32), weights_ref[...], 0.0),
        axis=1,
        keepdims=True,
    )
    picked = jnp.zeros((count, surface.shape[1]), jnp.float32)
    for row in range(rows):
        picked = jnp.where(source == float(row), surface[row : row + 1], picked)
    out_ref[0:count] = weight * picked
    code = table[1:2] * float(rows) + table[2:3]
    diagonal = lax.broadcasted_iota(jnp.int32, (count, 128), 0) == lane_ids((count, 128))
    weight_row = jnp.sum(jnp.where(diagonal, weight, 0.0), axis=0, keepdims=True)
    code_row = jnp.sum(jnp.where(diagonal, as_column(code), 0.0), axis=0, keepdims=True)
    land = as_column(land_ref[...].astype(jnp.float32))
    deep = land * as_column(depth_ref[...].astype(jnp.float32))
    out_ref[count : count + 1] = code_row
    out_ref[count + 1 : count + 2] = weight_row
    out_ref[count + 2 : count + 3] = spread(land)
    out_ref[count + 3 : count + 4] = spread(deep)
    out_ref[count + 4 : count + 8] = zero_ref[0:4]
    out_ref[count + 8 :] = surface


def write_operators(mixing_ref, diffuse_ref, mix_ref, rate_ref):
    levels = mixing_ref.shape[1]
    mix = mixing_ref[0]
    top = mix.astype(jnp.bfloat16)
    rest = (mix - top.astype(jnp.float32)).astype(jnp.bfloat16)
    mix_ref[...] = jnp.zeros_like(mix_ref)
    mix_ref[:, 0:levels] = top
    mix_ref[:, levels : 2 * levels] = top
    mix_ref[:, 2 * levels : 3 * levels] = rest
    rate = jnp.broadcast_to(as_column(diffuse_ref[...]), (levels, 128))
    rate_ref[0] = rate
    rate_ref[1] = 1.0 - 4.0 * rate


def fold_shift(group):
    return group % 2 * 4 + group // 2 * 64


def edge_kernel(state_ref, near_ref, far_ref, first_ref, second_ref):
    levels, rows, cells = state_ref.shape[1:]
    lat_odd = lax.rem(lax.axis_index("lat"), 2) == 1
    lon_odd = lax.rem(lax.axis_index("lon"), 2) == 1
    lane = lane_ids((levels, 128))
    first = last = jnp.zeros((levels, 128), jnp.float32)
    tiles = jnp.swapaxes(state_ref[0], 0, 1)
    for row in range(rows):
        turned = roll(tiles[row], row * EDGE)
        first = jnp.where(lane // EDGE == row, turned, first)
        last = jnp.where(lane // EDGE == (row - 1) % (128 // EDGE), turned, last)
    last = roll(last, 4)
    near, far = jnp.where(lon_odd, first, last), jnp.where(lon_odd, last, first)
    for ref, cells_out in ((near_ref, near), (far_ref, far)):
        folded = jnp.zeros((FOLD, 128), jnp.float32)
        lane_fold = lane_ids((FOLD, 128))
        for group in range(-(-levels // FOLD)):
            part = cells_out[group * FOLD : min((group + 1) * FOLD, levels)]
            if part.shape[0] < FOLD:
                part = jnp.concatenate([part, jnp.zeros((FOLD - part.shape[0], 128), jnp.float32)], axis=0)
            mine = (lane_fold // 64 == group // 2) & (lane_fold % EDGE // 4 == group % 2)
            folded = jnp.where(mine, roll(part, fold_shift(group)), folded)
        ref[...] = folded
    for k in range(4):
        low, high = tiles[k], tiles[rows - 4 + k]
        first_ref[k] = jnp.where(lat_odd, low, high)
        second_ref[k] = jnp.where(lat_odd, high, low)


def flux_kernel(count, slices, east_west, *refs):
    crossed_ref, zero_ref, *packs, own_ref, first_ref, second_ref = refs
    surface = crossed_ref[count + 8 :]
    rows = surface.shape[0]
    levels = own_ref.shape[0] - 2 * rows - 8
    lon, lon_count = lax.axis_index("lon"), lax.axis_size("lon")
    odd = lax.rem(lon, 2) == 1
    ocean = lax.axis_index("comp") == 0
    here = lon * rows
    after = lax.rem(lon + 1, lon_count) * rows
    before = lax.rem(lon + lon_count - 1, lon_count) * rows
    index = lax.broadcasted_iota(jnp.int32, (3 * rows, count), 0)
    wanted = jnp.where(
        index < rows, here + index, jnp.where(index < 2 * rows, after + index - rows, before + index - 2 * rows)
    ).astype(jnp.float32)
    accum = jnp.zeros((3 * rows, 128), jnp.float32)
    totals = jnp.zeros((3 * rows, 1), jnp.float32)
    for which, offset in slices:
        ref = packs[which]
        hit = (wanted == ref[offset + count : offset + count + 1, 0:count]).astype(jnp.float32)
        accum += jnp.dot(
            hit,
            ref[offset : offset + count],
            precision=lax.Precision.HIGHEST,
            preferred_element_type=jnp.float32,
        )
        totals += jnp.sum(
            hit * ref[offset + count + 1 : offset + count + 2, 0:count], axis=1, keepdims=True
        )
    imported = accum / jnp.maximum(totals, 1.0)
    spread_rows = packs[0][count + 2 : count + 4]
    column = lax.broadcasted_iota(jnp.int32, (rows, 128), 0) * EDGE == lane_ids((rows, 128))
    land = jnp.sum(jnp.where(column, spread_rows[0:1], 0.0), axis=1, keepdims=True)
    deep = jnp.sum(jnp.where(column, spread_rows[1:2], 0.0), axis=1, keepdims=True)
    all_levels = float(levels)
    deep = jnp.where(ocean, deep, all_levels)
    (first, first_at), (second, second_at) = east_west
    lane = lane_ids((1, 128))
    from_east = lax.rem(lane, EDGE) < 4

    one = packs[first][first_at : first_at + FOLD + count + 4]
    two = packs[second][second_at : second_at + FOLD + count + 4]
    to_east, to_west = jnp.where(odd, two, one), jnp.where(odd, one, two)

    def beside(at):
        return jnp.where(from_east, to_east[at : at + 1], to_west[at : at + 1])

    pieces = []
    for start in range(0, levels, FOLD):
        size = min(FOLD, levels - start)
        shift = fold_shift(start // FOLD)
        pieces.append(
            jnp.where(
                lane_ids((size, 128)) % EDGE < 4, roll(to_east[:size], -shift), roll(to_west[:size], 4 - shift)
            )
        )
    whole = jnp.concatenate(pieces, axis=0)
    land_beside = beside(FOLD + count + 2)
    deep_beside = jnp.where(ocean, beside(FOLD + count + 3), all_levels)
    imported_beside = jnp.zeros((1, 128), jnp.float32)
    for row in range(rows):
        start = row * EDGE
        east = roll(imported[rows + row : rows + row + 1], start)
        west = roll(imported[2 * rows + row : 2 * rows + row + 1], start + 8)
        mine = (lane >= start) & (lane < start + EDGE)
        imported_beside = jnp.where(mine, jnp.where(from_east, east, west), imported_beside)
    flux_beside = coupling_rate * land_beside * (imported_beside - whole[0:1])
    flux = coupling_rate * land * (imported[0:rows] - surface)
    deep = jnp.broadcast_to(deep, (rows, 128))
    own_ref[0:levels] = roll(whole, STEPS * EDGE)
    own_ref[levels : levels + rows] = flux
    own_ref[levels + rows : levels + 2 * rows] = deep
    own_ref[levels + 2 * rows : levels + 2 * rows + 1] = roll(flux_beside, STEPS * EDGE)
    own_ref[levels + 2 * rows + 1 : levels + 2 * rows + 2] = roll(deep_beside, STEPS * EDGE)
    own_ref[levels + 2 * rows + 2 :] = zero_ref[0:6]
    width = STEPS * EDGE
    sides = []
    for at in (0, rows - STEPS):
        lane_at = at * EDGE
        folded = jnp.zeros((FOLD, 128), jnp.float32)
        lane_fold = lane_ids((FOLD, 128))
        for group in range(-(-levels // FOLD)):
            part = whole[group * FOLD : min((group + 1) * FOLD, levels)]
            if part.shape[0] < FOLD:
                extra = jnp.zeros((FOLD - part.shape[0], 128), jnp.float32)
                index = lax.broadcasted_iota(jnp.int32, extra.shape, 0)
                extra = jnp.where(index == 0, flux_beside, jnp.where(index == 1, deep_beside, extra))
                part = jnp.concatenate([part, extra], axis=0)
            folded = jnp.where(lane_fold // width == group, roll(part, group * width - lane_at), folded)
        sides.append((folded, flux[at : at + STEPS], deep[at : at + STEPS]))
    lat_odd = lax.rem(lax.axis_index("lat"), 2) == 1
    starts = (0, FOLD, FOLD + STEPS, FOLD + 2 * STEPS)
    for (low, high), begin, end in zip(zip(*sides), starts, starts[1:]):
        first_ref[begin:end] = jnp.where(lat_odd, low, high)
        second_ref[begin:end] = jnp.where(lat_odd, high, low)


def halves(value):
    hi = value.astype(jnp.bfloat16)
    return hi, (value - hi.astype(jnp.float32)).astype(jnp.bfloat16)


class Update:
    def __init__(self, mix_ref, rate_ref):
        self.mixer, self.rate_ref = mix_ref[...], rate_ref
        self.levels = rate_ref.shape[1]
        self.pad = jnp.zeros((self.mixer.shape[1] - 3 * self.levels, 128), jnp.bfloat16)
        tail = lax.broadcasted_iota(jnp.int32, (8, 128), 0)
        self.first = tail == 0
        self.tail = (tail + (self.levels - 8)).astype(jnp.float32)

    def moved(self, x, neighbours, flux, deep):
        value = self.rate_ref[1] * x + self.rate_ref[0] * neighbours
        head = value[:8] + jnp.where(self.first, flux, 0.0)
        tail = jnp.where(self.tail < deep, value[-8:], 0.0)
        return jnp.concatenate([head, value[8:-8], tail], axis=0)

    def mixed(self, values):
        out = []
        for value in values:
            hi, lo = halves(value)
            full = jnp.concatenate([hi, lo, hi, self.pad], axis=0)
            out.append(jnp.dot(self.mixer, full, preferred_element_type=jnp.float32))
        return out

    def settled(self, new, x, deep):
        sea = jnp.broadcast_to(deep, (self.levels - 8, 128)) > 0.0
        body = jnp.where(sea, new[:-8], x[:-8])
        tail = jnp.where(self.tail < deep, new[-8:], x[-8:])
        return jnp.concatenate([body, tail], axis=0)

    def rows(self, tiles, flux, deep):
        values = [
            self.moved(x, above + below + roll(x, 1) + roll(x, -1), f, d)
            for (above, x, below), f, d in zip(tiles, flux, deep)
        ]
        return [self.settled(new, t[1], d) for new, t, d in zip(self.mixed(values), tiles, deep)]


def lat_place():
    lat = lax.axis_index("lat")
    return lax.rem(lat, 2) == 1, (lat > 0) & (lat < lax.axis_size("lat") - 1)


def gather_sides(x_ref, slots, left, right):
    lane = lane_ids(left.shape)
    for slot in slots:
        turned = roll(x_ref[slot], slot * EDGE)
        right = jnp.where(lane // EDGE == slot, turned, right)
        left = jnp.where(lane // EDGE == (slot - 1) % (128 // EDGE), turned, left)
    return left, right


def layout_kernel(state_ref, rows1_ref, mixing_ref, diffuse_ref, mix_ref, rate_ref, x_ref, side_ref):
    levels, rows, cells = state_ref.shape[1:]
    write_operators(mixing_ref, diffuse_ref, mix_ref, rate_ref)
    odd, inside = lat_place()
    first_at = jnp.where(odd, 0, rows + STEPS)
    for k in range(STEPS):
        x_ref[first_at + k] = rows1_ref[k]
    x_ref[STEPS : STEPS + rows] = jnp.swapaxes(state_ref[0], 0, 1)
    none = jnp.zeros((levels, 128), jnp.float32)
    side_ref[0], side_ref[1] = gather_sides(x_ref, range(STEPS, STEPS + rows), none, none)


def inner_kernel(
    own_ref, rows2_ref, mix_ref, rate_ref, x_in_ref, side_in_ref, x_ref, side_ref, *inner_refs
):
    slots, levels, cells = x_ref.shape
    rows = slots - 2 * STEPS
    odd, inside = lat_place()
    second_at = jnp.where(odd, rows + STEPS, 0)
    for k in range(STEPS):
        x_ref[second_at + k] = jnp.where(inside, rows2_ref[k], 0.0)
    update = Update(mix_ref, rate_ref)
    flux = [own_ref[levels + r : levels + r + 1] for r in range(rows)]
    deep = [own_ref[levels + rows + r : levels + rows + r + 1] for r in range(rows)]
    source, first = x_ref, 0
    for step in range(STEPS):
        target, at = inner_refs[step], STEPS + step
        for slot in range(at, slots - at, 2):
            pair = (slot, slot + 1)
            tiles = [[source[s - first + k] for k in (-1, 0, 1)] for s in pair]
            new = update.rows(tiles, [flux[s - STEPS] for s in pair], [deep[s - STEPS] for s in pair])
            for s, tile in zip(pair, new):
                target[s - at] = tile
        source, first = target, at
    halo = [*range(STEPS), *range(STEPS + rows, slots)]
    left, right = gather_sides(x_ref, halo, side_in_ref[0], side_in_ref[1])
    side_ref[0] = roll(left, EDGE)
    side_ref[1] = right


def outer_kernel(own_ref, msg1_ref, msg2_ref, mix_ref, rate_ref, x_ref, side_ref, *refs):
    inner_refs, out_ref, outer_refs = refs[:STEPS], refs[STEPS], refs[STEPS + 1 :]
    levels, rows, cells = out_ref.shape[1:]
    slots = rows + 2 * STEPS
    odd, inside = lat_place()
    one, two = msg1_ref[...], jnp.where(inside, msg2_ref[...], 0.0)
    top, bottom = jnp.where(odd, one, two), jnp.where(odd, two, one)

    def per_slot(at, own_at, slot):
        if slot < STEPS:
            return top[at + slot : at + slot + 1]
        if slot < STEPS + rows:
            return own_ref[own_at + slot - STEPS : own_at + slot - STEPS + 1]
        return bottom[at + slot - STEPS - rows : at + slot - STEPS - rows + 1]

    flux_rows = [per_slot(FOLD, levels, s) for s in range(slots)]
    deep_rows = [per_slot(FOLD + STEPS, levels + rows, s) for s in range(slots)]
    lane1 = lane_ids((1, 128))
    lane = lane_ids((levels, 128))
    place = lane % EDGE
    width = STEPS * EDGE

    def around(upper, own, lower, group):
        at = lane_ids(own.shape)
        upper, lower = roll(upper, -group * width), roll(lower, 128 - width - group * width)
        return jnp.where(at < width, upper, jnp.where(at < 128 - width, own, lower))

    pieces = []
    for start in range(0, levels, FOLD):
        size = min(FOLD, levels - start)
        pieces.append(around(top[:size], own_ref[start : start + size], bottom[:size], start // FOLD))
    mid = jnp.concatenate(pieces, axis=0)
    beside = levels % FOLD
    at = levels + 2 * rows
    flux_mid, deep_mid = (
        around(
            top[beside + k : beside + k + 1],
            own_ref[at + k : at + k + 1],
            bottom[beside + k : beside + k + 1],
            levels // FOLD,
        )
        for k in range(2)
    )
    left, right = side_ref[0], side_ref[1]
    flux_left = flux_right = deep_side = jnp.zeros((1, 128), jnp.float32)
    for slot in range(slots):
        start = slot * EDGE
        mine1 = (lane1 >= start) & (lane1 < start + EDGE)
        flux_left = jnp.where(mine1, roll(flux_rows[slot], start + EDGE), flux_left)
        flux_right = jnp.where(mine1, roll(flux_rows[slot], start), flux_right)
        deep_side = jnp.where(mine1, deep_rows[slot], deep_side)

    def strip(tile, west, east):
        above_below = roll(tile, EDGE) + roll(tile, -EDGE)
        to_west, to_east = roll(tile, 1), roll(tile, -1)
        if west is not None:
            to_west = jnp.where(place == 0, roll(west, 1 - EDGE), to_west)
        if east is not None:
            to_east = jnp.where(place == EDGE - 1, roll(east, EDGE - 1), to_east)
        return above_below + to_west + to_east

    update = Update(mix_ref, rate_ref)

    def tile_at(step, s):
        if step == 0:
            return x_ref[s]
        if 3 + step <= s <= slots - 4 - step:
            return inner_refs[step - 1][s - 3 - step]
        return outer_refs[step - 1][s - step if s < slots // 2 else s - (slots - 6 - step)]

    done = [None] * rows

    def put(s, tile):
        tile = jnp.where((lane < 4) | (lane >= cells - 4), roll(sides, -s * EDGE), tile)
        done[s - STEPS] = tile

    for step in range(STEPS):
        last = step == STEPS - 1
        z_left = update.moved(left, strip(left, None, mid), flux_left, deep_side)
        z_right = update.moved(right, strip(right, mid, None), flux_right, deep_side)
        new_left, new_right = update.mixed([z_left, z_right])
        if not last:
            z_mid = update.moved(mid, strip(mid, left, right), flux_mid, deep_mid)
            mid = update.settled(update.mixed([z_mid])[0], mid, deep_mid)
        left = update.settled(new_left, left, deep_side)
        right = update.settled(new_right, right, deep_side)
        if last:
            sides = jnp.where(place < 4, right, roll(left, -EDGE))
        low_rows = list(range(step + 1, step + 4))
        todo = low_rows + [slots - 1 - s for s in reversed(low_rows)]
        for k in range(0, len(todo), 3):
            group = todo[k : k + 3]
            tiles = [[tile_at(step, s + j) for j in (-1, 0, 1)] for s in group]
            new = update.rows(tiles, [flux_rows[s] for s in group], [deep_rows[s] for s in group])
            for j, (s, tile) in enumerate(zip(group, new)):
                if last:
                    put(s, tile)
                else:
                    outer_refs[step][k + j] = tile
    for s in (slots // 2 - 1, slots // 2):
        put(s, inner_refs[STEPS - 1][s - slots // 2 + 1])
    out_ref[0] = jnp.swapaxes(jnp.stack(done, axis=0), 0, 1)


def kernel_call(body, out_shape, blocks, scratch=(), flops=0, nbytes=0, vmem=VMEM_LIMIT, grid=(), aliases=None):
    return pl.pallas_call(
        body,
        out_shape=out_shape,
        grid=grid,
        in_specs=blocks,
        out_specs=jax.tree.map(lambda _: vmem_spec(), out_shape),
        scratch_shapes=scratch,
        input_output_aliases=aliases or {},
        compiler_params=pltpu.CompilerParams(vmem_limit_bytes=vmem),
        cost_estimate=pl.CostEstimate(flops=flops, bytes_accessed=nbytes, transcendentals=0),
    )


def f32(*shape):
    return jax.ShapeDtypeStruct(shape, jnp.float32)


def exchange(value, axis, partner):
    size = lax.axis_size(axis)
    pairs = [(i, partner(i)) for i in range(size) if 0 <= partner(i) < size]
    return lax.ppermute(value, axis, pairs)


def exchange_over(value, axis, partner):
    size, sections = lax.axis_size(axis), lax.axis_size("comp")
    pairs = [
        (section * size + i, (sections - 1 - section) * size + partner(i))
        for section in range(sections)
        for i in range(size)
    ]
    return lax.ppermute(value, ("comp", axis), pairs)


def on_device(state, mixing, diffusivity, weights, links, land, depth):
    levels, rows, cells = state.shape[1:]
    count = links.shape[-1]
    pack_rows = count + 8
    lat_count, lon_count = lax.axis_size("lat"), lax.axis_size("lon")

    def near(i):
        return i ^ 1

    def far_round(i):
        return (i - 1 if i % 2 == 0 else i + 1) % lon_count

    def far_lat(i):
        return (i - 1 if i % 2 == 0 else i + 1) % lat_count

    zeros = kernel_call(
        zero_kernel, f32(8, 128), [], flops=2_000_000_000, nbytes=4096, vmem=FRONT_VMEM_LIMIT
    )()
    pack = kernel_call(
        pack_kernel,
        f32(pack_rows + rows, 128),
        [vmem_spec()] * 6,
        flops=2_000_000_000,
        nbytes=700_000,
        vmem=FRONT_VMEM_LIMIT,
    )(state, weights, links, land.reshape(1, rows), depth.reshape(1, rows), zeros)
    state, pack = lax.optimization_barrier((state, pack))
    crossed = exchange(pack, "comp", near)
    edge_near, edge_far, up_down_1, up_down_2 = kernel_call(
        edge_kernel,
        (f32(FOLD, 128),) * 2 + (f32(STEPS, levels, 128),) * 2,
        [vmem_spec()],
        flops=2_000_000_000,
        nbytes=900_000,
        vmem=FRONT_VMEM_LIMIT,
    )(state)
    spare = kernel_call(
        zero_kernel, f32(16, 128), [], flops=2_000_000_000, nbytes=4096, vmem=FRONT_VMEM_LIMIT
    )()
    spare, edge_near = lax.optimization_barrier((spare, edge_near))
    beside_1 = exchange_over(jnp.concatenate([edge_near, crossed[:pack_rows]], axis=0), "lon", near)
    beside_2 = exchange_over(jnp.concatenate([edge_far, crossed[:pack_rows]], axis=0), "lon", far_round)
    if lon_count == 4:
        across = exchange_over(crossed[:pack_rows], "lon", lambda i: i ^ 2)
        packs = [pack, beside_1, across, beside_2]
        slices = [(0, 0), (1, FOLD), (2, 0), (3, FOLD)]
        east_west = ((1, 0), (3, 0))
    else:
        packs = [pack, beside_1, beside_2, lax.all_gather(pack[:pack_rows], "lon", axis=0, tiled=True)]
        slices = [(3, k * pack_rows) for k in range(lon_count)]
        east_west = ((1, 0), (2, 0))
    rows_1 = exchange(up_down_1, "lat", near)
    rows_2 = exchange(up_down_2, "lat", far_lat)
    *operators, tiles, sides = kernel_call(
        layout_kernel,
        (
            jax.ShapeDtypeStruct((levels, 256), jnp.bfloat16),
            f32(2, levels, 128),
            f32(rows + 2 * STEPS, levels, 128),
            f32(2, levels, 128),
        ),
        [vmem_spec()] * 4,
        flops=100_000,
        nbytes=100_000,
    )(state, rows_1, mixing, diffusivity)
    tiles, packs[0] = lax.optimization_barrier((tiles, packs[0]))
    own, for_first, for_second = kernel_call(
        functools.partial(flux_kernel, count, slices, east_west),
        (f32(levels + 2 * rows + 8, 128),) + (f32(FOLD + 2 * STEPS, 128),) * 2,
        [vmem_spec()] * (2 + len(packs)),
        flops=3_000_000_000,
        nbytes=100_000,
        vmem=FRONT_VMEM_LIMIT,
    )(crossed, spare, *packs)
    own = exchange(own, "comp", near)
    message_1 = exchange_over(for_first, "lat", near)
    message_2 = exchange_over(for_second, "lat", far_lat)
    stepped = kernel_call(
        inner_kernel,
        (f32(rows + 2 * STEPS, levels, 128), f32(2, levels, 128))
        + tuple(f32(rows - 2 * k, levels, 128) for k in range(STEPS)),
        [vmem_spec()] * 6,
        flops=2_000_000_000,
        nbytes=2_000_000,
        aliases={4: 0},
    )(own, rows_2, *operators, tiles, sides)
    return kernel_call(
        outer_kernel,
        f32(*state.shape),
        [vmem_spec()] * (5 + len(stepped)),
        scratch=[pltpu.VMEM((6, levels, 128), jnp.float32)] * (STEPS - 1),
        flops=300_000_000,
        nbytes=2_000_000,
    )(own, message_1, message_2, *operators, *stepped)


def solution(mesh):
    in_specs = (
        P("comp", None, "lat", "lon"),
        P("comp", None, None),
        P("comp", None),
        P("comp", None),
        P("comp", "lat", "lon", None, None),
        P("lat", "lon"),
        P("lat", "lon"),
    )
    out_specs = P("comp", None, "lat", "lon")
    return jax.shard_map(
        on_device, mesh=mesh, in_specs=in_specs, out_specs=out_specs, check_vma=False
    )
```

```python
import functools

import jax
import jax.numpy as jnp
from jax import lax
from jax.experimental import pallas as pl
from jax.experimental.pallas import tpu as pltpu
from jax.sharding import PartitionSpec as P

STEPS = 4
EDGE = 8
FOLD = 24
AXES = ("comp", "lat", "lon")
VMEM_LIMIT = 8 * 1024 * 1024
FRONT_VMEM_LIMIT = 4 * 1024 * 1024

coupling_rate = 0.5


def vmem_spec():
    return pl.BlockSpec(memory_space=pltpu.VMEM)


def lane_ids(shape):
    return lax.broadcasted_iota(jnp.int32, shape, len(shape) - 1)


def roll(value, shift):
    shift = shift % value.shape[-1]
    return value if shift == 0 else pltpu.roll(value, shift, 1)


def as_column(row):
    n = row.shape[1]
    diagonal = lax.broadcasted_iota(jnp.int32, (n, n), 0) == lane_ids((n, n))
    return jnp.sum(jnp.where(diagonal, row, 0.0), axis=1, keepdims=True)


def spread(column):
    rows = column.shape[0]
    shape = (rows, 128)
    mine = lane_ids(shape) // EDGE == lax.broadcasted_iota(jnp.int32, shape, 0)
    return jnp.sum(jnp.where(mine, column, 0.0), axis=0, keepdims=True)


def zero_kernel(out_ref):
    out_ref[...] = jnp.zeros_like(out_ref)


def pack_kernel(state_ref, weights_ref, links_ref, land_ref, depth_ref, zero_ref, out_ref):
    surface = state_ref[0, 0]
    rows = surface.shape[0]
    table = links_ref[0, 0, 0].astype(jnp.float32)
    count = table.shape[1]
    source = as_column(table[0:1])
    weight_id = as_column(table[3:4])
    entries = weights_ref.shape[1]
    weight = jnp.sum(
        jnp.where(weight_id == lane_ids((count, entries)).astype(jnp.float32), weights_ref[...], 0.0),
        axis=1,
        keepdims=True,
    )
    picked = jnp.zeros((count, surface.shape[1]), jnp.float32)
    for row in range(rows):
        picked = jnp.where(source == float(row), surface[row : row + 1], picked)
    out_ref[0:count] = weight * picked
    code = table[1:2] * float(rows) + table[2:3]
    diagonal = lax.broadcasted_iota(jnp.int32, (count, 128), 0) == lane_ids((count, 128))
    weight_row = jnp.sum(jnp.where(diagonal, weight, 0.0), axis=0, keepdims=True)
    code_row = jnp.sum(jnp.where(diagonal, as_column(code), 0.0), axis=0, keepdims=True)
    land = as_column(land_ref[...].astype(jnp.float32))
    deep = land * as_column(depth_ref[...].astype(jnp.float32))
    out_ref[count : count + 1] = code_row
    out_ref[count + 1 : count + 2] = weight_row
    out_ref[count + 2 : count + 3] = spread(land)
    out_ref[count + 3 : count + 4] = spread(deep)
    out_ref[count + 4 : count + 8] = zero_ref[0:4]
    out_ref[count + 8 :] = surface


def write_operators(mixing_ref, diffuse_ref, mix_ref, rate_ref):
    levels = mixing_ref.shape[1]
    mix = mixing_ref[0]
    top = mix.astype(jnp.bfloat16)
    rest = (mix - top.astype(jnp.float32)).astype(jnp.bfloat16)
    mix_ref[...] = jnp.zeros_like(mix_ref)
    mix_ref[:, 0:levels] = top
    mix_ref[:, levels : 2 * levels] = top
    mix_ref[:, 2 * levels : 3 * levels] = rest
    rate = jnp.broadcast_to(as_column(diffuse_ref[...]), (levels, 128))
    rate_ref[0] = rate
    rate_ref[1] = 1.0 - 4.0 * rate


def fold_shift(group):
    return group % 2 * 4 + group // 2 * 64


def edge_kernel(state_ref, near_ref, far_ref, first_ref, second_ref):
    levels, rows, cells = state_ref.shape[1:]
    lat_odd = lax.rem(lax.axis_index("lat"), 2) == 1
    lon_odd = lax.rem(lax.axis_index("lon"), 2) == 1
    lane = lane_ids((levels, 128))
    first = last = jnp.zeros((levels, 128), jnp.float32)
    tiles = jnp.swapaxes(state_ref[0], 0, 1)
    for row in range(rows):
        turned = roll(tiles[row], row * EDGE)
        first = jnp.where(lane // EDGE == row, turned, first)
        last = jnp.where(lane // EDGE == (row - 1) % (128 // EDGE), turned, last)
    last = roll(last, 4)
    near, far = jnp.where(lon_odd, first, last), jnp.where(lon_odd, last, first)
    for ref, cells_out in ((near_ref, near), (far_ref, far)):
        folded = jnp.zeros((FOLD, 128), jnp.float32)
        lane_fold = lane_ids((FOLD, 128))
        for group in range(-(-levels // FOLD)):
            part = cells_out[group * FOLD : min((group + 1) * FOLD, levels)]
            if part.shape[0] < FOLD:
                part = jnp.concatenate([part, jnp.zeros((FOLD - part.shape[0], 128), jnp.float32)], axis=0)
            mine = (lane_fold // 64 == group // 2) & (lane_fold % EDGE // 4 == group % 2)
            folded = jnp.where(mine, roll(part, fold_shift(group)), folded)
        ref[...] = folded
    for k in range(4):
        low, high = tiles[k], tiles[rows - 4 + k]
        first_ref[k] = jnp.where(lat_odd, low, high)
        second_ref[k] = jnp.where(lat_odd, high, low)


def flux_kernel(count, slices, east_west, *refs):
    crossed_ref, zero_ref, *packs, own_ref, first_ref, second_ref = refs
    surface = crossed_ref[count + 8 :]
    rows = surface.shape[0]
    levels = own_ref.shape[0] - 2 * rows - 8
    lon, lon_count = lax.axis_index("lon"), lax.axis_size("lon")
    odd = lax.rem(lon, 2) == 1
    ocean = lax.axis_index("comp") == 0
    here = lon * rows
    after = lax.rem(lon + 1, lon_count) * rows
    before = lax.rem(lon + lon_count - 1, lon_count) * rows
    index = lax.broadcasted_iota(jnp.int32, (3 * rows, count), 0)
    wanted = jnp.where(
        index < rows, here + index, jnp.where(index < 2 * rows, after + index - rows, before + index - 2 * rows)
    ).astype(jnp.float32)
    accum = jnp.zeros((3 * rows, 128), jnp.float32)
    totals = jnp.zeros((3 * rows, 1), jnp.float32)
    for which, offset in slices:
        ref = packs[which]
        hit = (wanted == ref[offset + count : offset + count + 1, 0:count]).astype(jnp.float32)
        accum += jnp.dot(
            hit,
            ref[offset : offset + count],
            precision=lax.Precision.HIGHEST,
            preferred_element_type=jnp.float32,
        )
        totals += jnp.sum(
            hit * ref[offset + count + 1 : offset + count + 2, 0:count], axis=1, keepdims=True
        )
    imported = accum / jnp.maximum(totals, 1.0)
    spread_rows = packs[0][count + 2 : count + 4]
    column = lax.broadcasted_iota(jnp.int32, (rows, 128), 0) * EDGE == lane_ids((rows, 128))
    land = jnp.sum(jnp.where(column, spread_rows[0:1], 0.0), axis=1, keepdims=True)
    deep = jnp.sum(jnp.where(column, spread_rows[1:2], 0.0), axis=1, keepdims=True)
    all_levels = float(levels)
    deep = jnp.where(ocean, deep, all_levels)
    (first, first_at), (second, second_at) = east_west
    lane = lane_ids((1, 128))
    from_east = lax.rem(lane, EDGE) < 4

    one = packs[first][first_at : first_at + FOLD + count + 4]
    two = packs[second][second_at : second_at + FOLD + count + 4]
    to_east, to_west = jnp.where(odd, two, one), jnp.where(odd, one, two)

    def beside(at):
        return jnp.where(from_east, to_east[at : at + 1], to_west[at : at + 1])

    pieces = []
    for start in range(0, levels, FOLD):
        size = min(FOLD, levels - start)
        shift = fold_shift(start // FOLD)
        pieces.append(
            jnp.where(
                lane_ids((size, 128)) % EDGE < 4, roll(to_east[:size], -shift), roll(to_west[:size], 4 - shift)
            )
        )
    whole = jnp.concatenate(pieces, axis=0)
    land_beside = beside(FOLD + count + 2)
    deep_beside = jnp.where(ocean, beside(FOLD + count + 3), all_levels)
    imported_beside = jnp.zeros((1, 128), jnp.float32)
    for row in range(rows):
        start = row * EDGE
        east = roll(imported[rows + row : rows + row + 1], start)
        west = roll(imported[2 * rows + row : 2 * rows + row + 1], start + 8)
        mine = (lane >= start) & (lane < start + EDGE)
        imported_beside = jnp.where(mine, jnp.where(from_east, east, west), imported_beside)
    flux_beside = coupling_rate * land_beside * (imported_beside - whole[0:1])
    flux = coupling_rate * land * (imported[0:rows] - surface)
    deep = jnp.broadcast_to(deep, (rows, 128))
    own_ref[0:levels] = roll(whole, STEPS * EDGE)
    own_ref[levels : levels + rows] = flux
    own_ref[levels + rows : levels + 2 * rows] = deep
    own_ref[levels + 2 * rows : levels + 2 * rows + 1] = roll(flux_beside, STEPS * EDGE)
    own_ref[levels + 2 * rows + 1 : levels + 2 * rows + 2] = roll(deep_beside, STEPS * EDGE)
    own_ref[levels + 2 * rows + 2 :] = zero_ref[0:6]
    width = STEPS * EDGE
    sides = []
    for at in (0, rows - STEPS):
        lane_at = at * EDGE
        folded = jnp.zeros((FOLD, 128), jnp.float32)
        lane_fold = lane_ids((FOLD, 128))
        for group in range(-(-levels // FOLD)):
            part = whole[group * FOLD : min((group + 1) * FOLD, levels)]
            if part.shape[0] < FOLD:
                extra = jnp.zeros((FOLD - part.shape[0], 128), jnp.float32)
                index = lax.broadcasted_iota(jnp.int32, extra.shape, 0)
                extra = jnp.where(index == 0, flux_beside, jnp.where(index == 1, deep_beside, extra))
                part = jnp.concatenate([part, extra], axis=0)
            folded = jnp.where(lane_fold // width == group, roll(part, group * width - lane_at), folded)
        sides.append((folded, flux[at : at + STEPS], deep[at : at + STEPS]))
    lat_odd = lax.rem(lax.axis_index("lat"), 2) == 1
    starts = (0, FOLD, FOLD + STEPS, FOLD + 2 * STEPS)
    for (low, high), begin, end in zip(zip(*sides), starts, starts[1:]):
        first_ref[begin:end] = jnp.where(lat_odd, low, high)
        second_ref[begin:end] = jnp.where(lat_odd, high, low)


def halves(value):
    hi = value.astype(jnp.bfloat16)
    return hi, (value - hi.astype(jnp.float32)).astype(jnp.bfloat16)


class Update:
    def __init__(self, mix_ref, rate_ref):
        self.mixer, self.rate_ref = mix_ref[...], rate_ref
        self.levels = rate_ref.shape[1]
        self.pad = jnp.zeros((self.mixer.shape[1] - 3 * self.levels, 128), jnp.bfloat16)
        tail = lax.broadcasted_iota(jnp.int32, (8, 128), 0)
        self.first = tail == 0
        self.tail = (tail + (self.levels - 8)).astype(jnp.float32)

    def moved(self, x, neighbours, flux, deep):
        value = self.rate_ref[1] * x + self.rate_ref[0] * neighbours
        head = value[:8] + jnp.where(self.first, flux, 0.0)
        tail = jnp.where(self.tail < deep, value[-8:], 0.0)
        return jnp.concatenate([head, value[8:-8], tail], axis=0)

    def mixed(self, values):
        out = []
        for value in values:
            hi, lo = halves(value)
            full = jnp.concatenate([hi, lo, hi, self.pad], axis=0)
            out.append(jnp.dot(self.mixer, full, preferred_element_type=jnp.float32))
        return out

    def settled(self, new, x, deep):
        sea = jnp.broadcast_to(deep, (self.levels - 8, 128)) > 0.0
        body = jnp.where(sea, new[:-8], x[:-8])
        tail = jnp.where(self.tail < deep, new[-8:], x[-8:])
        return jnp.concatenate([body, tail], axis=0)

    def rows(self, tiles, flux, deep):
        values = [
            self.moved(x, above + below + roll(x, 1) + roll(x, -1), f, d)
            for (above, x, below), f, d in zip(tiles, flux, deep)
        ]
        return [self.settled(new, t[1], d) for new, t, d in zip(self.mixed(values), tiles, deep)]


def lat_place():
    lat = lax.axis_index("lat")
    return lax.rem(lat, 2) == 1, (lat > 0) & (lat < lax.axis_size("lat") - 1)


def inner_kernel(
    state_ref, own_ref, rows1_ref, rows2_ref, mixing_ref, diffuse_ref, mix_ref, rate_ref, x_ref, side_ref, *inner_refs
):
    levels, rows, cells = state_ref.shape[1:]
    slots = rows + 2 * STEPS
    odd, inside = lat_place()
    first_at = jnp.where(odd, 0, rows + STEPS)
    for k in range(STEPS):
        x_ref[first_at + k] = rows1_ref[k]
        x_ref[rows + STEPS - first_at + k] = jnp.where(inside, rows2_ref[k], 0.0)
    x_ref[STEPS : STEPS + rows] = jnp.swapaxes(state_ref[0], 0, 1)
    write_operators(mixing_ref, diffuse_ref, mix_ref, rate_ref)
    update = Update(mix_ref, rate_ref)
    flux = [own_ref[levels + r : levels + r + 1] for r in range(rows)]
    deep = [own_ref[levels + rows + r : levels + rows + r + 1] for r in range(rows)]
    source, first = x_ref, 0
    for step in range(STEPS):
        target, at = inner_refs[step], STEPS + step
        for slot in range(at, slots - at, 2):
            pair = (slot, slot + 1)
            tiles = [[source[s - first + k] for k in (-1, 0, 1)] for s in pair]
            new = update.rows(tiles, [flux[s - STEPS] for s in pair], [deep[s - STEPS] for s in pair])
            for s, tile in zip(pair, new):
                target[s - at] = tile
        source, first = target, at
    lane = lane_ids((levels, 128))
    left = right = jnp.zeros((levels, 128), jnp.float32)
    for slot in range(slots):
        start = slot * EDGE
        turned = roll(x_ref[slot], start)
        right = jnp.where(lane // EDGE == slot, turned, right)
        left = jnp.where(lane // EDGE == (slot - 1) % slots, turned, left)
    side_ref[0] = roll(left, EDGE)
    side_ref[1] = right


def outer_kernel(own_ref, msg1_ref, msg2_ref, mix_ref, rate_ref, x_ref, side_ref, *refs):
    inner_refs, out_ref, outer_refs = refs[:STEPS], refs[STEPS], refs[STEPS + 1 :]
    levels, rows, cells = out_ref.shape[1:]
    slots = rows + 2 * STEPS
    odd, inside = lat_place()
    one, two = msg1_ref[...], jnp.where(inside, msg2_ref[...], 0.0)
    top, bottom = jnp.where(odd, one, two), jnp.where(odd, two, one)

    def per_slot(at, own_at, slot):
        if slot < STEPS:
            return top[at + slot : at + slot + 1]
        if slot < STEPS + rows:
            return own_ref[own_at + slot - STEPS : own_at + slot - STEPS + 1]
        return bottom[at + slot - STEPS - rows : at + slot - STEPS - rows + 1]

    flux_rows = [per_slot(FOLD, levels, s) for s in range(slots)]
    deep_rows = [per_slot(FOLD + STEPS, levels + rows, s) for s in range(slots)]
    lane1 = lane_ids((1, 128))
    lane = lane_ids((levels, 128))
    place = lane % EDGE
    width = STEPS * EDGE

    def around(upper, own, lower, group):
        at = lane_ids(own.shape)
        upper, lower = roll(upper, -group * width), roll(lower, 128 - width - group * width)
        return jnp.where(at < width, upper, jnp.where(at < 128 - width, own, lower))

    pieces = []
    for start in range(0, levels, FOLD):
        size = min(FOLD, levels - start)
        pieces.append(around(top[:size], own_ref[start : start + size], bottom[:size], start // FOLD))
    mid = jnp.concatenate(pieces, axis=0)
    beside = levels % FOLD
    at = levels + 2 * rows
    flux_mid, deep_mid = (
        around(
            top[beside + k : beside + k + 1],
            own_ref[at + k : at + k + 1],
            bottom[beside + k : beside + k + 1],
            levels // FOLD,
        )
        for k in range(2)
    )
    left, right = side_ref[0], side_ref[1]
    flux_left = flux_right = deep_side = jnp.zeros((1, 128), jnp.float32)
    for slot in range(slots):
        start = slot * EDGE
        mine1 = (lane1 >= start) & (lane1 < start + EDGE)
        flux_left = jnp.where(mine1, roll(flux_rows[slot], start + EDGE), flux_left)
        flux_right = jnp.where(mine1, roll(flux_rows[slot], start), flux_right)
        deep_side = jnp.where(mine1, deep_rows[slot], deep_side)

    def strip(tile, west, east):
        above_below = roll(tile, EDGE) + roll(tile, -EDGE)
        to_west, to_east = roll(tile, 1), roll(tile, -1)
        if west is not None:
            to_west = jnp.where(place == 0, roll(west, 1 - EDGE), to_west)
        if east is not None:
            to_east = jnp.where(place == EDGE - 1, roll(east, EDGE - 1), to_east)
        return above_below + to_west + to_east

    update = Update(mix_ref, rate_ref)

    def tile_at(step, s):
        if step == 0:
            return x_ref[s]
        if 3 + step <= s <= slots - 4 - step:
            return inner_refs[step - 1][s - 3 - step]
        return outer_refs[step - 1][s - step if s < slots // 2 else s - (slots - 6 - step)]

    done = [None] * rows

    def put(s, tile):
        tile = jnp.where((lane < 4) | (lane >= cells - 4), roll(sides, -s * EDGE), tile)
        done[s - STEPS] = tile

    for step in range(STEPS):
        last = step == STEPS - 1
        z_left = update.moved(left, strip(left, None, mid), flux_left, deep_side)
        z_right = update.moved(right, strip(right, mid, None), flux_right, deep_side)
        new_left, new_right = update.mixed([z_left, z_right])
        if not last:
            z_mid = update.moved(mid, strip(mid, left, right), flux_mid, deep_mid)
            mid = update.settled(update.mixed([z_mid])[0], mid, deep_mid)
        left = update.settled(new_left, left, deep_side)
        right = update.settled(new_right, right, deep_side)
        if last:
            sides = jnp.where(place < 4, right, roll(left, -EDGE))
        low_rows = list(range(step + 1, step + 4))
        todo = low_rows + [slots - 1 - s for s in reversed(low_rows)]
        for k in range(0, len(todo), 3):
            group = todo[k : k + 3]
            tiles = [[tile_at(step, s + j) for j in (-1, 0, 1)] for s in group]
            new = update.rows(tiles, [flux_rows[s] for s in group], [deep_rows[s] for s in group])
            for j, (s, tile) in enumerate(zip(group, new)):
                if last:
                    put(s, tile)
                else:
                    outer_refs[step][k + j] = tile
    for s in (slots // 2 - 1, slots // 2):
        put(s, inner_refs[STEPS - 1][s - slots // 2 + 1])
    out_ref[0] = jnp.swapaxes(jnp.stack(done, axis=0), 0, 1)


def kernel_call(body, out_shape, blocks, scratch=(), flops=0, nbytes=0, vmem=VMEM_LIMIT, grid=()):
    return pl.pallas_call(
        body,
        out_shape=out_shape,
        grid=grid,
        in_specs=blocks,
        out_specs=jax.tree.map(lambda _: vmem_spec(), out_shape),
        scratch_shapes=scratch,
        compiler_params=pltpu.CompilerParams(vmem_limit_bytes=vmem),
        cost_estimate=pl.CostEstimate(flops=flops, bytes_accessed=nbytes, transcendentals=0),
    )


def f32(*shape):
    return jax.ShapeDtypeStruct(shape, jnp.float32)


def exchange(value, axis, partner):
    size = lax.axis_size(axis)
    pairs = [(i, partner(i)) for i in range(size) if 0 <= partner(i) < size]
    return lax.ppermute(value, axis, pairs)


def exchange_over(value, axis, partner):
    size, sections = lax.axis_size(axis), lax.axis_size("comp")
    pairs = [
        (section * size + i, (sections - 1 - section) * size + partner(i))
        for section in range(sections)
        for i in range(size)
    ]
    return lax.ppermute(value, ("comp", axis), pairs)


def on_device(state, mixing, diffusivity, weights, links, land, depth):
    levels, rows, cells = state.shape[1:]
    count = links.shape[-1]
    pack_rows = count + 8
    lat_count, lon_count = lax.axis_size("lat"), lax.axis_size("lon")

    def near(i):
        return i ^ 1

    def far_round(i):
        return (i - 1 if i % 2 == 0 else i + 1) % lon_count

    def far_lat(i):
        return (i - 1 if i % 2 == 0 else i + 1) % lat_count

    zeros = kernel_call(
        zero_kernel, f32(8, 128), [], flops=2_000_000_000, nbytes=4096, vmem=FRONT_VMEM_LIMIT
    )()
    pack = kernel_call(
        pack_kernel,
        f32(pack_rows + rows, 128),
        [vmem_spec()] * 6,
        flops=2_000_000_000,
        nbytes=700_000,
        vmem=FRONT_VMEM_LIMIT,
    )(state, weights, links, land.reshape(1, rows), depth.reshape(1, rows), zeros)
    state, pack = lax.optimization_barrier((state, pack))
    crossed = exchange(pack, "comp", near)
    edge_near, edge_far, up_down_1, up_down_2 = kernel_call(
        edge_kernel,
        (f32(FOLD, 128),) * 2 + (f32(STEPS, levels, 128),) * 2,
        [vmem_spec()],
        flops=2_000_000_000,
        nbytes=900_000,
        vmem=FRONT_VMEM_LIMIT,
    )(state)
    spare = kernel_call(
        zero_kernel, f32(16, 128), [], flops=2_000_000_000, nbytes=4096, vmem=FRONT_VMEM_LIMIT
    )()
    spare, edge_near = lax.optimization_barrier((spare, edge_near))
    beside_1 = exchange_over(jnp.concatenate([edge_near, crossed[:pack_rows]], axis=0), "lon", near)
    beside_2 = exchange_over(jnp.concatenate([edge_far, crossed[:pack_rows]], axis=0), "lon", far_round)
    if lon_count == 4:
        across = exchange_over(crossed[:pack_rows], "lon", lambda i: i ^ 2)
        packs = [pack, beside_1, across, beside_2]
        slices = [(0, 0), (1, FOLD), (2, 0), (3, FOLD)]
        east_west = ((1, 0), (3, 0))
    else:
        packs = [pack, beside_1, beside_2, lax.all_gather(pack[:pack_rows], "lon", axis=0, tiled=True)]
        slices = [(3, k * pack_rows) for k in range(lon_count)]
        east_west = ((1, 0), (2, 0))
    rows_1 = exchange(up_down_1, "lat", near)
    rows_2 = exchange(up_down_2, "lat", far_lat)
    rows_1, packs[0] = lax.optimization_barrier((rows_1, packs[0]))
    own, for_first, for_second = kernel_call(
        functools.partial(flux_kernel, count, slices, east_west),
        (f32(levels + 2 * rows + 8, 128),) + (f32(FOLD + 2 * STEPS, 128),) * 2,
        [vmem_spec()] * (2 + len(packs)),
        flops=3_000_000_000,
        nbytes=100_000,
        vmem=FRONT_VMEM_LIMIT,
    )(crossed, spare, *packs)
    own = exchange(own, "comp", near)
    message_1 = exchange_over(for_first, "lat", near)
    message_2 = exchange_over(for_second, "lat", far_lat)
    laid_out = kernel_call(
        inner_kernel,
        (
            jax.ShapeDtypeStruct((levels, 256), jnp.bfloat16),
            f32(2, levels, 128),
            f32(rows + 2 * STEPS, levels, 128),
            f32(2, levels, 128),
        )
        + tuple(f32(rows - 2 * k, levels, 128) for k in range(STEPS)),
        [vmem_spec()] * 6,
        flops=2_000_000_000,
        nbytes=2_000_000,
    )(state, own, rows_1, rows_2, mixing, diffusivity)
    return kernel_call(
        outer_kernel,
        f32(*state.shape),
        [vmem_spec()] * (3 + len(laid_out)),
        scratch=[pltpu.VMEM((6, levels, 128), jnp.float32)] * (STEPS - 1),
        flops=300_000_000,
        nbytes=2_000_000,
    )(own, message_1, message_2, *laid_out)


def solution(mesh):
    in_specs = (
        P("comp", None, "lat", "lon"),
        P("comp", None, None),
        P("comp", None),
        P("comp", None),
        P("comp", "lat", "lon", None, None),
        P("lat", "lon"),
        P("lat", "lon"),
    )
    out_specs = P("comp", None, "lat", "lon")
    return jax.shard_map(
        on_device, mesh=mesh, in_specs=in_specs, out_specs=out_specs, check_vma=False
    )
```

```python
import functools

import jax
import jax.numpy as jnp
from jax import lax
from jax.experimental import pallas as pl
from jax.experimental.pallas import tpu as pltpu
from jax.sharding import PartitionSpec as P

STEPS = 4
EDGE = 8
FOLD = 24
AXES = ("comp", "lat", "lon")
VMEM_LIMIT = 8 * 1024 * 1024
FRONT_VMEM_LIMIT = 4 * 1024 * 1024

coupling_rate = 0.5


def vmem_spec():
    return pl.BlockSpec(memory_space=pltpu.VMEM)


def lane_ids(shape):
    return lax.broadcasted_iota(jnp.int32, shape, len(shape) - 1)


def roll(value, shift):
    shift = shift % value.shape[-1]
    return value if shift == 0 else pltpu.roll(value, shift, 1)


def as_column(row):
    n = row.shape[1]
    diagonal = lax.broadcasted_iota(jnp.int32, (n, n), 0) == lane_ids((n, n))
    return jnp.sum(jnp.where(diagonal, row, 0.0), axis=1, keepdims=True)


def spread(column):
    rows = column.shape[0]
    shape = (rows, 128)
    mine = lane_ids(shape) // EDGE == lax.broadcasted_iota(jnp.int32, shape, 0)
    return jnp.sum(jnp.where(mine, column, 0.0), axis=0, keepdims=True)


def zero_kernel(out_ref):
    out_ref[...] = jnp.zeros_like(out_ref)


def pack_kernel(state_ref, weights_ref, links_ref, land_ref, depth_ref, zero_ref, out_ref):
    surface = state_ref[0, 0]
    rows = surface.shape[0]
    table = links_ref[0, 0, 0].astype(jnp.float32)
    count = table.shape[1]
    source = as_column(table[0:1])
    weight_id = as_column(table[3:4])
    entries = weights_ref.shape[1]
    weight = jnp.sum(
        jnp.where(weight_id == lane_ids((count, entries)).astype(jnp.float32), weights_ref[...], 0.0),
        axis=1,
        keepdims=True,
    )
    picked = jnp.zeros((count, surface.shape[1]), jnp.float32)
    for row in range(rows):
        picked = jnp.where(source == float(row), surface[row : row + 1], picked)
    out_ref[0:count] = weight * picked
    code = table[1:2] * float(rows) + table[2:3]
    diagonal = lax.broadcasted_iota(jnp.int32, (count, 128), 0) == lane_ids((count, 128))
    weight_row = jnp.sum(jnp.where(diagonal, weight, 0.0), axis=0, keepdims=True)
    code_row = jnp.sum(jnp.where(diagonal, as_column(code), 0.0), axis=0, keepdims=True)
    land = as_column(land_ref[...].astype(jnp.float32))
    deep = land * as_column(depth_ref[...].astype(jnp.float32))
    out_ref[count : count + 1] = code_row
    out_ref[count + 1 : count + 2] = weight_row
    out_ref[count + 2 : count + 3] = spread(land)
    out_ref[count + 3 : count + 4] = spread(deep)
    out_ref[count + 4 : count + 8] = zero_ref[0:4]
    out_ref[count + 8 :] = surface


def write_operators(mixing_ref, diffuse_ref, mix_ref, rate_ref):
    levels = mixing_ref.shape[1]
    mix = mixing_ref[0]
    top = mix.astype(jnp.bfloat16)
    rest = (mix - top.astype(jnp.float32)).astype(jnp.bfloat16)
    mix_ref[...] = jnp.zeros_like(mix_ref)
    mix_ref[:, 0:levels] = top
    mix_ref[:, levels : 2 * levels] = top
    mix_ref[:, 2 * levels : 3 * levels] = rest
    rate = jnp.broadcast_to(as_column(diffuse_ref[...]), (levels, 128))
    rate_ref[0] = rate
    rate_ref[1] = 1.0 - 4.0 * rate


def fold_shift(group):
    return group % 2 * 4 + group // 2 * 64


def edge_kernel(state_ref, near_ref, far_ref, first_ref, second_ref):
    levels, rows, cells = state_ref.shape[1:]
    lat_odd = lax.rem(lax.axis_index("lat"), 2) == 1
    lon_odd = lax.rem(lax.axis_index("lon"), 2) == 1
    lane = lane_ids((levels, 128))
    first = last = jnp.zeros((levels, 128), jnp.float32)
    tiles = jnp.swapaxes(state_ref[0], 0, 1)
    for row in range(rows):
        turned = roll(tiles[row], row * EDGE)
        first = jnp.where(lane // EDGE == row, turned, first)
        last = jnp.where(lane // EDGE == (row - 1) % (128 // EDGE), turned, last)
    last = roll(last, 4)
    near, far = jnp.where(lon_odd, first, last), jnp.where(lon_odd, last, first)
    for ref, cells_out in ((near_ref, near), (far_ref, far)):
        folded = jnp.zeros((FOLD, 128), jnp.float32)
        lane_fold = lane_ids((FOLD, 128))
        for group in range(-(-levels // FOLD)):
            part = cells_out[group * FOLD : min((group + 1) * FOLD, levels)]
            if part.shape[0] < FOLD:
                part = jnp.concatenate([part, jnp.zeros((FOLD - part.shape[0], 128), jnp.float32)], axis=0)
            mine = (lane_fold // 64 == group // 2) & (lane_fold % EDGE // 4 == group % 2)
            folded = jnp.where(mine, roll(part, fold_shift(group)), folded)
        ref[...] = folded
    for k in range(4):
        low, high = tiles[k], tiles[rows - 4 + k]
        first_ref[k] = jnp.where(lat_odd, low, high)
        second_ref[k] = jnp.where(lat_odd, high, low)


def flux_kernel(count, slices, east_west, *refs):
    crossed_ref, zero_ref, *packs, own_ref, first_ref, second_ref = refs
    surface = crossed_ref[count + 8 :]
    rows = surface.shape[0]
    levels = own_ref.shape[0] - 2 * rows - 8
    lon, lon_count = lax.axis_index("lon"), lax.axis_size("lon")
    odd = lax.rem(lon, 2) == 1
    ocean = lax.axis_index("comp") == 0
    here = lon * rows
    after = lax.rem(lon + 1, lon_count) * rows
    before = lax.rem(lon + lon_count - 1, lon_count) * rows
    index = lax.broadcasted_iota(jnp.int32, (3 * rows, count), 0)
    wanted = jnp.where(
        index < rows, here + index, jnp.where(index < 2 * rows, after + index - rows, before + index - 2 * rows)
    ).astype(jnp.float32)
    accum = jnp.zeros((3 * rows, 128), jnp.float32)
    totals = jnp.zeros((3 * rows, 1), jnp.float32)
    for which, offset in slices:
        ref = packs[which]
        hit = (wanted == ref[offset + count : offset + count + 1, 0:count]).astype(jnp.float32)
        accum += jnp.dot(
            hit,
            ref[offset : offset + count],
            precision=lax.Precision.HIGHEST,
            preferred_element_type=jnp.float32,
        )
        totals += jnp.sum(
            hit * ref[offset + count + 1 : offset + count + 2, 0:count], axis=1, keepdims=True
        )
    imported = accum / jnp.maximum(totals, 1.0)
    spread_rows = packs[0][count + 2 : count + 4]
    column = lax.broadcasted_iota(jnp.int32, (rows, 128), 0) * EDGE == lane_ids((rows, 128))
    land = jnp.sum(jnp.where(column, spread_rows[0:1], 0.0), axis=1, keepdims=True)
    deep = jnp.sum(jnp.where(column, spread_rows[1:2], 0.0), axis=1, keepdims=True)
    all_levels = float(levels)
    deep = jnp.where(ocean, deep, all_levels)
    (first, first_at), (second, second_at) = east_west
    lane = lane_ids((1, 128))
    from_east = lax.rem(lane, EDGE) < 4

    one = packs[first][first_at : first_at + FOLD + count + 4]
    two = packs[second][second_at : second_at + FOLD + count + 4]
    to_east, to_west = jnp.where(odd, two, one), jnp.where(odd, one, two)

    def beside(at):
        return jnp.where(from_east, to_east[at : at + 1], to_west[at : at + 1])

    pieces = []
    for start in range(0, levels, FOLD):
        size = min(FOLD, levels - start)
        shift = fold_shift(start // FOLD)
        pieces.append(
            jnp.where(
                lane_ids((size, 128)) % EDGE < 4, roll(to_east[:size], -shift), roll(to_west[:size], 4 - shift)
            )
        )
    whole = jnp.concatenate(pieces, axis=0)
    land_beside = beside(FOLD + count + 2)
    deep_beside = jnp.where(ocean, beside(FOLD + count + 3), all_levels)
    block_lane = lane_ids((rows, 128))
    mine = block_lane // EDGE == lax.broadcasted_iota(jnp.int32, (rows, 128), 0)
    east = pltpu.roll(imported[rows : 2 * rows], 0, 1, stride=EDGE, stride_axis=0)
    west = pltpu.roll(imported[2 * rows :], EDGE, 1, stride=EDGE, stride_axis=0)
    spread_out = jnp.where(block_lane % EDGE < 4, east, west)
    imported_beside = jnp.sum(jnp.where(mine, spread_out, 0.0), axis=0, keepdims=True)
    flux_beside = coupling_rate * land_beside * (imported_beside - whole[0:1])
    flux = coupling_rate * land * (imported[0:rows] - surface)
    deep = jnp.broadcast_to(deep, (rows, 128))
    own_ref[0:levels] = roll(whole, STEPS * EDGE)
    own_ref[levels : levels + rows] = flux
    own_ref[levels + rows : levels + 2 * rows] = deep
    own_ref[levels + 2 * rows : levels + 2 * rows + 1] = roll(flux_beside, STEPS * EDGE)
    own_ref[levels + 2 * rows + 1 : levels + 2 * rows + 2] = roll(deep_beside, STEPS * EDGE)
    own_ref[levels + 2 * rows + 2 :] = zero_ref[0:6]
    width = STEPS * EDGE
    sides = []
    for at in (0, rows - STEPS):
        lane_at = at * EDGE
        folded = jnp.zeros((FOLD, 128), jnp.float32)
        lane_fold = lane_ids((FOLD, 128))
        for group in range(-(-levels // FOLD)):
            part = whole[group * FOLD : min((group + 1) * FOLD, levels)]
            if part.shape[0] < FOLD:
                extra = jnp.zeros((FOLD - part.shape[0], 128), jnp.float32)
                index = lax.broadcasted_iota(jnp.int32, extra.shape, 0)
                extra = jnp.where(index == 0, flux_beside, jnp.where(index == 1, deep_beside, extra))
                part = jnp.concatenate([part, extra], axis=0)
            folded = jnp.where(lane_fold // width == group, roll(part, group * width - lane_at), folded)
        sides.append((folded, flux[at : at + STEPS], deep[at : at + STEPS]))
    lat_odd = lax.rem(lax.axis_index("lat"), 2) == 1
    starts = (0, FOLD, FOLD + STEPS, FOLD + 2 * STEPS)
    for (low, high), begin, end in zip(zip(*sides), starts, starts[1:]):
        first_ref[begin:end] = jnp.where(lat_odd, low, high)
        second_ref[begin:end] = jnp.where(lat_odd, high, low)


def halves(value):
    hi = value.astype(jnp.bfloat16)
    return hi, (value - hi.astype(jnp.float32)).astype(jnp.bfloat16)


class Update:
    def __init__(self, mix_ref, rate_ref):
        self.mixer, self.rate_ref = mix_ref[...], rate_ref
        self.levels = rate_ref.shape[1]
        self.pad = jnp.zeros((self.mixer.shape[1] - 3 * self.levels, 128), jnp.bfloat16)
        tail = lax.broadcasted_iota(jnp.int32, (8, 128), 0)
        self.first = tail == 0
        self.tail = (tail + (self.levels - 8)).astype(jnp.float32)

    def moved(self, x, neighbours, flux, deep):
        value = self.rate_ref[1] * x + self.rate_ref[0] * neighbours
        head = value[:8] + jnp.where(self.first, flux, 0.0)
        tail = jnp.where(self.tail < deep, value[-8:], 0.0)
        return jnp.concatenate([head, value[8:-8], tail], axis=0)

    def mixed(self, values):
        out = []
        for value in values:
            hi, lo = halves(value)
            full = jnp.concatenate([hi, lo, hi, self.pad], axis=0)
            out.append(jnp.dot(self.mixer, full, preferred_element_type=jnp.float32))
        return out

    def settled(self, new, x, deep):
        sea = jnp.broadcast_to(deep, (self.levels - 8, 128)) > 0.0
        body = jnp.where(sea, new[:-8], x[:-8])
        tail = jnp.where(self.tail < deep, new[-8:], x[-8:])
        return jnp.concatenate([body, tail], axis=0)

    def rows(self, tiles, flux, deep):
        values = [
            self.moved(x, above + below + roll(x, 1) + roll(x, -1), f, d)
            for (above, x, below), f, d in zip(tiles, flux, deep)
        ]
        return [self.settled(new, t[1], d) for new, t, d in zip(self.mixed(values), tiles, deep)]


def lat_place():
    lat = lax.axis_index("lat")
    return lax.rem(lat, 2) == 1, (lat > 0) & (lat < lax.axis_size("lat") - 1)


def inner_kernel(
    state_ref, own_ref, rows1_ref, rows2_ref, mixing_ref, diffuse_ref, mix_ref, rate_ref, x_ref, side_ref, *inner_refs
):
    levels, rows, cells = state_ref.shape[1:]
    slots = rows + 2 * STEPS
    odd, inside = lat_place()
    first_at = jnp.where(odd, 0, rows + STEPS)
    for k in range(STEPS):
        x_ref[first_at + k] = rows1_ref[k]
        x_ref[rows + STEPS - first_at + k] = jnp.where(inside, rows2_ref[k], 0.0)
    x_ref[STEPS : STEPS + rows] = jnp.swapaxes(state_ref[0], 0, 1)
    write_operators(mixing_ref, diffuse_ref, mix_ref, rate_ref)
    update = Update(mix_ref, rate_ref)
    flux = [own_ref[levels + r : levels + r + 1] for r in range(rows)]
    deep = [own_ref[levels + rows + r : levels + rows + r + 1] for r in range(rows)]
    source, first = x_ref, 0
    for step in range(STEPS):
        target, at = inner_refs[step], STEPS + step
        for slot in range(at, slots - at, 2):
            pair = (slot, slot + 1)
            tiles = [[source[s - first + k] for k in (-1, 0, 1)] for s in pair]
            new = update.rows(tiles, [flux[s - STEPS] for s in pair], [deep[s - STEPS] for s in pair])
            for s, tile in zip(pair, new):
                target[s - at] = tile
        source, first = target, at
    lane = lane_ids((levels, 128))
    left = right = jnp.zeros((levels, 128), jnp.float32)
    for slot in range(slots):
        start = slot * EDGE
        turned = roll(x_ref[slot], start)
        right = jnp.where(lane // EDGE == slot, turned, right)
        left = jnp.where(lane // EDGE == (slot - 1) % slots, turned, left)
    side_ref[0] = roll(left, EDGE)
    side_ref[1] = right


def outer_kernel(own_ref, msg1_ref, msg2_ref, mix_ref, rate_ref, x_ref, side_ref, *refs):
    inner_refs, out_ref, outer_refs = refs[:STEPS], refs[STEPS], refs[STEPS + 1 :]
    levels, rows, cells = out_ref.shape[1:]
    slots = rows + 2 * STEPS
    odd, inside = lat_place()
    one, two = msg1_ref[...], jnp.where(inside, msg2_ref[...], 0.0)
    top, bottom = jnp.where(odd, one, two), jnp.where(odd, two, one)

    def per_slot(at, own_at, slot):
        if slot < STEPS:
            return top[at + slot : at + slot + 1]
        if slot < STEPS + rows:
            return own_ref[own_at + slot - STEPS : own_at + slot - STEPS + 1]
        return bottom[at + slot - STEPS - rows : at + slot - STEPS - rows + 1]

    flux_rows = [per_slot(FOLD, levels, s) for s in range(slots)]
    deep_rows = [per_slot(FOLD + STEPS, levels + rows, s) for s in range(slots)]
    lane1 = lane_ids((1, 128))
    lane = lane_ids((levels, 128))
    place = lane % EDGE
    width = STEPS * EDGE

    def around(upper, own, lower, group):
        at = lane_ids(own.shape)
        upper, lower = roll(upper, -group * width), roll(lower, 128 - width - group * width)
        return jnp.where(at < width, upper, jnp.where(at < 128 - width, own, lower))

    pieces = []
    for start in range(0, levels, FOLD):
        size = min(FOLD, levels - start)
        pieces.append(around(top[:size], own_ref[start : start + size], bottom[:size], start // FOLD))
    mid = jnp.concatenate(pieces, axis=0)
    beside = levels % FOLD
    at = levels + 2 * rows
    flux_mid, deep_mid = (
        around(
            top[beside + k : beside + k + 1],
            own_ref[at + k : at + k + 1],
            bottom[beside + k : beside + k + 1],
            levels // FOLD,
        )
        for k in range(2)
    )
    left, right = side_ref[0], side_ref[1]
    flux_left = flux_right = deep_side = jnp.zeros((1, 128), jnp.float32)
    for slot in range(slots):
        start = slot * EDGE
        mine1 = (lane1 >= start) & (lane1 < start + EDGE)
        flux_left = jnp.where(mine1, roll(flux_rows[slot], start + EDGE), flux_left)
        flux_right = jnp.where(mine1, roll(flux_rows[slot], start), flux_right)
        deep_side = jnp.where(mine1, deep_rows[slot], deep_side)

    def strip(tile, west, east):
        above_below = roll(tile, EDGE) + roll(tile, -EDGE)
        to_west, to_east = roll(tile, 1), roll(tile, -1)
        if west is not None:
            to_west = jnp.where(place == 0, roll(west, 1 - EDGE), to_west)
        if east is not None:
            to_east = jnp.where(place == EDGE - 1, roll(east, EDGE - 1), to_east)
        return above_below + to_west + to_east

    update = Update(mix_ref, rate_ref)

    def tile_at(step, s):
        if step == 0:
            return x_ref[s]
        if 3 + step <= s <= slots - 4 - step:
            return inner_refs[step - 1][s - 3 - step]
        return outer_refs[step - 1][s - step if s < slots // 2 else s - (slots - 6 - step)]

    done = [None] * rows

    def put(s, tile):
        tile = jnp.where((lane < 4) | (lane >= cells - 4), roll(sides, -s * EDGE), tile)
        done[s - STEPS] = tile

    for step in range(STEPS):
        last = step == STEPS - 1
        z_left = update.moved(left, strip(left, None, mid), flux_left, deep_side)
        z_right = update.moved(right, strip(right, mid, None), flux_right, deep_side)
        new_left, new_right = update.mixed([z_left, z_right])
        if not last:
            z_mid = update.moved(mid, strip(mid, left, right), flux_mid, deep_mid)
            mid = update.settled(update.mixed([z_mid])[0], mid, deep_mid)
        left = update.settled(new_left, left, deep_side)
        right = update.settled(new_right, right, deep_side)
        if last:
            sides = jnp.where(place < 4, right, roll(left, -EDGE))
        low_rows = list(range(step + 1, step + 4))
        todo = low_rows + [slots - 1 - s for s in reversed(low_rows)]
        for k in range(0, len(todo), 3):
            group = todo[k : k + 3]
            tiles = [[tile_at(step, s + j) for j in (-1, 0, 1)] for s in group]
            new = update.rows(tiles, [flux_rows[s] for s in group], [deep_rows[s] for s in group])
            for j, (s, tile) in enumerate(zip(group, new)):
                if last:
                    put(s, tile)
                else:
                    outer_refs[step][k + j] = tile
    for s in (slots // 2 - 1, slots // 2):
        put(s, inner_refs[STEPS - 1][s - slots // 2 + 1])
    out_ref[0] = jnp.swapaxes(jnp.stack(done, axis=0), 0, 1)


def kernel_call(body, out_shape, blocks, scratch=(), flops=0, nbytes=0, vmem=VMEM_LIMIT, grid=()):
    return pl.pallas_call(
        body,
        out_shape=out_shape,
        grid=grid,
        in_specs=blocks,
        out_specs=jax.tree.map(lambda _: vmem_spec(), out_shape),
        scratch_shapes=scratch,
        compiler_params=pltpu.CompilerParams(vmem_limit_bytes=vmem),
        cost_estimate=pl.CostEstimate(flops=flops, bytes_accessed=nbytes, transcendentals=0),
    )


def f32(*shape):
    return jax.ShapeDtypeStruct(shape, jnp.float32)


def exchange(value, axis, partner):
    size = lax.axis_size(axis)
    pairs = [(i, partner(i)) for i in range(size) if 0 <= partner(i) < size]
    return lax.ppermute(value, axis, pairs)


def exchange_over(value, axis, partner):
    size, sections = lax.axis_size(axis), lax.axis_size("comp")
    pairs = [
        (section * size + i, (sections - 1 - section) * size + partner(i))
        for section in range(sections)
        for i in range(size)
    ]
    return lax.ppermute(value, ("comp", axis), pairs)


def on_device(state, mixing, diffusivity, weights, links, land, depth):
    levels, rows, cells = state.shape[1:]
    count = links.shape[-1]
    pack_rows = count + 8
    lat_count, lon_count = lax.axis_size("lat"), lax.axis_size("lon")

    def near(i):
        return i ^ 1

    def far_round(i):
        return (i - 1 if i % 2 == 0 else i + 1) % lon_count

    def far_lat(i):
        return (i - 1 if i % 2 == 0 else i + 1) % lat_count

    zeros = kernel_call(
        zero_kernel, f32(8, 128), [], flops=2_000_000_000, nbytes=4096, vmem=FRONT_VMEM_LIMIT
    )()
    pack = kernel_call(
        pack_kernel,
        f32(pack_rows + rows, 128),
        [vmem_spec()] * 6,
        flops=2_000_000_000,
        nbytes=700_000,
        vmem=FRONT_VMEM_LIMIT,
    )(state, weights, links, land.reshape(1, rows), depth.reshape(1, rows), zeros)
    state, pack = lax.optimization_barrier((state, pack))
    crossed = exchange(pack, "comp", near)
    edge_near, edge_far, up_down_1, up_down_2 = kernel_call(
        edge_kernel,
        (f32(FOLD, 128),) * 2 + (f32(STEPS, levels, 128),) * 2,
        [vmem_spec()],
        flops=2_000_000_000,
        nbytes=900_000,
        vmem=FRONT_VMEM_LIMIT,
    )(state)
    spare = kernel_call(
        zero_kernel, f32(16, 128), [], flops=2_000_000_000, nbytes=4096, vmem=FRONT_VMEM_LIMIT
    )()
    spare, edge_near = lax.optimization_barrier((spare, edge_near))
    beside_1 = exchange_over(jnp.concatenate([edge_near, crossed[:pack_rows]], axis=0), "lon", near)
    beside_2 = exchange_over(jnp.concatenate([edge_far, crossed[:pack_rows]], axis=0), "lon", far_round)
    if lon_count == 4:
        across = exchange_over(crossed[:pack_rows], "lon", lambda i: i ^ 2)
        packs = [pack, beside_1, across, beside_2]
        slices = [(0, 0), (1, FOLD), (2, 0), (3, FOLD)]
        east_west = ((1, 0), (3, 0))
    else:
        packs = [pack, beside_1, beside_2, lax.all_gather(pack[:pack_rows], "lon", axis=0, tiled=True)]
        slices = [(3, k * pack_rows) for k in range(lon_count)]
        east_west = ((1, 0), (2, 0))
    rows_1 = exchange(up_down_1, "lat", near)
    rows_2 = exchange(up_down_2, "lat", far_lat)
    rows_1, packs[0] = lax.optimization_barrier((rows_1, packs[0]))
    own, for_first, for_second = kernel_call(
        functools.partial(flux_kernel, count, slices, east_west),
        (f32(levels + 2 * rows + 8, 128),) + (f32(FOLD + 2 * STEPS, 128),) * 2,
        [vmem_spec()] * (2 + len(packs)),
        flops=3_000_000_000,
        nbytes=100_000,
        vmem=FRONT_VMEM_LIMIT,
    )(crossed, spare, *packs)
    own = exchange(own, "comp", near)
    message_1 = exchange_over(for_first, "lat", near)
    message_2 = exchange_over(for_second, "lat", far_lat)
    laid_out = kernel_call(
        inner_kernel,
        (
            jax.ShapeDtypeStruct((levels, 256), jnp.bfloat16),
            f32(2, levels, 128),
            f32(rows + 2 * STEPS, levels, 128),
            f32(2, levels, 128),
        )
        + tuple(f32(rows - 2 * k, levels, 128) for k in range(STEPS)),
        [vmem_spec()] * 6,
        flops=2_000_000_000,
        nbytes=2_000_000,
    )(state, own, rows_1, rows_2, mixing, diffusivity)
    return kernel_call(
        outer_kernel,
        f32(*state.shape),
        [vmem_spec()] * (3 + len(laid_out)),
        scratch=[pltpu.VMEM((6, levels, 128), jnp.float32)] * (STEPS - 1),
        flops=300_000_000,
        nbytes=2_000_000,
    )(own, message_1, message_2, *laid_out)


def solution(mesh):
    in_specs = (
        P("comp", None, "lat", "lon"),
        P("comp", None, None),
        P("comp", None),
        P("comp", None),
        P("comp", "lat", "lon", None, None),
        P("lat", "lon"),
        P("lat", "lon"),
    )
    out_specs = P("comp", None, "lat", "lon")
    return jax.shard_map(
        on_device, mesh=mesh, in_specs=in_specs, out_specs=out_specs, check_vma=False
    )
```

```python
import functools

import jax
import jax.numpy as jnp
from jax import lax
from jax.experimental import pallas as pl
from jax.experimental.pallas import tpu as pltpu
from jax.sharding import PartitionSpec as P

STEPS = 4
EDGE = 8
FOLD = 24
AXES = ("comp", "lat", "lon")
VMEM_LIMIT = 8 * 1024 * 1024
FRONT_VMEM_LIMIT = 4 * 1024 * 1024

coupling_rate = 0.5


def vmem_spec():
    return pl.BlockSpec(memory_space=pltpu.VMEM)


def lane_ids(shape):
    return lax.broadcasted_iota(jnp.int32, shape, len(shape) - 1)


def roll(value, shift):
    shift = shift % value.shape[-1]
    return value if shift == 0 else pltpu.roll(value, shift, 1)


def as_column(row):
    n = row.shape[1]
    diagonal = lax.broadcasted_iota(jnp.int32, (n, n), 0) == lane_ids((n, n))
    return jnp.sum(jnp.where(diagonal, row, 0.0), axis=1, keepdims=True)


def spread(column):
    rows = column.shape[0]
    shape = (rows, 128)
    mine = lane_ids(shape) // EDGE == lax.broadcasted_iota(jnp.int32, shape, 0)
    return jnp.sum(jnp.where(mine, column, 0.0), axis=0, keepdims=True)


def zero_kernel(out_ref):
    out_ref[...] = jnp.zeros_like(out_ref)


def pack_kernel(state_ref, weights_ref, links_ref, land_ref, depth_ref, zero_ref, out_ref):
    surface = state_ref[0, 0]
    rows = surface.shape[0]
    table = links_ref[0, 0, 0].astype(jnp.float32)
    count = table.shape[1]
    source = as_column(table[0:1])
    weight_id = as_column(table[3:4])
    entries = weights_ref.shape[1]
    weight = jnp.sum(
        jnp.where(weight_id == lane_ids((count, entries)).astype(jnp.float32), weights_ref[...], 0.0),
        axis=1,
        keepdims=True,
    )
    picked = jnp.zeros((count, surface.shape[1]), jnp.float32)
    for row in range(rows):
        picked = jnp.where(source == float(row), surface[row : row + 1], picked)
    out_ref[0:count] = weight * picked
    code = table[1:2] * float(rows) + table[2:3]
    diagonal = lax.broadcasted_iota(jnp.int32, (count, 128), 0) == lane_ids((count, 128))
    weight_row = jnp.sum(jnp.where(diagonal, weight, 0.0), axis=0, keepdims=True)
    code_row = jnp.sum(jnp.where(diagonal, as_column(code), 0.0), axis=0, keepdims=True)
    land = as_column(land_ref[...].astype(jnp.float32))
    deep = land * as_column(depth_ref[...].astype(jnp.float32))
    out_ref[count : count + 1] = code_row
    out_ref[count + 1 : count + 2] = weight_row
    out_ref[count + 2 : count + 3] = spread(land)
    out_ref[count + 3 : count + 4] = spread(deep)
    out_ref[count + 4 : count + 8] = zero_ref[0:4]
    out_ref[count + 8 :] = surface


def write_operators(mixing_ref, diffuse_ref, mix_ref, rate_ref):
    levels = mixing_ref.shape[1]
    mix = mixing_ref[0]
    top = mix.astype(jnp.bfloat16)
    rest = (mix - top.astype(jnp.float32)).astype(jnp.bfloat16)
    mix_ref[...] = jnp.zeros_like(mix_ref)
    mix_ref[:, 0:levels] = top
    mix_ref[:, levels : 2 * levels] = top
    mix_ref[:, 2 * levels : 3 * levels] = rest
    rate = jnp.broadcast_to(as_column(diffuse_ref[...]), (levels, 128))
    rate_ref[0] = rate
    rate_ref[1] = 1.0 - 4.0 * rate


def fold_shift(group):
    return group % 2 * 4 + group // 2 * 64


def edge_kernel(state_ref, near_ref, far_ref, first_ref, second_ref):
    levels, rows, cells = state_ref.shape[1:]
    lat_odd = lax.rem(lax.axis_index("lat"), 2) == 1
    lon_odd = lax.rem(lax.axis_index("lon"), 2) == 1
    lane = lane_ids((levels, 128))
    first = last = jnp.zeros((levels, 128), jnp.float32)
    tiles = jnp.swapaxes(state_ref[0], 0, 1)
    for row in range(rows):
        turned = roll(tiles[row], row * EDGE)
        first = jnp.where(lane // EDGE == row, turned, first)
        last = jnp.where(lane // EDGE == (row - 1) % (128 // EDGE), turned, last)
    last = roll(last, 4)
    near, far = jnp.where(lon_odd, first, last), jnp.where(lon_odd, last, first)
    for ref, cells_out in ((near_ref, near), (far_ref, far)):
        folded = jnp.zeros((FOLD, 128), jnp.float32)
        lane_fold = lane_ids((FOLD, 128))
        for group in range(-(-levels // FOLD)):
            part = cells_out[group * FOLD : min((group + 1) * FOLD, levels)]
            if part.shape[0] < FOLD:
                part = jnp.concatenate([part, jnp.zeros((FOLD - part.shape[0], 128), jnp.float32)], axis=0)
            mine = (lane_fold // 64 == group // 2) & (lane_fold % EDGE // 4 == group % 2)
            folded = jnp.where(mine, roll(part, fold_shift(group)), folded)
        ref[...] = folded
    for k in range(4):
        low, high = tiles[k], tiles[rows - 4 + k]
        first_ref[k] = jnp.where(lat_odd, low, high)
        second_ref[k] = jnp.where(lat_odd, high, low)


def flux_kernel(count, slices, east_west, *refs):
    crossed_ref, zero_ref, *packs, own_ref, first_ref, second_ref = refs
    surface = crossed_ref[count + 8 :]
    rows = surface.shape[0]
    levels = own_ref.shape[0] - 2 * rows - 8
    lon, lon_count = lax.axis_index("lon"), lax.axis_size("lon")
    odd = lax.rem(lon, 2) == 1
    ocean = lax.axis_index("comp") == 0
    here = lon * rows
    after = lax.rem(lon + 1, lon_count) * rows
    before = lax.rem(lon + lon_count - 1, lon_count) * rows
    index = lax.broadcasted_iota(jnp.int32, (3 * rows, count), 0)
    wanted = jnp.where(
        index < rows, here + index, jnp.where(index < 2 * rows, after + index - rows, before + index - 2 * rows)
    ).astype(jnp.float32)
    accum = jnp.zeros((3 * rows, 128), jnp.float32)
    totals = jnp.zeros((3 * rows, 1), jnp.float32)
    for which, offset in slices:
        ref = packs[which]
        hit = (wanted == ref[offset + count : offset + count + 1, 0:count]).astype(jnp.float32)
        accum += jnp.dot(
            hit,
            ref[offset : offset + count],
            precision=lax.Precision.HIGHEST,
            preferred_element_type=jnp.float32,
        )
        totals += jnp.sum(
            hit * ref[offset + count + 1 : offset + count + 2, 0:count], axis=1, keepdims=True
        )
    imported = accum / jnp.maximum(totals, 1.0)
    spread_rows = packs[0][count + 2 : count + 4]
    column = lax.broadcasted_iota(jnp.int32, (rows, 128), 0) * EDGE == lane_ids((rows, 128))
    land = jnp.sum(jnp.where(column, spread_rows[0:1], 0.0), axis=1, keepdims=True)
    deep = jnp.sum(jnp.where(column, spread_rows[1:2], 0.0), axis=1, keepdims=True)
    all_levels = float(levels)
    deep = jnp.where(ocean, deep, all_levels)
    (first, first_at), (second, second_at) = east_west
    lane = lane_ids((1, 128))
    from_east = lax.rem(lane, EDGE) < 4

    one = packs[first][first_at : first_at + FOLD + count + 4]
    two = packs[second][second_at : second_at + FOLD + count + 4]
    to_east, to_west = jnp.where(odd, two, one), jnp.where(odd, one, two)

    def beside(at):
        return jnp.where(from_east, to_east[at : at + 1], to_west[at : at + 1])

    pieces = []
    for start in range(0, levels, FOLD):
        size = min(FOLD, levels - start)
        shift = fold_shift(start // FOLD)
        pieces.append(
            jnp.where(
                lane_ids((size, 128)) % EDGE < 4, roll(to_east[:size], -shift), roll(to_west[:size], 4 - shift)
            )
        )
    whole = jnp.concatenate(pieces, axis=0)
    land_beside = beside(FOLD + count + 2)
    deep_beside = jnp.where(ocean, beside(FOLD + count + 3), all_levels)
    block_lane = lane_ids((rows, 128))
    mine = block_lane // EDGE == lax.broadcasted_iota(jnp.int32, (rows, 128), 0)
    east = pltpu.roll(imported[rows : 2 * rows], 0, 1, stride=EDGE, stride_axis=0)
    west = pltpu.roll(imported[2 * rows :], EDGE, 1, stride=EDGE, stride_axis=0)
    spread_out = jnp.where(block_lane % EDGE < 4, east, west)
    imported_beside = jnp.sum(jnp.where(mine, spread_out, 0.0), axis=0, keepdims=True)
    flux_beside = coupling_rate * land_beside * (imported_beside - whole[0:1])
    flux = coupling_rate * land * (imported[0:rows] - surface)
    deep = jnp.broadcast_to(deep, (rows, 128))
    own_ref[0:levels] = roll(whole, STEPS * EDGE)
    own_ref[levels : levels + rows] = flux
    own_ref[levels + rows : levels + 2 * rows] = deep
    own_ref[levels + 2 * rows : levels + 2 * rows + 1] = roll(flux_beside, STEPS * EDGE)
    own_ref[levels + 2 * rows + 1 : levels + 2 * rows + 2] = roll(deep_beside, STEPS * EDGE)
    own_ref[levels + 2 * rows + 2 :] = zero_ref[0:6]
    width = STEPS * EDGE
    sides = []
    for at in (0, rows - STEPS):
        lane_at = at * EDGE
        folded = jnp.zeros((FOLD, 128), jnp.float32)
        lane_fold = lane_ids((FOLD, 128))
        for group in range(-(-levels // FOLD)):
            part = whole[group * FOLD : min((group + 1) * FOLD, levels)]
            if part.shape[0] < FOLD:
                extra = jnp.zeros((FOLD - part.shape[0], 128), jnp.float32)
                index = lax.broadcasted_iota(jnp.int32, extra.shape, 0)
                extra = jnp.where(index == 0, flux_beside, jnp.where(index == 1, deep_beside, extra))
                part = jnp.concatenate([part, extra], axis=0)
            folded = jnp.where(lane_fold // width == group, roll(part, group * width - lane_at), folded)
        sides.append((folded, flux[at : at + STEPS], deep[at : at + STEPS]))
    lat_odd = lax.rem(lax.axis_index("lat"), 2) == 1
    starts = (0, FOLD, FOLD + STEPS, FOLD + 2 * STEPS)
    for (low, high), begin, end in zip(zip(*sides), starts, starts[1:]):
        first_ref[begin:end] = jnp.where(lat_odd, low, high)
        second_ref[begin:end] = jnp.where(lat_odd, high, low)


def halves(value):
    hi = value.astype(jnp.bfloat16)
    return hi, (value - hi.astype(jnp.float32)).astype(jnp.bfloat16)


class Update:
    def __init__(self, mix_ref, rate_ref):
        self.mixer, self.rate_ref = mix_ref[...], rate_ref
        self.levels = rate_ref.shape[1]
        self.pad = jnp.zeros((self.mixer.shape[1] - 3 * self.levels, 128), jnp.bfloat16)
        tail = lax.broadcasted_iota(jnp.int32, (8, 128), 0)
        self.first = tail == 0
        self.tail = (tail + (self.levels - 8)).astype(jnp.float32)

    def moved(self, x, neighbours, flux, deep):
        value = self.rate_ref[1] * x + self.rate_ref[0] * neighbours
        head = value[:8] + jnp.where(self.first, flux, 0.0)
        tail = jnp.where(self.tail < deep, value[-8:], 0.0)
        return jnp.concatenate([head, value[8:-8], tail], axis=0)

    def mixed(self, values):
        out = []
        for value in values:
            hi, lo = halves(value)
            full = jnp.concatenate([hi, lo, hi, self.pad], axis=0)
            out.append(jnp.dot(self.mixer, full, preferred_element_type=jnp.float32))
        return out

    def settled(self, new, x, deep):
        sea = jnp.broadcast_to(deep, (self.levels - 8, 128)) > 0.0
        body = jnp.where(sea, new[:-8], x[:-8])
        tail = jnp.where(self.tail < deep, new[-8:], x[-8:])
        return jnp.concatenate([body, tail], axis=0)

    def rows(self, tiles, flux, deep):
        values = [
            self.moved(x, above + below + roll(x, 1) + roll(x, -1), f, d)
            for (above, x, below), f, d in zip(tiles, flux, deep)
        ]
        return [self.settled(new, t[1], d) for new, t, d in zip(self.mixed(values), tiles, deep)]


def lat_place():
    lat = lax.axis_index("lat")
    return lax.rem(lat, 2) == 1, (lat > 0) & (lat < lax.axis_size("lat") - 1)


def inner_kernel(
    state_ref, own_ref, rows1_ref, rows2_ref, mixing_ref, diffuse_ref, mix_ref, rate_ref, x_ref, side_ref, *inner_refs
):
    levels, rows, cells = state_ref.shape[1:]
    slots = rows + 2 * STEPS
    odd, inside = lat_place()
    first_at = jnp.where(odd, 0, rows + STEPS)
    for k in range(STEPS):
        x_ref[first_at + k] = rows1_ref[k]
        x_ref[rows + STEPS - first_at + k] = jnp.where(inside, rows2_ref[k], 0.0)
    x_ref[STEPS : STEPS + rows] = jnp.swapaxes(state_ref[0], 0, 1)
    write_operators(mixing_ref, diffuse_ref, mix_ref, rate_ref)
    update = Update(mix_ref, rate_ref)
    flux = [own_ref[levels + r : levels + r + 1] for r in range(rows)]
    deep = [own_ref[levels + rows + r : levels + rows + r + 1] for r in range(rows)]
    source, first = x_ref, 0
    for step in range(STEPS):
        target, at = inner_refs[step], STEPS + step
        for slot in range(at, slots - at, 2):
            pair = (slot, slot + 1)
            tiles = [[source[s - first + k] for k in (-1, 0, 1)] for s in pair]
            new = update.rows(tiles, [flux[s - STEPS] for s in pair], [deep[s - STEPS] for s in pair])
            for s, tile in zip(pair, new):
                target[s - at] = tile
        source, first = target, at
    lane = lane_ids((levels, 128))
    left = right = jnp.zeros((levels, 128), jnp.float32)
    for slot in range(slots):
        start = slot * EDGE
        turned = roll(x_ref[slot], start)
        right = jnp.where(lane // EDGE == slot, turned, right)
        left = jnp.where(lane // EDGE == (slot - 1) % slots, turned, left)
    side_ref[0] = roll(left, EDGE)
    side_ref[1] = right


def outer_kernel(own_ref, msg1_ref, msg2_ref, mix_ref, rate_ref, x_ref, side_ref, *refs):
    inner_refs, out_ref, outer_refs = refs[:STEPS], refs[STEPS], refs[STEPS + 1 :]
    levels, rows, cells = out_ref.shape[1:]
    slots = rows + 2 * STEPS
    odd, inside = lat_place()
    one, two = msg1_ref[...], jnp.where(inside, msg2_ref[...], 0.0)
    top, bottom = jnp.where(odd, one, two), jnp.where(odd, two, one)

    def per_slot(at, own_at, slot):
        if slot < STEPS:
            return top[at + slot : at + slot + 1]
        if slot < STEPS + rows:
            return own_ref[own_at + slot - STEPS : own_at + slot - STEPS + 1]
        return bottom[at + slot - STEPS - rows : at + slot - STEPS - rows + 1]

    flux_rows = [per_slot(FOLD, levels, s) for s in range(slots)]
    deep_rows = [per_slot(FOLD + STEPS, levels + rows, s) for s in range(slots)]
    lane1 = lane_ids((1, 128))
    lane = lane_ids((levels, 128))
    place = lane % EDGE
    width = STEPS * EDGE

    def around(upper, own, lower, group):
        at = lane_ids(own.shape)
        upper, lower = roll(upper, -group * width), roll(lower, 128 - width - group * width)
        return jnp.where(at < width, upper, jnp.where(at < 128 - width, own, lower))

    pieces = []
    for start in range(0, levels, FOLD):
        size = min(FOLD, levels - start)
        pieces.append(around(top[:size], own_ref[start : start + size], bottom[:size], start // FOLD))
    mid = jnp.concatenate(pieces, axis=0)
    beside = levels % FOLD
    at = levels + 2 * rows
    flux_mid, deep_mid = (
        around(
            top[beside + k : beside + k + 1],
            own_ref[at + k : at + k + 1],
            bottom[beside + k : beside + k + 1],
            levels // FOLD,
        )
        for k in range(2)
    )
    left, right = side_ref[0], side_ref[1]
    flux_left = flux_right = deep_side = jnp.zeros((1, 128), jnp.float32)
    for slot in range(slots):
        start = slot * EDGE
        mine1 = (lane1 >= start) & (lane1 < start + EDGE)
        turned = roll(flux_rows[slot], start)
        flux_left = jnp.where(lane1 // EDGE == (slot - 1) % slots, turned, flux_left)
        flux_right = jnp.where(mine1, turned, flux_right)
        deep_side = jnp.where(mine1, deep_rows[slot], deep_side)
    flux_left = roll(flux_left, EDGE)

    def strip(tile, west, east):
        above_below = roll(tile, EDGE) + roll(tile, -EDGE)
        to_west, to_east = roll(tile, 1), roll(tile, -1)
        if west is not None:
            to_west = jnp.where(place == 0, roll(west, 1 - EDGE), to_west)
        if east is not None:
            to_east = jnp.where(place == EDGE - 1, roll(east, EDGE - 1), to_east)
        return above_below + to_west + to_east

    update = Update(mix_ref, rate_ref)

    def tile_at(step, s):
        if step == 0:
            return x_ref[s]
        if 3 + step <= s <= slots - 4 - step:
            return inner_refs[step - 1][s - 3 - step]
        return outer_refs[step - 1][s - step if s < slots // 2 else s - (slots - 6 - step)]

    done = [None] * rows

    def put(s, tile):
        tile = jnp.where((lane < 4) | (lane >= cells - 4), roll(sides, -s * EDGE), tile)
        done[s - STEPS] = tile

    for step in range(STEPS):
        last = step == STEPS - 1
        z_left = update.moved(left, strip(left, None, mid), flux_left, deep_side)
        z_right = update.moved(right, strip(right, mid, None), flux_right, deep_side)
        new_left, new_right = update.mixed([z_left, z_right])
        if not last:
            z_mid = update.moved(mid, strip(mid, left, right), flux_mid, deep_mid)
            mid = update.settled(update.mixed([z_mid])[0], mid, deep_mid)
        left = update.settled(new_left, left, deep_side)
        right = update.settled(new_right, right, deep_side)
        if last:
            sides = jnp.where(place < 4, right, roll(left, -EDGE))
        low_rows = list(range(step + 1, step + 4))
        todo = low_rows + [slots - 1 - s for s in reversed(low_rows)]
        for k in range(0, len(todo), 3):
            group = todo[k : k + 3]
            tiles = [[tile_at(step, s + j) for j in (-1, 0, 1)] for s in group]
            new = update.rows(tiles, [flux_rows[s] for s in group], [deep_rows[s] for s in group])
            for j, (s, tile) in enumerate(zip(group, new)):
                if last:
                    put(s, tile)
                else:
                    outer_refs[step][k + j] = tile
    for s in (slots // 2 - 1, slots // 2):
        put(s, inner_refs[STEPS - 1][s - slots // 2 + 1])
    out_ref[0] = jnp.swapaxes(jnp.stack(done, axis=0), 0, 1)


def kernel_call(body, out_shape, blocks, scratch=(), flops=0, nbytes=0, vmem=VMEM_LIMIT, grid=()):
    return pl.pallas_call(
        body,
        out_shape=out_shape,
        grid=grid,
        in_specs=blocks,
        out_specs=jax.tree.map(lambda _: vmem_spec(), out_shape),
        scratch_shapes=scratch,
        compiler_params=pltpu.CompilerParams(vmem_limit_bytes=vmem),
        cost_estimate=pl.CostEstimate(flops=flops, bytes_accessed=nbytes, transcendentals=0),
    )


def f32(*shape):
    return jax.ShapeDtypeStruct(shape, jnp.float32)


def exchange(value, axis, partner):
    size = lax.axis_size(axis)
    pairs = [(i, partner(i)) for i in range(size) if 0 <= partner(i) < size]
    return lax.ppermute(value, axis, pairs)


def exchange_over(value, axis, partner):
    size, sections = lax.axis_size(axis), lax.axis_size("comp")
    pairs = [
        (section * size + i, (sections - 1 - section) * size + partner(i))
        for section in range(sections)
        for i in range(size)
    ]
    return lax.ppermute(value, ("comp", axis), pairs)


def on_device(state, mixing, diffusivity, weights, links, land, depth):
    levels, rows, cells = state.shape[1:]
    count = links.shape[-1]
    pack_rows = count + 8
    lat_count, lon_count = lax.axis_size("lat"), lax.axis_size("lon")

    def near(i):
        return i ^ 1

    def far_round(i):
        return (i - 1 if i % 2 == 0 else i + 1) % lon_count

    def far_lat(i):
        return (i - 1 if i % 2 == 0 else i + 1) % lat_count

    zeros = kernel_call(
        zero_kernel, f32(8, 128), [], flops=2_000_000_000, nbytes=4096, vmem=FRONT_VMEM_LIMIT
    )()
    pack = kernel_call(
        pack_kernel,
        f32(pack_rows + rows, 128),
        [vmem_spec()] * 6,
        flops=2_000_000_000,
        nbytes=700_000,
        vmem=FRONT_VMEM_LIMIT,
    )(state, weights, links, land.reshape(1, rows), depth.reshape(1, rows), zeros)
    state, pack = lax.optimization_barrier((state, pack))
    crossed = exchange(pack, "comp", near)
    edge_near, edge_far, up_down_1, up_down_2 = kernel_call(
        edge_kernel,
        (f32(FOLD, 128),) * 2 + (f32(STEPS, levels, 128),) * 2,
        [vmem_spec()],
        flops=2_000_000_000,
        nbytes=900_000,
        vmem=FRONT_VMEM_LIMIT,
    )(state)
    spare = kernel_call(
        zero_kernel, f32(16, 128), [], flops=2_000_000_000, nbytes=4096, vmem=FRONT_VMEM_LIMIT
    )()
    spare, edge_near = lax.optimization_barrier((spare, edge_near))
    beside_1 = exchange_over(jnp.concatenate([edge_near, crossed[:pack_rows]], axis=0), "lon", near)
    beside_2 = exchange_over(jnp.concatenate([edge_far, crossed[:pack_rows]], axis=0), "lon", far_round)
    if lon_count == 4:
        across = exchange_over(crossed[:pack_rows], "lon", lambda i: i ^ 2)
        packs = [pack, beside_1, across, beside_2]
        slices = [(0, 0), (1, FOLD), (2, 0), (3, FOLD)]
        east_west = ((1, 0), (3, 0))
    else:
        packs = [pack, beside_1, beside_2, lax.all_gather(pack[:pack_rows], "lon", axis=0, tiled=True)]
        slices = [(3, k * pack_rows) for k in range(lon_count)]
        east_west = ((1, 0), (2, 0))
    rows_1 = exchange(up_down_1, "lat", near)
    rows_2 = exchange(up_down_2, "lat", far_lat)
    rows_1, packs[0] = lax.optimization_barrier((rows_1, packs[0]))
    own, for_first, for_second = kernel_call(
        functools.partial(flux_kernel, count, slices, east_west),
        (f32(levels + 2 * rows + 8, 128),) + (f32(FOLD + 2 * STEPS, 128),) * 2,
        [vmem_spec()] * (2 + len(packs)),
        flops=3_000_000_000,
        nbytes=100_000,
        vmem=FRONT_VMEM_LIMIT,
    )(crossed, spare, *packs)
    own = exchange(own, "comp", near)
    message_1 = exchange_over(for_first, "lat", near)
    message_2 = exchange_over(for_second, "lat", far_lat)
    laid_out = kernel_call(
        inner_kernel,
        (
            jax.ShapeDtypeStruct((levels, 256), jnp.bfloat16),
            f32(2, levels, 128),
            f32(rows + 2 * STEPS, levels, 128),
            f32(2, levels, 128),
        )
        + tuple(f32(rows - 2 * k, levels, 128) for k in range(STEPS)),
        [vmem_spec()] * 6,
        flops=2_000_000_000,
        nbytes=2_000_000,
    )(state, own, rows_1, rows_2, mixing, diffusivity)
    return kernel_call(
        outer_kernel,
        f32(*state.shape),
        [vmem_spec()] * (3 + len(laid_out)),
        scratch=[pltpu.VMEM((6, levels, 128), jnp.float32)] * (STEPS - 1),
        flops=300_000_000,
        nbytes=2_000_000,
    )(own, message_1, message_2, *laid_out)


def solution(mesh):
    in_specs = (
        P("comp", None, "lat", "lon"),
        P("comp", None, None),
        P("comp", None),
        P("comp", None),
        P("comp", "lat", "lon", None, None),
        P("lat", "lon"),
        P("lat", "lon"),
    )
    out_specs = P("comp", None, "lat", "lon")
    return jax.shard_map(
        on_device, mesh=mesh, in_specs=in_specs, out_specs=out_specs, check_vma=False
    )
```
